32 devices in a mesh: req: 8 (over y, x, core), tp: 4 (over z).
Axes of the slice: x: 2, y: 2, z: 4, core: 2. Of those that a mesh axis runs over, the one named last changes fastest.
Arguments:
- queries: bfloat16 [2, 64, 2304], P(None, 'req', 'tp'), may hold values from -10 to 10
- new_keys: bfloat16 [2, 64, 2304], P(None, 'req', 'tp'), may hold values from -4 to 4
- new_values: bfloat16 [2, 64, 2304], P(None, 'req', 'tp'), may hold values from -4 to 4
- cache_keys: bfloat16 [2048, 2304], P('req', 'tp'), may hold values from -10 to 10
- cache_values: bfloat16 [2048, 2304], P('req', 'tp'), may hold values from -4 to 4
- lengths: int32 [8, 16], P('req'), may hold values from 1 to 128, 256 in all within a row
- hidden: bfloat16 [2, 64, 2304], P(None, 'req'), may hold values from -6 to 6
- gain: float32 [2304], replicated, may hold values from 0.5 to 1.5
- expert_ids: int32 [2, 64, 2], P(None, 'req'), may hold values from 0 to 7, all different within a row; in each aligned block of 8 rows (0 to 7, 8 to 15, ..., all dimensions but the last counted through in order) at most 3 rows name the same one
- route_weights: float32 [2, 64, 2], P(None, 'req'), may hold values from 0.2 to 1
- old_place: int32 [8], replicated, may hold values from 0 to 7, as said below
- new_place: int32 [8], replicated, may hold values from 0 to 7, as said below
- old_weights: bfloat16 [8, 2304, 13824], P('req', None, 'tp'), as said below
Outputs:
- context: bfloat16 [2, 64, 2304], P(None, 'req', 'tp')
- layer_out: bfloat16 [2, 64, 2304], P(None, 'req', 'tp')
- new_weights: bfloat16 [8, 2304, 13824], P('req', None, 'tp')
The draws below stay inside these ranges and needn't reach their ends.
Inputs may be any that keep to these rules, and one draw needn't show every extreme that they name: `old_place`: every one of the 8 shards is held by at least one device; the others hold duplicates. `new_place`: every one of the 8 shards is held by at least one device; the others hold duplicates. `old_weights`: devices with equal old_place hold equal weights. `expert_ids`: in a batch, the 8 tokens of one device name one expert at most 3 times, and each token names distinct experts. `lengths`: each row sums to 256.
All inputs are finite; a program needn't handle non-finite values.
Results may differ from the reference program's by a relative error of at most 0.009.
Values may be sent and summed in bfloat16 or wider, within the bound.
No kernel may reach another device: no remote copies, remote signals or barrier semaphores. Data moves between devices by JAX's collectives and lax.ppermute only.
A program may use at most 128 MiB of HBM per device.

```python
import math
import jax
import jax.numpy as jnp
import numpy as np
from jax import lax

D = 2304
HEADS = 36
HEAD_SIZE = 64
EXPERTS = 8
TOPK = 2
FFW = 4608
REQ_DEV = 8
POOL = 256
TOKENS = 64
SPLIT = 1
SHARDS = 8
HID_DEV = 1152
CAP = 3
LONGEST = 128
N_REQ = 8
N_TP = 4


def placement(key, salt):
    salted = jax.random.fold_in(key, salt)
    ordering = jax.random.permutation(jax.random.fold_in(salted, 1), N_REQ)
    extras = jax.random.randint(jax.random.fold_in(salted, 2), (N_REQ,), 0, SHARDS)
    slots = jnp.arange(N_REQ, dtype=jnp.int32)
    assigned = jnp.where(slots < SHARDS, slots, extras).astype(jnp.int32)
    return jnp.zeros((N_REQ,), jnp.int32).at[ordering].set(assigned)


def draw_queries(key, part):
    base = jnp.clip(jax.random.normal(jax.random.fold_in(key, 1), (2, TOKENS, D), jnp.float32), -4.0, 4.0)
    return base.astype(jnp.bfloat16)


def draw_cache_keys(key, part):
    base = jnp.clip(jax.random.normal(jax.random.fold_in(key, 2), (N_REQ * POOL, D), jnp.float32), -4.0, 4.0)
    return base.astype(jnp.bfloat16)


def draw_old_place(key, part):
    return placement(key, 21)


def draw_new_place(key, part):
    return placement(key, 22)


def draw_old_weights(key, part):
    holders = placement(key, 21)
    scales = jnp.array([D ** (-0.5), D ** (-0.5), FFW ** (-0.5)], jnp.float32).reshape(1, 1, 3, 1)

    def one_shard(shard_id):
        shard_key = jax.random.fold_in(jax.random.fold_in(key, 31), shard_id)
        values = jax.random.normal(shard_key, (D, N_TP, 3, HID_DEV), jnp.float32) * scales
        return values.reshape(D, N_TP * 3 * HID_DEV).astype(jnp.bfloat16)
    return lax.map(one_shard, holders)


def level_of(own_key, shape, pieces, smallest, largest):
    level = 1.0
    for axis_at, parts in pieces:
        steps = jax.random.uniform(jax.random.fold_in(jax.random.fold_in(own_key, 6), axis_at), (parts,), jnp.float32, smallest / len(pieces), largest / len(pieces))
        level = level * jnp.repeat(jnp.exp(steps), shape[axis_at] // parts).reshape((-1,) + (1,) * (len(shape) - 1 - axis_at))
    return level


def split_up(number_of, total, limit, lean):
    weights = [(1 << 20) // math.isqrt(grade ** lean) + 1 for grade in range(2, number_of + 1)]
    spare, holding = total - limit - (number_of - 1), [1] * (number_of - 1)
    while spare > 0:
        candidates = [i for i in range(number_of - 1) if holding[i] < limit]
        whole, left = sum([weights[i] for i in candidates]), spare
        for i in candidates:
            addition = min(limit - holding[i], max(1, left * weights[i] // whole), spare)
            holding[i] = holding[i] + addition
            spare = spare - addition
    return np.array([limit] + holding)


def uneven(rng, number_of, total, bound, lean):
    if number_of == 2:
        one = jax.random.randint(rng, (), max(1, total - bound), min(bound, total - 1) + 1)
        return jnp.stack([one, total - one])
    tallies = jnp.asarray(split_up(number_of, total, bound, lean), jnp.int32)
    couples = (number_of - 1) // 2
    source_of, receiver = tallies[1:1 + 2 * couples:2], tallies[2:2 + 2 * couples:2]
    margin = jnp.minimum(source_of - 1, bound - receiver)
    passed = jax.random.randint(jax.random.fold_in(rng, 1), (couples,), 0, 1 << 20) % (margin + 1)
    tallies = tallies.at[1:1 + 2 * couples:2].set(source_of - passed).at[2:2 + 2 * couples:2].set(receiver + passed)
    return tallies[jax.random.permutation(jax.random.fold_in(rng, 2), number_of)]


def routed_block(rng, own, number, rows, number_of, top, limit, skew):
    ranking = jax.random.permutation(rng, number_of)
    heavy_load, usual = load_shares(number_of, rows * top, limit, skew, True), load_shares(number_of, rows * top, limit, skew, False)
    places = jnp.arange(number_of)

    def named(sizes, offset_by):
        used = int((sizes > 0).sum())
        fixed = max(1, used // 4)
        moved = fixed + (places - fixed + offset_by * (used - fixed)) % max(1, number_of - fixed)
        return jnp.zeros((number_of,), jnp.int32).at[ranking[jnp.where(places < fixed, places, moved)]].set(jnp.asarray(sizes, jnp.int32))

    sizes = jnp.where(number % 4 == 0, named(heavy_load, number // 4), named(usual, number - number // 4 - 1))
    mixed = jax.random.permutation(jax.random.fold_in(own, 3), number_of)
    donor, taker = mixed[0:number_of // 2 * 2:2], mixed[1:number_of // 2 * 2:2]
    slack = jnp.minimum(sizes[donor] - 1, limit - sizes[taker]) // 2
    slack = jnp.where((donor == ranking[0]) | (taker == ranking[0]) | (sizes[taker] == 0), 0, jnp.maximum(slack, 0))
    moved = jax.random.randint(jax.random.fold_in(own, 4), (number_of // 2,), 0, 1 << 20) % (slack + 1)
    sizes = sizes.at[donor].add(-moved).at[taker].add(moved)
    members = jnp.searchsorted(jnp.cumsum(sizes), jnp.arange(rows * top), side="right").astype(jnp.int32)
    listing = members.reshape(top, rows).T
    listing = listing[jax.random.permutation(jax.random.fold_in(own, 1), rows)]
    offset_by = jax.random.randint(jax.random.fold_in(own, 2), (rows, 1), 0, top)
    return jnp.take_along_axis(listing, (jnp.arange(top)[None, :] + offset_by) % top, axis=1)


def load_shares(number_of, total, most, lean, full):
    portions = [(1 << 20) // math.isqrt(standing ** lean) + 1 for standing in range(1, number_of + 1)]
    largest = most if full else min(most, max(-(-total // number_of), total * portions[0] // sum(portions)))
    least = 1 if total - largest >= number_of - 1 else 0
    holding, surplus = [largest] + [least] * (number_of - 1), total - largest - least * (number_of - 1)
    while surplus > 0:
        candidates = [i for i in range(1, number_of) if holding[i] < largest] or [i for i in range(1, number_of) if holding[i] < most]
        mass, remaining = sum([portions[i] for i in candidates]), surplus
        for i in candidates:
            extra = min(most - holding[i], max(1, remaining * portions[i] // mass), surplus)
            holding[i] = holding[i] + extra
            surplus = surplus - extra
    return np.array(holding)


def bell_draw(rng, extent, width, reach, shards=(), kind=jnp.bfloat16):
    loudness = level_of(rng, extent, shards, -0.22, 0.18) if shards else 1.0
    entries = jax.random.normal(rng, extent, jnp.float32) * width * loudness
    return jnp.minimum(jnp.maximum(entries, -reach), reach).astype(kind)


def setup_inputs(seed: int = 0) -> dict:
    keys = jax.random.split(jax.random.key(seed), 14)
    queries = draw_queries(jax.random.fold_in(keys[13], 71), 0)
    new_keys = bell_draw(keys[1], (2, TOKENS, D), 1.0, 4.0, ((1, 8), (2, 4)))
    new_values = bell_draw(keys[2], (2, TOKENS, D), 1.0, 4.0, ((1, 8), (2, 4)))
    cache_keys = draw_cache_keys(jax.random.fold_in(keys[13], 71), 0)
    cache_values = bell_draw(keys[4], (N_REQ * POOL, D), 1.0, 4.0, ((0, 8), (1, 4)))
    lengths = jax.vmap(lambda own: uneven(own, 2 * REQ_DEV, POOL, LONGEST, 2))(jax.random.split(keys[5], N_REQ)).reshape((N_REQ, 2 * REQ_DEV)).astype(jnp.int32)
    hidden = bell_draw(keys[6], (2, TOKENS, D), 1.0, 6.0, ((1, 8),))
    gain = jnp.clip(1.0 + 0.1 * jax.random.normal(keys[7], (D,), jnp.float32), 0.5, 1.5)
    expert_ids_keys = jax.random.split(jax.random.fold_in(keys[8], 1), 2 * TOKENS // REQ_DEV)
    expert_ids_turns = jax.random.permutation(jax.random.fold_in(keys[8], 3), 2 * TOKENS // REQ_DEV)
    expert_ids = jax.vmap(lambda own, number: routed_block(jax.random.fold_in(keys[8], 2), own, number, REQ_DEV, EXPERTS, TOPK, CAP, 2))(expert_ids_keys, expert_ids_turns).reshape((2, TOKENS, TOPK))
    route_weights = jnp.clip(0.2 + 0.8 * jax.random.uniform(keys[9], (2, TOKENS, TOPK), jnp.float32) ** level_of(keys[9], (2, TOKENS, TOPK), ((1, 8),), -0.2, 0.2), 0.2, 1.0)
    old_place = draw_old_place(jax.random.fold_in(keys[13], 71), 0)
    new_place = draw_new_place(jax.random.fold_in(keys[13], 71), 0)
    old_weights = draw_old_weights(jax.random.fold_in(keys[13], 71), 0)
    return {"queries": queries, "new_keys": new_keys, "new_values": new_values, "cache_keys": cache_keys, "cache_values": cache_values, "lengths": lengths, "hidden": hidden, "gain": gain, "expert_ids": expert_ids, "route_weights": route_weights, "old_place": old_place, "new_place": new_place, "old_weights": old_weights}


def reference(queries, new_keys, new_values, cache_keys, cache_values, lengths, hidden, gain, expert_ids, route_weights, old_place, new_place, old_weights):
    flt = jnp.float32
    scale = HEAD_SIZE ** (-0.5)

    def to_requests(array):
        shaped = array.astype(flt).reshape(2, N_REQ, REQ_DEV, HEADS, HEAD_SIZE)
        return shaped.transpose(1, 0, 2, 3, 4).reshape(N_REQ, 2 * REQ_DEV, HEADS, HEAD_SIZE)
    query_rows = to_requests(queries)
    own_keys = to_requests(new_keys)
    own_values = to_requests(new_values)
    pool_keys = cache_keys.astype(flt).reshape(N_REQ, POOL, HEADS, HEAD_SIZE)
    pool_values = cache_values.astype(flt).reshape(N_REQ, POOL, HEADS, HEAD_SIZE)
    starts = jnp.cumsum(lengths, axis=1) - lengths
    position = jnp.arange(POOL, dtype=jnp.int32)
    owned = (position[None, None, :] >= starts[:, :, None]) & (position[None, None, :] < (starts + lengths)[:, :, None])
    scores = jnp.einsum('nqhd,nphd->nhqp', query_rows, pool_keys) * scale
    scores = jnp.where(owned[:, None], scores, -jnp.inf)
    own_score = jnp.einsum('nqhd,nqhd->nhq', query_rows, own_keys) * scale
    highest = jnp.maximum(lax.optimization_barrier(jnp.max(scores, axis=-1)), own_score)
    exp_pool = jnp.exp(scores - highest[..., None])
    exp_own = jnp.exp(own_score - highest)
    denom = lax.optimization_barrier(jnp.sum(exp_pool, axis=-1)) + exp_own
    prob_pool = lax.optimization_barrier(exp_pool.astype(jnp.bfloat16)).astype(flt)
    prob_own = lax.optimization_barrier(exp_own.astype(jnp.bfloat16)).astype(flt)
    summed = jnp.einsum('nhqp,nphd->nqhd', prob_pool, pool_values)
    summed = summed + prob_own.transpose(0, 2, 1)[..., None] * own_values
    context = (summed / denom.transpose(0, 2, 1)[..., None]).astype(jnp.bfloat16)
    context = context.reshape(N_REQ, 2, REQ_DEV, D).transpose(1, 0, 2, 3).reshape(2, TOKENS, D)
    resid = hidden.astype(flt)
    normed = (resid * gain / jnp.sqrt(lax.optimization_barrier(jnp.mean(resid * resid, axis=-1, keepdims=True)) + 1e-05)).astype(jnp.bfloat16)
    normed_f = lax.optimization_barrier(normed).astype(flt).reshape(2 * TOKENS, D)
    devices = jnp.arange(N_REQ, dtype=jnp.int32)
    shard_ids = jnp.arange(SHARDS, dtype=jnp.int32)
    first_old = lax.optimization_barrier(jnp.min(jnp.where(old_place[None, :] == shard_ids[:, None], devices[None, :], N_REQ), axis=1)).astype(jnp.int32)
    flat_ids = expert_ids.reshape(2 * TOKENS, TOPK)
    flat_weights = route_weights.reshape(2 * TOKENS, TOPK)
    coef = lax.optimization_barrier(jnp.sum(jnp.where(flat_ids[:, :, None] == jnp.arange(EXPERTS, dtype=jnp.int32)[None, None, :], flat_weights[:, :, None], 0.0), axis=1))

    def add_shard(total, shard_id):
        holder = lax.dynamic_index_in_dim(first_old, shard_id, 0, keepdims=False)
        weight_block = lax.dynamic_index_in_dim(old_weights, holder, 0, keepdims=False).astype(flt)
        weight_block = weight_block.reshape(D, N_TP, 3, HID_DEV)
        gate_out = jnp.einsum('td,dph->tph', normed_f, weight_block[:, :, 0])
        up_out = jnp.einsum('td,dph->tph', normed_f, weight_block[:, :, 1])
        act = lax.optimization_barrier((jax.nn.silu(gate_out) * up_out).astype(jnp.bfloat16)).astype(flt)
        part = jnp.einsum('tph,dph->tpd', act, weight_block[:, :, 2])
        part = lax.optimization_barrier(part.astype(jnp.bfloat16)).astype(flt)
        expert_col = lax.dynamic_slice_in_dim(coef, (shard_id // SPLIT).astype(jnp.int32), 1, 1)
        return (total + expert_col * lax.optimization_barrier(jnp.sum(part, axis=1)), None)
    total, _ = lax.scan(add_shard, jnp.zeros((2 * TOKENS, D), flt), shard_ids)
    layer_out = (resid + total.reshape(2, TOKENS, D)).astype(jnp.bfloat16)
    source = lax.optimization_barrier(jnp.sum(jnp.where(new_place[:, None] == shard_ids[None, :], first_old[None, :], 0), axis=1)).astype(jnp.int32)
    new_weights = jnp.take(old_weights, source, axis=0)
    return (context, layer_out, new_weights)
```

```python
import jax
import jax.numpy as jnp
from jax import lax
from jax.sharding import PartitionSpec as P

HEAD_SIZE = 64
EXPERTS = 8
CAP = 3


def attend(queries, new_keys, new_values, cache_keys, cache_values, lengths):
    batches, tok_rows, width = queries.shape
    heads = width // HEAD_SIZE
    pool = cache_keys.shape[0]
    scale = HEAD_SIZE ** (-0.5)
    req_lengths = lengths.reshape(-1)
    starts = jnp.cumsum(req_lengths) - req_lengths
    position = jnp.arange(pool, dtype=jnp.int32)
    owned = (position[None, :] >= starts[:, None]) & (
        position[None, :] < (starts + req_lengths)[:, None]
    )
    query_rows = queries.reshape(batches * tok_rows, heads, HEAD_SIZE)
    own_keys = new_keys.reshape(batches * tok_rows, heads, HEAD_SIZE)
    own_values = new_values.reshape(batches * tok_rows, heads, HEAD_SIZE)
    pool_keys = cache_keys.reshape(pool, heads, HEAD_SIZE)
    pool_values = cache_values.reshape(pool, heads, HEAD_SIZE)
    scores = (
        jnp.einsum("qhd,phd->hqp", query_rows, pool_keys, preferred_element_type=jnp.float32)
        * scale
    )
    scores = jnp.where(owned[None], scores, -jnp.inf)
    own_score = (
        jnp.einsum("qhd,qhd->hq", query_rows, own_keys, preferred_element_type=jnp.float32) * scale
    )
    highest = jnp.maximum(jnp.max(scores, axis=-1), own_score)
    exp_pool = jnp.exp(scores - highest[..., None])
    exp_own = jnp.exp(own_score - highest)
    denom = jnp.sum(exp_pool, axis=-1) + exp_own
    summed = jnp.einsum(
        "hqp,phd->qhd",
        exp_pool.astype(jnp.bfloat16),
        pool_values,
        preferred_element_type=jnp.float32,
    )
    prob_own = lax.optimization_barrier(exp_own.astype(jnp.bfloat16)).astype(jnp.float32)
    summed = summed + prob_own.T[:, :, None] * own_values.astype(jnp.float32)
    context = (summed / denom.T[:, :, None]).astype(jnp.bfloat16)
    return context.reshape(batches, tok_rows, width)


def choose_holders(place, me_index, nreq, shard_count):
    devices = jnp.arange(nreq, dtype=jnp.int32)
    holder = place[None, :] == jnp.arange(shard_count, dtype=jnp.int32)[:, None]
    before = (place[:, None] == place[None, :]) & (devices[:, None] < devices[None, :])
    rank_in = jnp.sum(before.astype(jnp.int32), axis=0)
    count = jnp.sum(holder.astype(jnp.int32), axis=1)
    wanted = me_index % count
    match = holder & (rank_in[None, :] == wanted[:, None])
    return jnp.sum(jnp.where(match, devices[None, :], 0), axis=1)


def expert_block(hidden, chosen, weights_now, place, shard_weights, gain):
    nreq = lax.axis_size("req")
    me_index = lax.axis_index("req")
    split_count = max(1, nreq // 16)
    shard_count = EXPERTS * split_count
    batches, tok_rows, width = hidden.shape
    topk = chosen.shape[-1]
    tokens = batches * tok_rows
    hid_dev = shard_weights.shape[1] // 3
    resid = hidden.reshape(tokens, width).astype(jnp.float32)
    normed = (
        resid * gain / jnp.sqrt(jnp.mean(resid * resid, axis=-1, keepdims=True) + 1e-05)
    ).astype(jnp.bfloat16)
    flat_ids = chosen.reshape(-1)
    assigns = flat_ids.shape[0]
    slots_dev = batches * CAP
    shard_dest = choose_holders(place, me_index, nreq, shard_count)
    shard_list = flat_ids[:, None] * split_count + jnp.arange(split_count, dtype=jnp.int32)[None, :]
    pick = shard_list[:, :, None] == jnp.arange(shard_count, dtype=jnp.int32)[None, None, :]
    dest = jnp.sum(jnp.where(pick, shard_dest[None, None, :], 0), axis=-1)
    assign_index = jnp.arange(assigns, dtype=jnp.int32)
    batch_of = assign_index // (tok_rows * topk)
    earlier = (
        (flat_ids[:, None] == flat_ids[None, :])
        & (batch_of[:, None] == batch_of[None, :])
        & (assign_index[None, :] < assign_index[:, None])
    )
    rank_in = jnp.sum(earlier.astype(jnp.int32), axis=1)
    slot = dest * slots_dev + (batch_of * CAP + rank_in)[:, None]
    slot_hit = slot[:, :, None] == jnp.arange(nreq * slots_dev, dtype=jnp.int32)[None, None, :]
    by_token = jnp.any(slot_hit.reshape(tokens, topk * split_count, nreq * slots_dev), axis=1)
    outgoing = jnp.dot(
        by_token.T.astype(jnp.bfloat16), normed, preferred_element_type=jnp.float32
    )
    outgoing = outgoing.astype(jnp.bfloat16).reshape(nreq, slots_dev, width)
    received = lax.all_to_all(outgoing, "req", split_axis=0, concat_axis=0, tiled=True)
    flat_rows = received.reshape(nreq * slots_dev, width)
    gate_up = jnp.dot(
        flat_rows, shard_weights[:, : 2 * hid_dev], preferred_element_type=jnp.float32
    )
    act = (jax.nn.silu(gate_up[:, :hid_dev]) * gate_up[:, hid_dev:]).astype(jnp.bfloat16)
    part = lax.dot_general(
        act,
        shard_weights[:, 2 * hid_dev :],
        (((1,), (1,)), ((), ())),
        preferred_element_type=jnp.float32,
    )
    part = part.astype(jnp.bfloat16).reshape(nreq, slots_dev, width)
    returned = lax.all_to_all(part, "req", split_axis=0, concat_axis=0, tiled=True)
    returned = returned.reshape(nreq * slots_dev, width)
    coef = jnp.sum(
        jnp.where(
            slot_hit.reshape(tokens, topk, split_count, nreq * slots_dev),
            weights_now.reshape(tokens, topk)[:, :, None, None],
            0.0,
        ),
        axis=(1, 2),
    )
    partial_sum = jnp.dot(
        coef,
        returned.astype(jnp.float32),
        precision=lax.Precision.HIGHEST,
        preferred_element_type=jnp.float32,
    )
    tp_width = width // lax.axis_size("tp")
    tp_start = lax.axis_index("tp") * tp_width
    resid_share = lax.dynamic_slice_in_dim(resid, tp_start, tp_width, 1)
    share = lax.psum_scatter(
        partial_sum.astype(jnp.bfloat16), "tp", scatter_dimension=1, tiled=True
    ).astype(jnp.float32)
    summed = (resid_share + share).astype(jnp.bfloat16)
    return summed.reshape(batches, tok_rows, tp_width)


def migrate(old_weights, old_place, new_place):
    nreq = lax.axis_size("req")
    shard_count = EXPERTS * max(1, nreq // 16)
    _, width, columns = old_weights.shape
    piece = width // nreq
    pieces = old_weights.reshape(nreq, piece, columns)
    spread = lax.all_to_all(pieces, "req", split_axis=0, concat_axis=0, tiled=True)
    devices = jnp.arange(nreq, dtype=jnp.int32)
    shard_ids = jnp.arange(shard_count, dtype=jnp.int32)
    first_old = jnp.min(
        jnp.where(old_place[None, :] == shard_ids[:, None], devices[None, :], nreq), axis=1
    )
    needed = jnp.sum(
        jnp.where(new_place[:, None] == shard_ids[None, :], first_old[None, :], 0), axis=1
    )
    sending = spread[needed]
    collected = lax.all_to_all(sending, "req", split_axis=0, concat_axis=0, tiled=True)
    return collected.reshape(1, width, columns)


def on_device(
    queries,
    new_keys,
    new_values,
    cache_keys,
    cache_values,
    lengths,
    hidden,
    gain,
    expert_ids,
    route_weights,
    old_place,
    new_place,
    old_weights,
):
    context = attend(queries, new_keys, new_values, cache_keys, cache_values, lengths)
    moved = migrate(old_weights, old_place, new_place)
    layer_out = expert_block(
        hidden, expert_ids, route_weights, old_place, old_weights[0], gain
    )
    return (context, layer_out, moved)


def solution(mesh):
    in_specs = (
        P(None, "req", "tp"),
        P(None, "req", "tp"),
        P(None, "req", "tp"),
        P("req", "tp"),
        P("req", "tp"),
        P("req", None),
        P(None, "req", None),
        P(),
        P(None, "req", None),
        P(None, "req", None),
        P(),
        P(),
        P("req", None, "tp"),
    )
    out_specs = (P(None, "req", "tp"), P(None, "req", "tp"), P("req", None, "tp"))
    return jax.shard_map(
        on_device, mesh=mesh, in_specs=in_specs, out_specs=out_specs, check_vma=False
    )
```

```python
import functools

import jax
import jax.numpy as jnp
import numpy as np
from jax import lax
from jax.experimental import pallas as pl
from jax.experimental.pallas import tpu as pltpu
from jax.sharding import PartitionSpec as P

HEAD_SIZE = 64
EXPERTS = 8
CAP = 3
PIECES = 8
TOTALS = (9, 12, 16)
SPANS = ((0, 2), (2, 4))
STAGES = {1: 1, 3: 1, 4: 1, 5: 1, 6: 1, 8: 1}
SLOTS = 8
LOCAL_PIECES = {4: (0, 1), 5: (2, 3), 6: (4, 5), 7: (6, 7)}
PLAN_STEPS = max(TOTALS)
CORE_AT = 2 * PLAN_STEPS
SWAP_AT = CORE_AT + 1
LOCAL_AT = CORE_AT + 2
GOAL_AT = CORE_AT + 3
TOTAL_AT = CORE_AT + 11
META = CORE_AT + 12

ROUTES = (
    (((0, 0), (1, 1), (2, 2), (3, 3)), 9, 0x924924924924924924924924924924924924924924924924924924),
    (((0, 0), (1, 1), (2, 3), (2, 3)), 9, 0x9249248a39248a39248a39248a39248a39248a39248a39248a3924),
    (((0, 0), (1, 1), (3, 3), (2, 2)), 12, 0x8a39248a39248a39248a39248a37148a37148a36938a369349b8a349b8a349b92449b924),
    (((0, 0), (1, 2), (1, 2), (3, 3)), 9, 0x9249249249249249242a49112a49112894912894919094a49094a4),
    (((0, 0), (1, 2), (1, 3), (2, 3)), 9, 0x8a39118a391188b89188b89188b89188b89128b89188b8a48894a4),
    (((0, 0), (1, 2), (2, 3), (1, 3)), 9, 0x9249243239243239242a39142a39142a34942a34943234a43234a4),
    (((0, 0), (1, 2), (3, 3), (1, 2)), 12, 0x9239248a39248a39248a39242a37242a37142a37132a369329b89329b49329b4a429b4a4),
    (((0, 0), (1, 3), (1, 3), (2, 2)), 12, 0x8a49248a49248a49248a39218a371188b71188b69128b69148b6a148b6a148972448b724),
    (((0, 0), (1, 3), (2, 3), (1, 2)), 9, 0x9249242a37242a37242a37242a37242a37242a37242a37242a3724),
    (((0, 0), (2, 2), (1, 1), (3, 3)), 12, 0x9249249249242a49112a49112894912894912894912894912894912894919094a49094a4),
    (((0, 0), (2, 2), (1, 3), (1, 3)), 12, 0x9249249249248a49142a39112a349128b49128b49128b49128b49128b49130b4a43094a4),
    (((0, 0), (2, 2), (3, 3), (1, 1)), 12, 0x3239143239142a36912a369128b49128b49324b69125b69328b49329b49325b4a425b4a4),
    (((0, 0), (2, 3), (1, 3), (1, 2)), 9, 0x2a37112a371128b69128b69128b69128b69128969128b6a428b4a4),
    (((0, 1), (0, 1), (2, 3), (2, 3)), 9, 0x9249248a38218a38218a38218a38218a38218a38218a38218a3821),
    (((0, 1), (0, 1), (3, 3), (2, 2)), 12, 0x8a38218a38218a38218a38218a36118a36118a36938a369349b8a349b8a349b82149b821),
    (((0, 1), (0, 2), (1, 3), (2, 3)), 12, 0x8a38218a38218a38218a38218a38218a38212a38112a38112894912894918894a18894a1),
    (((0, 1), (0, 2), (2, 3), (1, 3)), 9, 0x8a48242a38212a34212a34212a34212a34212a34113234213234a1),
    (((0, 1), (0, 2), (3, 3), (1, 2)), 12, 0x8a38218a38218a38218a38212a36212a36212a36132a361329b49329b49329b4a129b4a1),
    (((0, 1), (0, 3), (1, 2), (2, 3)), 9, 0x3249212a46212a16212a16212a16212a16212a16218a1621889621),
    (((0, 1), (0, 3), (1, 3), (2, 2)), 12, 0x8a38218a38218a38218a38212a36112a36112a16912a169148b6a148b6a1489621489621),
    (((0, 1), (0, 3), (2, 3), (1, 2)), 9, 0x9249242a36212a36212a36212a36212a36212a36212a36212a3621),
    (((0, 1), (1, 2), (2, 3), (0, 3)), 9, 0x9249248a38218a38218a38210834110834110034910234a10234a1),
    (((0, 1), (1, 2), (3, 3), (0, 2)), 12, 0x8a38218a38218a38218a38210a36210a36210a36130a361309b49309b49309b4a109b4a1),
    (((0, 1), (1, 3), (0, 2), (2, 3)), 9, 0x924924884721884721884721884721884721884721884721884721),
    (((0, 1), (1, 3), (0, 3), (2, 2)), 12, 0x8a49248a49248a49248a49248837118837118836918836914836a14836a1483721483721),
    (((0, 1), (2, 2), (0, 3), (1, 3)), 12, 0x9249249249248a49148a49142834912834912834912834912834912834913034a13034a1),
    (((0, 1), (2, 2), (1, 3), (0, 3)), 12, 0x8a38218a38218a38118a381108349128b49128b49120149108149120149100b4a10094a1),
    (((0, 1), (2, 2), (3, 3), (0, 1)), 12, 0x8a38212a36112a341128369108349320369100369300349329b49129b49321b4a121b4a1),
    (((0, 1), (2, 3), (0, 1), (2, 3)), 9, 0x2847112847112894912816912816912816912816918816a18816a1),
    (((0, 1), (2, 3), (0, 3), (1, 2)), 9, 0x8a47142837112836912836912836912836912836912834a12836a1),
    (((0, 1), (2, 3), (1, 2), (0, 3)), 9, 0x3246113046112816912016912016912016912014910216a10096a1),
    (((0, 1), (2, 3), (1, 3), (0, 2)), 12, 0x8a38218a38218a38212a34112a36112836910816912896910036910096910896a100b6a1),
    (((0, 1), (2, 3), (2, 3), (0, 1)), 9, 0x3047142836112036912034912036912036910036912236a12236a1),
    (((0, 1), (3, 3), (0, 1), (2, 2)), 12, 0x8a47248a47242837112837112816912816994836912836d92896994816d94896e14816e1),
    (((0, 1), (3, 3), (1, 2), (0, 2)), 12, 0x9247218a47218a47212a46212a362128362108361908b6192896d90016d90096e10096e1),
    (((0, 3), (0, 2), (1, 3), (1, 2)), 12, 0x8a38218a38218a38218a382128b61128b41128b49128b69b28b61128b69b28b49b28b41b),
    (((0, 3), (0, 3), (1, 1), (2, 2)), 12, 0x8a38218a382128b61928b61128961128969128b69148969928b61948969948961b48961b),
    (((0, 3), (0, 3), (1, 2), (1, 2)), 9, 0x3237212a362128b61928b61928b61928b61928b61928c61c28961b),
    (((0, 3), (1, 2), (1, 2), (0, 3)), 9, 0x92492428361128361128961b08949320369100341900949b00949b),
    (((0, 3), (1, 2), (1, 3), (0, 2)), 12, 0x8a38218a38218a38218a382128b61108b61108949308369308b61908b69300b49b08b49b),
    (((0, 3), (2, 2), (1, 1), (0, 3)), 12, 0x28361128361128149320341128969120969920969308149128949328949100949b00949b),
    (((0, 3), (2, 2), (1, 3), (0, 1)), 12, 0x28361128361120361108369128b49328b49120b69100949128b49328349b20b49b00b49b),
    (((1, 1), (0, 0), (3, 3), (2, 2)), 16, 0x8a38218a38218a38218a38218a38218a38218a38218a38218a38218a38218a38218a38218a38218a38218a38218a3821),
    (((1, 1), (0, 2), (3, 3), (0, 2)), 16, 0x8a38218a38218a38218a38218a38218a38218a38218a38218a38218a38218a38210834110834110034910234a10234a1),
    (((1, 1), (0, 3), (0, 3), (2, 2)), 12, 0x8a38218a38218a38218a3821283611283611281691281691481689481689483609483609),
    (((1, 1), (2, 2), (3, 3), (0, 0)), 16, 0x8a38218a38218a38218a38218a38218a38218a38210834110834110034910034910034910034910034910234a10234a1),
    (((1, 1), (2, 3), (0, 3), (0, 2)), 12, 0x8a38218a3821283611283611081691283491281689081491081611003609083689003689),
    (((1, 1), (3, 3), (0, 0), (2, 2)), 12, 0x2836112836112836110836190816912806d90816890816994806d94816894806c94806c9),
    (((1, 2), (0, 3), (0, 3), (1, 2)), 9, 0x924924283611283611283611283611283611283611283611283611),
    (((1, 2), (0, 3), (1, 3), (0, 2)), 12, 0x8a38218a38218a38218a382128361128b61120361108161100b611201611089611009611),
    (((1, 2), (2, 3), (1, 3), (0, 0)), 12, 0x28361128361100361120369128961100961100361108341100141100349100969100b491),
    (((1, 3), (0, 2), (1, 3), (0, 2)), 16, 0x8a38218a38218a38218a38218a38218a38218a38218a382128361108b41920169108b61900349328941b08b41b009499),
    (((1, 3), (2, 2), (1, 3), (0, 0)), 16, 0x8a38218a38218a38218a382128b41108341108349908b69100141120349108b61b20369100149100341b00b49b009499),
    (((1, 3), (2, 3), (0, 1), (0, 2)), 12, 0x28361128361128349108361b28361908b49908961108161128b699081419001699081699),
    (((3, 3), (2, 2), (1, 1), (0, 0)), 16, 0x28361128361100b69308141920369328349320361128949120969900169b28161308141300949b20b61900949b00949b),
)


def route_tables():
    pairs = [(a, b) for b in range(4) for a in range(b + 1)]
    pair_at = {pair: i for i, pair in enumerate(pairs)}
    row_of = np.zeros((79 * 128,), np.int32)
    rows, rooms = [], 0
    seen = set()
    for (goals, steps, code) in ROUTES:
        for flip in range(8):
            names = []
            for chip in range(4):
                y, x = chip // 2 ^ (flip & 1), chip % 2 ^ (flip >> 1 & 1)
                names.append(x * 2 + y if flip & 4 else y * 2 + x)
            moved = [None] * 4
            for chip in range(4):
                moved[names[chip]] = tuple(sorted(names[g] for g in goals[chip]))
            key = sum(pair_at[moved[chip]] * 10**chip for chip in range(4))
            if key in seen:
                continue
            seen.add(key)
            row_of[key] = len(rows)
            plan, room = plan_of(moved, steps, code, names, flip >> 2)
            rows.append(plan)
            rooms = max(rooms, room)
    plans = np.stack(rows).reshape(-1, 1, 128)
    return row_of.reshape(79, 1, 128), plans, rooms


def plan_of(goals, steps, code, names, swapped):
    back = [names.index(chip) for chip in range(4)]
    own = [{} for _ in range(4)]
    for chip in range(4):
        for which in range(2):
            own[chip].setdefault(goals[chip][which], []).append(which)
    waiting = [{} for _ in range(4)]
    for chip in range(4):
        for goal, members in own[chip].items():
            if goal != chip:
                waiting[chip][goal] = [
                    (-2, which, piece, None) for piece in range(PIECES) for which in members
                ]
    plan = np.zeros((4, 128), np.int32)
    plan[:, 2 * PLAN_STEPS] = sum(steps > total for total in TOTALS)
    free = [list(range(32)) for _ in range(4)]
    room = 0
    for step in range(steps):
        landed = []
        for chip in range(4):
            for link in range(2):
                at = (step * 4 + back[chip]) * 2 + (link ^ swapped)
                goal = code >> 3 * at & 7
                if goal == 4:
                    continue
                goal = names[goal]
                queue = waiting[chip][goal]
                pick = next(i for i, item in enumerate(queue) if item[0] < step - 1)
                ready, which, piece, held = queue.pop(pick)
                if held is None:
                    source = chip
                    sent = which | piece << 2
                else:
                    source = held[0]
                    sent = 2 | held[1] << 2
                    free[chip].insert(0, held[1])
                plan[chip, 2 * step + link] |= sent
                landed.append((chip ^ 1 << link, link, source, which, piece, goal))
        for chip, link, source, which, piece, goal in landed:
            got = (source * 2 + which) << 9 | piece << 12
            if goal == chip:
                got |= 1 << 7
            else:
                slot = free[chip].pop(0)
                room = max(room, slot + 1)
                got |= 2 << 7 | slot << 16
                waiting[chip].setdefault(goal, []).append((step, which, piece, (source, slot)))
            plan[chip, 2 * step + link] |= got
    assert not any(queue for chip in waiting for queue in chip.values())
    return plan, room


def copy_all(moves, sems, base, phase):
    for number, (condition, source, target) in enumerate(moves):

        @pl.when(condition)
        def _(number=number, source=source, target=target):
            copy = pltpu.make_async_copy(source, target, sems.at[base + number])
            if phase == 0:
                copy.start()
            else:
                copy.wait()


def piece_rows(ref, row, rows):
    return ref.at[pl.ds(pl.multiple_of(row, 16), rows)]


def store_moves(meta, step, landed, room, rows):
    moves = []
    for link in range(2):
        word = meta[2 * step + link]
        slot = (word >> 16) & 31
        moves.append(((word >> 7) & 3 == 2, landed[link], piece_rows(room, slot * rows, rows)))
    return moves


def place_moves(meta, step, landed, out_hbm, rows):
    half = PIECES * rows
    core = meta[CORE_AT]
    moves = []
    for link in range(2):
        word = meta[2 * step + link]
        code = (word >> 9) & 7
        row = ((word >> 12) & 15) * rows
        final = ((word >> 7) & 3 == 1) & (meta[GOAL_AT + code] == core)
        for piece, start in ((landed[link], core * half), (landed[2 + link], (1 - core) * half)):
            moves.append((final, piece, piece_rows(out_hbm, start + row, rows)))
    return moves


def plan_kernel(old_place, new_place, row_of, plans, weights, meta, *refs):
    *early, row_part, plan_part, sem, early_sems = refs
    me_index = lax.axis_index("req")
    core = me_index % 2
    rows = weights.shape[0] // (2 * PIECES)
    copies = []
    for number, (low, high) in enumerate(SPANS):
        row = ((1 - core) * PIECES + low) * rows
        part = weights.at[pl.ds(pl.multiple_of(row, 16), (high - low) * rows)]
        copies.append(pltpu.make_async_copy(part, early[number], early_sems.at[number]))
        copies[-1].start()
    chip = me_index // 2
    goals = []
    for holder in range(8):
        goal = jnp.int32(0)
        for device in range(8):
            goal = jnp.where(new_place[device] == old_place[holder], device, goal)
        goals.append(goal)
    key = jnp.int32(0)
    my_swap = jnp.int32(0)
    for at in range(4):
        first, second = goals[2 * at], goals[2 * at + 1]
        low, high = jnp.minimum(first, second), jnp.maximum(first, second)
        high_chip = high // 2
        key = key + (high_chip * (high_chip + 1) // 2 + low // 2) * 10**at
        my_swap = jnp.where((first > second) & (chip == at), 1, my_swap)
        meta[GOAL_AT + 2 * at] = low % 2
        meta[GOAL_AT + 2 * at + 1] = high % 2
    meta[CORE_AT] = core
    meta[SWAP_AT] = my_swap
    wanted = new_place[me_index]
    beside = jnp.where(wanted == old_place[me_index + 1 - 2 * core], 2, 0)
    meta[LOCAL_AT] = jnp.where(wanted == old_place[me_index], 1, beside)
    copy = pltpu.make_async_copy(row_of.at[key // 128], row_part, sem)
    copy.start()
    copy.wait()
    row = row_part[0, key % 128]
    copy = pltpu.make_async_copy(plans.at[row * 4 + chip], plan_part, sem)
    copy.start()
    copy.wait()
    for at in range(2 * PLAN_STEPS):
        meta[at] = plan_part[0, at]
    meta[TOTAL_AT] = plan_part[0, 2 * PLAN_STEPS]
    for copy in copies:
        copy.wait()


def step_kernel(rows, step, spans, local_pieces, names, count, meta, *refs):
    refs = list(zip(names, refs))
    semaphores = refs.pop()[1]
    given = {}
    for number, (name, ref) in enumerate(refs):
        if number >= count or name not in ("out", "room"):
            given.setdefault(name, []).append(ref)
    w_hbm = given["weights"][0]
    if step is None:
        step = given["turn"][0][0]
    out_hbm = given.get("out", [None])[0]
    room = given.get("room", [None])[0]
    half = PIECES * rows
    core = meta[CORE_AT]
    local = meta[LOCAL_AT]
    used = 0
    moves = []
    for back in range(4):
        if ("going", back) in given:
            moves += store_moves(meta, step - back, given["going", back], room, rows)
    copy_all(moves, semaphores, used, 0)
    copy_all(moves, semaphores, used, 1)
    used += len(moves)
    fetched = given.get("sent", [])
    for link, target in enumerate(fetched):
        word = meta[2 * step + link]
        kind = word & 3
        piece = (word >> 2) & 31
        held = kind == 2
        mine = (kind ^ meta[SWAP_AT]) == core
        row = core * half + piece * rows
        options = [(jnp.logical_not(held) & mine, piece_rows(w_hbm, row, rows))]
        for ref, (low, high) in zip(given["group"], spans):
            inside = jnp.logical_not(held | mine) & (piece >= low) & (piece < high)
            start = row if high - low == PIECES else (piece - low) * rows
            options.append((inside, piece_rows(ref, start, rows)))
        if room is not None:
            options.append((held, piece_rows(room, piece * rows, rows)))
        for condition, source in options:

            @pl.when(condition)
            def _(source=source, target=target, link=link):
                pltpu.make_async_copy(source, target, semaphores.at[used + link]).start()

    first_fetch = used
    used += len(fetched)
    moves = []
    for back in range(4):
        if ("landed", back) in given:
            moves += place_moves(meta, step - back, given["landed", back], out_hbm, rows)
    copy_all(moves, semaphores, used, 0)
    first_move = used
    used += len(moves)
    reads, writes = [], []
    for number, piece in enumerate(local_pieces):
        for side in range(2):
            row = side * half + piece * rows
            part = given["staged"][0].at[2 * number + side]
            reads.append((local == 1, piece_rows(w_hbm, row, rows), part))
            reads.append((local == 2, piece_rows(given["group"][-1], row, rows), part))
            writes.append((local != 0, part, piece_rows(out_hbm, row, rows)))
    copy_all(reads, semaphores, used, 0)
    for link, target in enumerate(fetched):
        copy = pltpu.make_async_copy(
            w_hbm.at[pl.ds(0, rows)], target, semaphores.at[first_fetch + link]
        )
        copy.wait()
    copy_all(reads, semaphores, used, 1)
    used += len(reads)
    copy_all(writes, semaphores, used, 0)
    copy_all(moves, semaphores, first_move, 1)
    copy_all(writes, semaphores, used, 1)


def across(array, link):
    return lax.ppermute(array, "req", [(i, i ^ (1, 2, 4)[link]) for i in range(8)])


def plan_plane(old_place, new_place, weights):
    row_of, plans, _ = route_tables()
    smem = pl.BlockSpec(memory_space=pltpu.SMEM)
    anywhere = pl.BlockSpec(memory_space=pl.ANY)
    near = pl.BlockSpec(memory_space=pltpu.VMEM)
    width, columns = weights.shape
    rows = width // (2 * PIECES)
    meta, *early = pl.pallas_call(
        plan_kernel,
        out_shape=[jax.ShapeDtypeStruct((META,), jnp.int32)]
        + [jax.ShapeDtypeStruct(((b - a) * rows, columns), weights.dtype) for a, b in SPANS],
        in_specs=[smem, smem, anywhere, anywhere, anywhere],
        out_specs=[smem] + [near] * len(SPANS),
        scratch_shapes=[
            pltpu.SMEM((1, 128), jnp.int32),
            pltpu.SMEM((1, 128), jnp.int32),
            pltpu.SemaphoreType.DMA,
            pltpu.SemaphoreType.DMA((len(SPANS),)),
        ],
        compiler_params=pltpu.CompilerParams(vmem_limit_bytes=32 << 20),
        name="plan_steps",
    )(old_place, new_place, jnp.asarray(row_of), jnp.asarray(plans), weights)
    return meta, [across(part, 0) for part in early]


def migrate_plane(weights, meta, early, total, beside):
    width, columns = weights.shape
    rows = width // (2 * PIECES)
    slots = route_tables()[2]
    smem = pl.BlockSpec(memory_space=pltpu.SMEM)
    anywhere = pl.BlockSpec(memory_space=pl.ANY)
    near = pl.BlockSpec(memory_space=pltpu.VMEM)
    chunk = jax.ShapeDtypeStruct((rows, columns), weights.dtype)
    whole = jax.ShapeDtypeStruct((width, columns), weights.dtype)
    room_like = jax.ShapeDtypeStruct((slots * rows, columns), weights.dtype)

    def run(step, meta, groups, spans, fetch, going, landed, local_pieces, out, room):
        operands, specs, names, aliases = [meta, weights], [smem, anywhere], ["weights"], {}

        def add(name, array, spec):
            operands.append(array)
            specs.append(spec)
            names.append(name)

        for group in groups:
            add("group", group, anywhere)
        for back, pieces in going.items():
            for piece in pieces[:2]:
                add(("going", back), piece, near)
        for back, pieces in landed.items():
            for piece in pieces:
                add(("landed", back), piece, near)
        results = [("sent", chunk, near)] * (2 * fetch)
        for name, array, like, wanted in (
            ("out", out, whole, bool(landed or local_pieces)),
            ("room", room, room_like, bool(going)),
        ):
            if wanted:
                if array is not None:
                    aliases[len(operands)] = len(results)
                    add(name, array, anywhere)
                results.append((name, like, anywhere))
        count = len(names)
        names += [name for name, _, _ in results]
        scratch = []
        if local_pieces:
            scratch.append(pltpu.VMEM((2 * len(local_pieces), rows, columns), weights.dtype))
            names.append("staged")
        scratch.append(pltpu.SemaphoreType.DMA((40,)))
        names.append("semaphores")
        values = pl.pallas_call(
            functools.partial(step_kernel, rows, step, spans, local_pieces, names, count),
            out_shape=[like for _, like, _ in results],
            in_specs=specs,
            out_specs=[spec for _, _, spec in results],
            scratch_shapes=scratch,
            input_output_aliases=aliases,
            compiler_params=pltpu.CompilerParams(vmem_limit_bytes=32 << 20),
            cost_estimate=pl.CostEstimate(
                flops=0, bytes_accessed=8 * rows * columns * 2, transcendentals=0
            ),
            name="step_pieces" if fetch else "place_pieces",
        )(*operands)
        found = dict(zip([name for name, _, _ in results], values))
        return values[:2] if fetch else None, found.get("out", out), found.get("room", room)

    every = (0, PIECES)
    landed = {}
    out = room = None
    for step in range(total):
        meta = beside(step, meta)
        use, spans = ([other], (every,)) if step >= 2 else (early[: step + 1], SPANS[: step + 1])
        sent, out, room = run(
            step,
            meta,
            use,
            spans,
            True,
            {2: landed[step - 2]} if step >= 2 else {},
            {3: landed[step - 3]} if step >= 3 else {},
            LOCAL_PIECES.get(step, ()),
            out,
            room,
        )
        if step == 1:
            source, _ = lax.optimization_barrier((weights, sent[0]))
            other = across(source, 0)
        brought = [across(sent[0], 1), across(sent[1], 2)]
        landed[step] = brought + [across(piece, 0) for piece in brought]
    last = total - 1
    meta = beside(total, meta)
    before = {2: landed[last - 2], 1: landed[last - 1]}
    _, out, _ = run(last, meta, [], (), False, {}, before, (), out, None)
    _, out, _ = run(last, meta, [], (), False, {}, {0: landed[last]}, (), out, None)
    return out


def plane_work(context, hidden, chosen, weights_now, place, shard_weights, gain):
    batches, tok_rows, width = hidden.shape
    topk = chosen.shape[-1]
    tokens = batches * tok_rows
    nreq, ntp = lax.axis_size("req"), lax.axis_size("tp")
    me_index = lax.axis_index("req")
    hid_dev = shard_weights.shape[1] // 3
    resid = hidden.reshape(tokens, width).astype(jnp.float32)
    normed = (
        resid * gain / jnp.sqrt(jnp.mean(resid * resid, axis=-1, keepdims=True) + 1e-05)
    ).astype(jnp.bfloat16)
    flat_ids = chosen.reshape(-1)
    devices = jnp.arange(nreq, dtype=jnp.int32)
    holder = jnp.sum(jnp.where(flat_ids[:, None] == place[None, :], devices[None, :], 0), axis=1)
    assign_index = jnp.arange(flat_ids.shape[0], dtype=jnp.int32)
    batch_of = assign_index // (tok_rows * topk)
    earlier = (
        (flat_ids[:, None] == flat_ids[None, :])
        & (batch_of[:, None] == batch_of[None, :])
        & (assign_index[None, :] < assign_index[:, None])
    )
    rank_in = jnp.sum(earlier.astype(jnp.int32), axis=1)
    slot = (holder ^ me_index) * SLOTS + batch_of * CAP + rank_in
    slots = nreq * SLOTS
    hit = slot[:, None] == jnp.arange(slots, dtype=jnp.int32)[None, :]
    hit = hit.reshape(tokens, topk, slots)
    coef = jnp.sum(jnp.where(hit, weights_now.reshape(tokens, topk, 1), 0.0), axis=1)
    outgoing = jnp.dot(
        jnp.any(hit, axis=1).T.astype(jnp.bfloat16), normed, preferred_element_type=jnp.float32
    )
    outgoing = yield outgoing.astype(jnp.bfloat16)

    def exchanged(blocks):
        parts = [blocks[:SLOTS]]
        for k in range(1, nreq):
            part = blocks[k * SLOTS : (k + 1) * SLOTS]
            parts.append(lax.ppermute(part, "req", [(i, i ^ k) for i in range(nreq)]))
        return jnp.concatenate(parts)

    received = yield exchanged(outgoing)
    gate_up = jnp.dot(
        received, shard_weights[:, : 2 * hid_dev], preferred_element_type=jnp.float32
    )
    act = (jax.nn.silu(gate_up[:, :hid_dev]) * gate_up[:, hid_dev:]).astype(jnp.bfloat16)
    part = lax.dot_general(
        act,
        shard_weights[:, 2 * hid_dev :],
        (((1,), (1,)), ((), ())),
        preferred_element_type=jnp.float32,
    )
    part = yield part.astype(jnp.bfloat16)
    context = yield context
    returned = yield exchanged(part)
    partial_sum = jnp.dot(
        coef,
        returned.astype(jnp.float32),
        precision=lax.Precision.HIGHEST,
        preferred_element_type=jnp.float32,
    )
    tp_index = lax.axis_index("tp")
    tp_width = width // ntp

    def share_of(index):
        start = lax.rem(index, ntp) * tp_width
        return lax.dynamic_slice_in_dim(partial_sum, start, tp_width, 1)

    total = share_of(tp_index)
    for ahead in range(1, ntp):
        pairs = [(i, (i + ahead) % ntp) for i in range(ntp)]
        share = share_of(tp_index + ahead).astype(jnp.bfloat16)
        total = total + lax.ppermute(share, "tp", pairs).astype(jnp.float32)
    total = yield total
    resid_share = lax.dynamic_slice_in_dim(resid, tp_index * tp_width, tp_width, 1)
    summed = (resid_share + total).astype(jnp.bfloat16)
    return context, summed.reshape(batches, tok_rows, tp_width)


def attend(queries, new_keys, new_values, cache_keys, cache_values, lengths):
    batches, tok_rows, width = queries.shape
    heads = width // HEAD_SIZE
    pool = cache_keys.shape[0]
    scale = HEAD_SIZE ** (-0.5)
    req_lengths = lengths.reshape(-1)
    starts = jnp.cumsum(req_lengths) - req_lengths
    position = jnp.arange(pool, dtype=jnp.int32)
    owned = (position[None, :] >= starts[:, None]) & (
        position[None, :] < (starts + req_lengths)[:, None]
    )
    query_rows = queries.reshape(batches * tok_rows, heads, HEAD_SIZE)
    own_keys = new_keys.reshape(batches * tok_rows, heads, HEAD_SIZE)
    own_values = new_values.reshape(batches * tok_rows, heads, HEAD_SIZE)
    pool_keys = cache_keys.reshape(pool, heads, HEAD_SIZE)
    pool_values = cache_values.reshape(pool, heads, HEAD_SIZE)
    scores = (
        jnp.einsum("qhd,phd->hqp", query_rows, pool_keys, preferred_element_type=jnp.float32)
        * scale
    )
    scores = jnp.where(owned[None], scores, -jnp.inf)
    own_score = (
        jnp.einsum("qhd,qhd->hq", query_rows, own_keys, preferred_element_type=jnp.float32) * scale
    )
    highest = jnp.maximum(jnp.max(scores, axis=-1), own_score)
    exp_pool = jnp.exp(scores - highest[..., None])
    exp_own = jnp.exp(own_score - highest)
    denom = jnp.sum(exp_pool, axis=-1) + exp_own
    summed = jnp.einsum(
        "hqp,phd->qhd",
        exp_pool.astype(jnp.bfloat16),
        pool_values,
        preferred_element_type=jnp.float32,
    )
    prob_own = lax.optimization_barrier(exp_own.astype(jnp.bfloat16)).astype(jnp.float32)
    summed = summed + prob_own.T[:, :, None] * own_values.astype(jnp.float32)
    context = (summed / denom.T[:, :, None]).astype(jnp.bfloat16)
    return context.reshape(batches, tok_rows, width)


def choose_holders(place, me_index, nreq, shard_count):
    devices = jnp.arange(nreq, dtype=jnp.int32)
    holder = place[None, :] == jnp.arange(shard_count, dtype=jnp.int32)[:, None]
    before = (place[:, None] == place[None, :]) & (devices[:, None] < devices[None, :])
    rank_in = jnp.sum(before.astype(jnp.int32), axis=0)
    count = jnp.sum(holder.astype(jnp.int32), axis=1)
    wanted = me_index % count
    match = holder & (rank_in[None, :] == wanted[:, None])
    return jnp.sum(jnp.where(match, devices[None, :], 0), axis=1)


def expert_block(hidden, chosen, weights_now, place, shard_weights, gain):
    nreq = lax.axis_size("req")
    me_index = lax.axis_index("req")
    split_count = max(1, nreq // 16)
    shard_count = EXPERTS * split_count
    batches, tok_rows, width = hidden.shape
    topk = chosen.shape[-1]
    tokens = batches * tok_rows
    hid_dev = shard_weights.shape[1] // 3
    resid = hidden.reshape(tokens, width).astype(jnp.float32)
    normed = (
        resid * gain / jnp.sqrt(jnp.mean(resid * resid, axis=-1, keepdims=True) + 1e-05)
    ).astype(jnp.bfloat16)
    flat_ids = chosen.reshape(-1)
    assigns = flat_ids.shape[0]
    slots_dev = batches * CAP
    shard_dest = choose_holders(place, me_index, nreq, shard_count)
    shard_list = flat_ids[:, None] * split_count + jnp.arange(split_count, dtype=jnp.int32)[None, :]
    pick = shard_list[:, :, None] == jnp.arange(shard_count, dtype=jnp.int32)[None, None, :]
    dest = jnp.sum(jnp.where(pick, shard_dest[None, None, :], 0), axis=-1)
    assign_index = jnp.arange(assigns, dtype=jnp.int32)
    batch_of = assign_index // (tok_rows * topk)
    earlier = (
        (flat_ids[:, None] == flat_ids[None, :])
        & (batch_of[:, None] == batch_of[None, :])
        & (assign_index[None, :] < assign_index[:, None])
    )
    rank_in = jnp.sum(earlier.astype(jnp.int32), axis=1)
    slot = dest * slots_dev + (batch_of * CAP + rank_in)[:, None]
    slot_hit = slot[:, :, None] == jnp.arange(nreq * slots_dev, dtype=jnp.int32)[None, None, :]
    by_token = jnp.any(slot_hit.reshape(tokens, topk * split_count, nreq * slots_dev), axis=1)
    outgoing = jnp.dot(
        by_token.T.astype(jnp.bfloat16), normed, preferred_element_type=jnp.float32
    )
    outgoing = outgoing.astype(jnp.bfloat16).reshape(nreq, slots_dev, width)
    received = lax.all_to_all(outgoing, "req", split_axis=0, concat_axis=0, tiled=True)
    flat_rows = received.reshape(nreq * slots_dev, width)
    gate_up = jnp.dot(
        flat_rows, shard_weights[:, : 2 * hid_dev], preferred_element_type=jnp.float32
    )
    act = (jax.nn.silu(gate_up[:, :hid_dev]) * gate_up[:, hid_dev:]).astype(jnp.bfloat16)
    part = lax.dot_general(
        act,
        shard_weights[:, 2 * hid_dev :],
        (((1,), (1,)), ((), ())),
        preferred_element_type=jnp.float32,
    )
    part = part.astype(jnp.bfloat16).reshape(nreq, slots_dev, width)
    returned = lax.all_to_all(part, "req", split_axis=0, concat_axis=0, tiled=True)
    returned = returned.reshape(nreq * slots_dev, width)
    coef = jnp.sum(
        jnp.where(
            slot_hit.reshape(tokens, topk, split_count, nreq * slots_dev),
            weights_now.reshape(tokens, topk)[:, :, None, None],
            0.0,
        ),
        axis=(1, 2),
    )
    partial_sum = jnp.dot(
        coef,
        returned.astype(jnp.float32),
        precision=lax.Precision.HIGHEST,
        preferred_element_type=jnp.float32,
    )
    tp_width = width // lax.axis_size("tp")
    tp_start = lax.axis_index("tp") * tp_width
    resid_share = lax.dynamic_slice_in_dim(resid, tp_start, tp_width, 1)
    share = lax.psum_scatter(
        partial_sum.astype(jnp.bfloat16), "tp", scatter_dimension=1, tiled=True
    ).astype(jnp.float32)
    summed = (resid_share + share).astype(jnp.bfloat16)
    return summed.reshape(batches, tok_rows, tp_width)


def migrate(old_weights, old_place, new_place):
    nreq = lax.axis_size("req")
    shard_count = EXPERTS * max(1, nreq // 16)
    _, width, columns = old_weights.shape
    piece = width // nreq
    pieces = old_weights.reshape(nreq, piece, columns)
    spread = lax.all_to_all(pieces, "req", split_axis=0, concat_axis=0, tiled=True)
    devices = jnp.arange(nreq, dtype=jnp.int32)
    shard_ids = jnp.arange(shard_count, dtype=jnp.int32)
    first_old = jnp.min(
        jnp.where(old_place[None, :] == shard_ids[:, None], devices[None, :], nreq), axis=1
    )
    needed = jnp.sum(
        jnp.where(new_place[:, None] == shard_ids[None, :], first_old[None, :], 0), axis=1
    )
    sending = spread[needed]
    collected = lax.all_to_all(sending, "req", split_axis=0, concat_axis=0, tiled=True)
    return collected.reshape(1, width, columns)


def plane_outputs(attention, layer, new_place):
    *_, old_place, weights, _ = layer
    meta, early = plan_plane(old_place, new_place, weights)

    def within(total):
        def outputs(weights, meta, early, attention, layer):
            work = plane_work(attend(*attention), *layer)
            stage = next(work)
            done = None

            def beside(step, meta):
                nonlocal stage, done
                for _ in range(STAGES.get(step, 0)):
                    meta, value = lax.optimization_barrier((meta, stage))
                    try:
                        stage = work.send(value)
                    except StopIteration as end:
                        done = end.value
                return meta

            moved = migrate_plane(weights, meta, early, total, beside)
            return (*done, moved[None])

        return outputs

    branches = [within(total) for total in TOTALS]
    return lax.switch(meta[TOTAL_AT], branches, weights, meta, early, attention, layer)


def on_device(
    queries,
    new_keys,
    new_values,
    cache_keys,
    cache_values,
    lengths,
    hidden,
    gain,
    expert_ids,
    route_weights,
    old_place,
    new_place,
    old_weights,
):
    attention = (queries, new_keys, new_values, cache_keys, cache_values, lengths)
    layer = (hidden, expert_ids, route_weights, old_place, old_weights[0], gain)
    if lax.axis_size("req") == 8:
        return plane_outputs(attention, layer, new_place)
    context = attend(*attention)
    moved = migrate(old_weights, old_place, new_place)
    layer_out = expert_block(*layer)
    return (context, layer_out, moved)


def solution(mesh):
    in_specs = (
        P(None, "req", "tp"),
        P(None, "req", "tp"),
        P(None, "req", "tp"),
        P("req", "tp"),
        P("req", "tp"),
        P("req", None),
        P(None, "req", None),
        P(),
        P(None, "req", None),
        P(None, "req", None),
        P(),
        P(),
        P("req", None, "tp"),
    )
    out_specs = (P(None, "req", "tp"), P(None, "req", "tp"), P("req", None, "tp"))
    return jax.shard_map(
        on_device, mesh=mesh, in_specs=in_specs, out_specs=out_specs, check_vma=False
    )
```

```python
import functools

import jax
import jax.numpy as jnp
import numpy as np
from jax import lax
from jax.experimental import pallas as pl
from jax.experimental.pallas import tpu as pltpu
from jax.sharding import PartitionSpec as P

HEAD_SIZE = 64
EXPERTS = 8
CAP = 3
PIECES = 8
TOTALS = (9, 12, 16)
EARLY = 2
LAG = 5
ROOM = 16
SLOTS = 6
RIDE = 16
RIDES = 8
STAGES = {0: 1, 2: 2, 4: 2, 5: 1, 7: 2, 9: 2}
LOCAL_PIECES = {4: (0, 1), 5: (2, 3), 6: (4, 5), 7: (6, 7)}
PLAN_STEPS = max(TOTALS)
CORE_AT = 2 * PLAN_STEPS
SWAP_AT = CORE_AT + 1
LOCAL_AT = CORE_AT + 2
GOAL_AT = CORE_AT + 3
TOTAL_AT = CORE_AT + 11
META = CORE_AT + 12

ROUTES = (
    (((0, 0), (1, 1), (2, 2), (3, 3)), 9, 0x81020408102040810204081020408102040810204081020408102040810204081020408102040810204081020408102040810204081020408102040810204),
    (((0, 0), (1, 1), (2, 3), (2, 3)), 9, 0x81020408102040808203081020408082030810204080820308102040808203081020408082030810204080820308102040808203081020408082030810204),
    (((0, 0), (1, 1), (3, 3), (2, 2)), 12, 0x80820308102040808203081020408082030810204080820308102040808203261090408082032610904080820326489130808203264891304081830848213040818308482130408183081020404081830810204),
    (((0, 0), (1, 2), (1, 2), (3, 3)), 9, 0x81020408102040810204081020408102040810204224820408109112248204081091122480810408911224808104089110810081040820408100810408204),
    (((0, 0), (1, 2), (1, 3), (2, 3)), 9, 0x80820308109110808203081091108080830808911080808308089110808083080891108080830808911224808308089110808083080820408080810408204),
    (((0, 0), (1, 2), (2, 3), (1, 3)), 9, 0x81020408102040210203081020402102030810204024820308109040248203081090402482030408904024820304089040210203040820402102030408204),
    (((0, 0), (1, 2), (3, 3), (1, 2)), 12, 0x81020308102040810203081020408082030810204080820308102040208203261090402082032610904020820326089130208203260891302481830808913024818308089130208183040820402081830408204),
    (((0, 0), (1, 3), (1, 3), (2, 2)), 12, 0x80820408102040808204081020408082040810204080820308102110808203061091108080830610911080808306489112208083064891104080830648211040808106482110408083061020404080830610204),
    (((0, 0), (1, 3), (2, 3), (1, 2)), 9, 0x81020408102040208203061020402082030610204020820306102040208203061020402082030610204020820306102040208203061020402082030610204),
    (((0, 0), (2, 2), (1, 1), (3, 3)), 12, 0x81020408102040810204081020422482040810911224820408109112248081040891122480810408911224808104089112248081040891122480810408911224808104089110810081040820408100810408204),
    (((0, 0), (2, 2), (1, 3), (1, 3)), 12, 0x81020408102040810204081020408482040810911084820408109110248083040891102480830408911024808304089110248083040891102480830408911024808304089110210083040820402100830408204),
    (((0, 0), (2, 2), (3, 3), (1, 1)), 12, 0x210203081090402102030810911024820326089040248883260891102a8203040891302048830408913024818326089110204183260891102488830408913024888304089130204183040820402041830408204),
    (((0, 0), (2, 3), (1, 3), (1, 2)), 9, 0x20820306109110248203061091102080830608911020808304089110208083060891122080830608911020808306089110208081060820402080830608204),
    (((0, 1), (0, 1), (2, 3), (2, 3)), 9, 0x81020408102040808203080020108082030800201080820308002010808203080020108082030800201080820308002010808203080020108082030800201),
    (((0, 1), (0, 1), (3, 3), (2, 2)), 12, 0x80820308002010808203080020108082030800201080820308002010808203260090108082032600901080820326489130808203264891304081830848213040818308482130408183080020104081830800201),
    (((0, 1), (0, 2), (1, 3), (2, 3)), 12, 0x80820308002010808203080020108082030800201080820308002010808203080020108082030800201224820308009112248203080091122480810408911224808104089110808081040820108080810408201),
    (((0, 1), (0, 2), (2, 3), (1, 3)), 9, 0x84820408002040248203080020102482030400201024820304002010248203040020102482030400201024820304009010210203040020102102030408201),
    (((0, 1), (0, 2), (3, 3), (1, 2)), 12, 0x80820308002010808203080020108082030800201080820308002010208203260020102082032600201024820326009130248203260091302481830408913024818304089130208183040820102081830408201),
    (((0, 1), (0, 3), (1, 2), (2, 3)), 9, 0x221020408102012208204060020122082010600201220820106002012208201060020122082010600201220820106002110808201060020108080810600201),
    (((0, 1), (0, 3), (1, 3), (2, 2)), 12, 0x80820308002010808203080020108082030800201080820308002012208203060090122082030600901220820106489112208201064891104080810648211040808106482110408083060020104080830600201),
    (((0, 1), (0, 3), (2, 3), (1, 2)), 9, 0x81020408102040208203060020102082030600201020820306002010208203060020102082030600201020820306002010208203060020102082030600201),
    (((0, 1), (1, 2), (2, 3), (0, 3)), 9, 0x81020408102040848203084020108482030840201004820304402010048203044020100488030440901004880304409010000203040820100002030408201),
    (((0, 1), (1, 2), (3, 3), (0, 2)), 12, 0x80820308a0201080820308c020108082030840201080820308a020100082032640201000820326a0201004820326a09130048203264091300481830408913004818304089130008183040820100081830408201),
    (((0, 1), (1, 3), (0, 2), (2, 3)), 9, 0x81020408102040808004061020108080040610201080800406102010808004061020108080040610201080800406102010808004061020108080040610201),
    (((0, 1), (1, 3), (0, 3), (2, 2)), 12, 0x80820408102040808204081020408082040810204080820408102040808003061090108080030610901080800306489010808003064890104080030648201040800306482010408003061020104080030610201),
    (((0, 1), (2, 2), (0, 3), (1, 3)), 12, 0x81020408102040810204081020408482040810904084820408109040248003040890102480030408901024800304089010248003040890102480030408901024800304089010210003040820102100030408201),
    (((0, 1), (2, 2), (1, 3), (0, 3)), 12, 0x8482030840201084820308402010048203044020100482030440201004820304e0911004820304a0911224808304089012248083040890122488010408911224880104089110000081040820100000810408201),
    (((0, 1), (2, 2), (3, 3), (0, 1)), 12, 0x848203084020102e82032640901004820304409010048803260891300c8803040890102001830408913020080326089010248183260890102008030408913024880304089130200183040820102001830408201),
    (((0, 1), (2, 3), (0, 1), (2, 3)), 9, 0x220800406109012208004061090122480010608901220800106089012208001040890122080010608901220800106089110808001060820108080810608201),
    (((0, 1), (2, 3), (0, 3), (1, 2)), 9, 0x80820406109040208003061090102080030608901020800306089010208003060890102480030608901020800306089010208003040820102080030608201),
    (((0, 1), (2, 3), (1, 2), (0, 3)), 9, 0x22102040700901221080406c090122488010608901220080106089012200801040890122008010608901220080106089110000201060820100000810608201),
    (((0, 1), (2, 3), (1, 3), (0, 2)), 12, 0x8082030860201080820309202010808203084020100082030640901000820306e091100088030608901224808306089012200803060891122088010408911220008106089110000081060820100080810608201),
    (((0, 1), (2, 3), (2, 3), (0, 1)), 9, 0x21080406109040248803064090102008030608901000080304089010200803060890102008030608901020080306089010200203060820102002030608201),
    (((0, 1), (3, 3), (0, 1), (2, 2)), 12, 0x808204061020408082040610904220801306102012208013064891152080010610981040808106489812208013060c9010408013060c90122080010648981220800106489910408001060c2010408081060c201),
    (((0, 1), (3, 3), (1, 2), (0, 2)), 12, 0x8082040610204080820406102010808204061020122082130640211520821b061020100080810640981220881306a02010008813060c981220080106409912200801060c9910000081060c2010000081060c201),
    (((0, 3), (0, 2), (1, 3), (1, 2)), 12, 0x80820308002410808203080022908082030800211080821308002110248083260092902480832600191020809304089030208083040090302480932608191024809326089110208083040018302080830408183),
    (((0, 3), (0, 3), (1, 1), (2, 2)), 12, 0x80822b0800211080823b08002112208093060091122080b306009112208081064819122080810648191040808106009110408081060091122080932648191220809326481910408081060018304080810600183),
    (((0, 3), (0, 3), (1, 2), (1, 2)), 9, 0x21021306102110208213060021102080930600191020809306001910208093060019102080930600191220809326001910208084060018402080810600183),
    (((0, 3), (1, 2), (1, 2), (0, 3)), 9, 0x81020408102042248813264091122488132640911000008104081830000081040818322488132640911224881326409110000081040818300000810408183),
    (((0, 3), (1, 2), (1, 3), (0, 2)), 12, 0x80820308c0229080820308e02390808203084021108082030840231004809326a091100480932640911000808304081830008083040818300480932640911004809326409110008083040818300080830408183),
    (((0, 3), (2, 2), (1, 1), (0, 3)), 12, 0x2248c3b2640911224a813a64091100480810408903000008104081912249813040891122480ab5640911224808104081910048081040819122480810440911224809304409110000081040818300000810408183),
    (((0, 3), (2, 2), (1, 3), (0, 1)), 12, 0x24880326409110248803264091100000830408903000008304089032248803260891102488032608911020008104089030200083040890302488132608911224881326089110200083040818302000810408183),
    (((1, 1), (0, 0), (3, 3), (2, 2)), 16, 0x8082030800201080820308002010808203080020108082030800201080820308002010808203080020108082030800201080820308002010808203080020108082030800201080820308002010808203080020108082030800201080820308002010808203080020108082030800201),
    (((1, 1), (0, 2), (3, 3), (0, 2)), 16, 0x8082030800201080820308002010808203080020108082030800201080820308002010808203080020108082030800201080820308002010848203084020108482030840201004820304402010048203044020100488030440901004880304409010000203040820100002030408201),
    (((1, 1), (0, 3), (0, 3), (2, 2)), 12, 0x80820308002010808203080020108082030800201080820308002012208003060090122080030600901220801106489012208011064890104080110648081040801106480810408003060008104080030600081),
    (((1, 1), (2, 2), (3, 3), (0, 0)), 16, 0x8482030840201084820308402010048203044020100482030440201004820304402010048203044020100482030440201004820304402010048203044020100482030440201004820304402010048203044020100488030440901004880304409010000203040820100002030408201),
    (((1, 1), (2, 3), (0, 3), (0, 2)), 12, 0x80820308402010808203090020100080030640901220800306a09010048003060890122080110608901224880304095012208811060808100000110440901000001106400810008003060808100080030608081),
    (((1, 1), (3, 3), (0, 0), (2, 2)), 12, 0x220801306409012208013064090120080110648981200801106489810408000060c0810408000060c081220801306409012208013064090120080110648981200801106489810408000060c0810408000060c081),
    (((1, 2), (0, 3), (0, 3), (1, 2)), 9, 0x81020408102040208003060010102080030600101020800306001010208003060010102080030600101020800306001010208003060010102080030600101),
    (((1, 2), (0, 3), (1, 3), (0, 2)), 12, 0x80820308002010808203080020108082030800211080820308402012208083060010100088030640111220880106001010000083060010122008010640111220880306401110000081060010100000810600101),
    (((1, 2), (2, 3), (1, 3), (0, 0)), 12, 0x224880306401112248803064010100000810440101000080104401010048803064090100008030640911000080304081010000083060810122008030640911224880306409110000081060810100000810408101),
    (((1, 3), (0, 2), (1, 3), (0, 2)), 16, 0x8082030800201080820308002010808203080020108082030800201080820308002010808203080020108482130840211080821308402110048093044019100480932640191004809304401910048083040018300480930440191224881304409110008083040018100000810408181),
    (((1, 3), (2, 2), (1, 3), (0, 0)), 16, 0x8482030840201084820308402010048203044020100482030440201004821304402110048213044021100480830440191004809304401810048093044091100488130440191004808304081810000083044018122488130440911004881326409110000081040818100000830408183),
    (((1, 3), (2, 3), (0, 1), (0, 2)), 12, 0x220801306409012208813064090100480012608191000000106081812248093044090322080130640901000880104081810008001060819122000132640901220809306409010008001060818300080010608181),
    (((3, 3), (2, 2), (1, 1), (0, 0)), 16, 0x22488132640911224881326409110000081040818300000810408183224881326409112248813264091100000810408183000008104081832248813264091122488132640911000008104081830000081040818322488132640911224881326409110000081040818300000810408183),
)


def route_tables():
    pairs = [(a, b) for b in range(4) for a in range(b + 1)]
    pair_at = {pair: i for i, pair in enumerate(pairs)}
    row_of = np.zeros((79 * 128,), np.int32)
    rows = []
    seen = set()
    for goals, steps, code in ROUTES:
        for flip in range(8):
            names = []
            for chip in range(4):
                y, x = chip // 2 ^ (flip & 1), chip % 2 ^ (flip >> 1 & 1)
                names.append(x * 2 + y if flip & 4 else y * 2 + x)
            moved = [None] * 4
            for chip in range(4):
                moved[names[chip]] = tuple(sorted(names[g] for g in goals[chip]))
            key = sum(pair_at[moved[chip]] * 10**chip for chip in range(4))
            if key in seen:
                continue
            seen.add(key)
            row_of[key] = len(rows)
            rows.append(plan_of(moved, steps, code, names, flip >> 2))
    return row_of.reshape(79, 1, 128), np.stack(rows).reshape(-1, 1, 128)


def plan_of(goals, steps, code, names, swapped):
    back = [names.index(chip) for chip in range(4)]
    own = [{} for _ in range(4)]
    passing = [{} for _ in range(4)]
    for chip in range(4):
        for which in range(2):
            if goals[chip][which] != chip:
                pool = own[chip].setdefault(goals[chip][which], [])
                pool += [(piece, which) for piece in range(PIECES)]
                pool.sort()
    plan = np.full((4, 128), 3, np.int32)
    plan[:, 2 * PLAN_STEPS] = sum(steps > total for total in TOTALS)
    free = [[(0, slot) for slot in range(ROOM)] for _ in range(4)]
    for step in range(steps):
        landed = []
        for chip in range(4):
            for link in range(2):
                at = (step * 4 + back[chip]) * 2 + (link ^ swapped)
                goal, since = code >> 7 * at & 7, code >> 7 * at + 3 & 15
                if goal == 4:
                    continue
                goal = names[goal]
                if since == 0:
                    piece, which = own[chip][goal].pop(-link)
                    source, sent = chip, which | piece << 2
                else:
                    which, piece, source, slot = passing[chip].pop((step - since, 1 - link))
                    sent = 2 | slot << 2
                    free[chip].append((max(step, step - since + LAG), slot))
                plan[chip, 2 * step + link] += sent - 3
                landed.append((chip ^ 1 << link, link, source, which, piece, goal))
        for chip, link, source, which, piece, goal in landed:
            got = (source * 2 + which) << 9 | piece << 12
            if goal == chip:
                got |= 1 << 7
            else:
                at = next(i for i, item in enumerate(free[chip]) if item[0] <= step)
                slot = free[chip].pop(at)[1]
                got |= 2 << 7 | slot << 16
                passing[chip][step, link] = (which, piece, source, slot)
            plan[chip, 2 * step + link] |= got
    assert not any(passing) and not any(pool for chip in own for pool in chip.values())
    return plan


def copy_all(moves, sems, base, phase):
    for number, (condition, source, target) in enumerate(moves):

        def act(number=number, source=source, target=target):
            copy = pltpu.make_async_copy(source, target, sems.at[base + number])
            if phase == 0:
                copy.start()
            else:
                copy.wait()

        if condition is True:
            act()
        else:
            pl.when(condition)(act)


def piece_rows(ref, row, rows):
    return ref.at[pl.ds(pl.multiple_of(row, 16), rows)]


def link_of(step, core):
    return 1 - core if step // 2 % 2 else core


def early_kernel(weights, early, semaphores):
    rows = weights.shape[0] // PIECES
    core = lax.axis_index("req") % 2
    copies = []
    for number in range(EARLY):
        piece = jnp.where(core == 1, number, PIECES - 1 - number)
        part = piece_rows(weights, piece * rows, rows)
        copies.append(pltpu.make_async_copy(part, piece_rows(early, number * rows, rows), semaphores.at[number]))
        copies[-1].start()
    for copy in copies:
        copy.wait()


def plan_kernel(old_place, new_place, row_of, plans, meta, row_part, plan_part, sem):
    me_index = lax.axis_index("req")
    core = me_index % 2
    chip = me_index // 2
    goals = []
    for holder in range(8):
        goal = jnp.int32(0)
        for device in range(8):
            goal = jnp.where(new_place[device] == old_place[holder], device, goal)
        goals.append(goal)
    key = jnp.int32(0)
    my_swap = jnp.int32(0)
    for at in range(4):
        first, second = goals[2 * at], goals[2 * at + 1]
        low, high = jnp.minimum(first, second), jnp.maximum(first, second)
        high_chip = high // 2
        key = key + (high_chip * (high_chip + 1) // 2 + low // 2) * 10**at
        my_swap = jnp.where((first > second) & (chip == at), 1, my_swap)
        meta[GOAL_AT + 2 * at] = low % 2
        meta[GOAL_AT + 2 * at + 1] = high % 2
    meta[CORE_AT] = core
    meta[SWAP_AT] = my_swap
    wanted = new_place[me_index]
    beside = jnp.where(wanted == old_place[me_index + 1 - 2 * core], 2, 0)
    meta[LOCAL_AT] = jnp.where(wanted == old_place[me_index], 1, beside)
    copy = pltpu.make_async_copy(row_of.at[key // 128], row_part, sem)
    copy.start()
    copy.wait()
    row = row_part[0, key % 128]
    copy = pltpu.make_async_copy(plans.at[row * 4 + chip], plan_part, sem)
    copy.start()
    copy.wait()
    for at in range(2 * PLAN_STEPS):
        meta[at] = plan_part[0, at]
    meta[TOTAL_AT] = plan_part[0, 2 * PLAN_STEPS]


def step_kernel(rows, step, come, local_pieces, names, count, meta, *refs):
    refs = list(zip(names, refs))
    semaphores = refs.pop()[1]
    given = {}
    for number, (name, ref) in enumerate(refs):
        if number >= count or name not in ("out", "room"):
            given.setdefault(name, []).append(ref)
    w_hbm = given["weights"][0]
    out_hbm = given.get("out", [None])[0]
    room = given.get("room", [None])[0]
    core = meta[CORE_AT]
    local = meta[LOCAL_AT]
    used = 0
    stores, moves = [], []
    swap = given.get("swap", [None])[0]
    brought = [("landed", core, step_at) for step_at in come[0]]
    brought += [("swapped", 1 - core, step_at) for step_at in come[1]]
    for name, side, step_at in brought:
        word = meta[2 * step_at + link_of(step_at, side)]
        kind = (word >> 7) & 3
        row = ((word >> 12) & 15) * rows
        source = given[name].pop(0).at[pl.ds(0, rows)]
        if room is not None:
            slot = (word >> 16) & 31
            stores.append((kind == 2, source, piece_rows(room, slot * rows, rows)))
        final = (kind == 1) & (meta[GOAL_AT + ((word >> 9) & 7)] == core)
        moves.append((final, source, piece_rows(out_hbm, row, rows)))
        if name == "landed" and swap is not None:
            moves.append((jnp.logical_not(final), source, swap))
    copy_all(stores, semaphores, used, 0)
    copy_all(stores, semaphores, used, 1)
    used += len(stores)
    riding = []
    if "sent" in given:
        target = given["sent"][0].at[pl.ds(0, rows)]
        if "extra" in given:
            riding.append((True, given["extra"][0], given["sent"][0].at[pl.ds(rows, RIDE)]))
        word = meta[2 * step + link_of(step, core)]
        kind = word & 3
        piece = (word >> 2) & 31
        held = kind == 2
        mine = ((kind ^ meta[SWAP_AT]) == core) | (kind == 3)
        theirs = jnp.logical_not(held | mine)
        options = [(jnp.logical_not(held) & mine, piece_rows(w_hbm, piece * rows, rows))]
        if "other" in given:
            options.append((theirs, piece_rows(given["other"][0], piece * rows, rows)))
        place = jnp.where(core == 0, piece, PIECES - 1 - piece)
        if "early" in given:
            options.append((theirs, piece_rows(given["early"][0], place * rows, rows)))
        if room is not None:
            options.append((held, piece_rows(room, piece * rows, rows)))
        for condition, source in options:

            @pl.when(condition)
            def _(source=source):
                pltpu.make_async_copy(source, target, semaphores.at[used]).start()

        fetched = pltpu.make_async_copy(w_hbm.at[pl.ds(0, rows)], target, semaphores.at[used])
        used += 1
    copy_all(riding, semaphores, used, 0)
    first_ride = used
    used += len(riding)
    copy_all(moves, semaphores, used, 0)
    first_move = used
    used += len(moves)
    reads, writes = [], []
    for number, piece in enumerate(local_pieces):
        part = given["staged"][0].at[number]
        row = piece * rows
        reads.append((local == 1, piece_rows(w_hbm, row, rows), part))
        reads.append((local == 2, piece_rows(given["other"][0], row, rows), part))
        writes.append((local != 0, part, piece_rows(out_hbm, row, rows)))
    copy_all(reads, semaphores, used, 0)
    if "sent" in given:
        fetched.wait()
    copy_all(riding, semaphores, first_ride, 1)
    copy_all(reads, semaphores, used, 1)
    used += len(reads)
    copy_all(writes, semaphores, used, 0)
    copy_all(moves, semaphores, first_move, 1)
    copy_all(writes, semaphores, used, 1)


def between_cores(array):
    return lax.ppermute(array, "req", [(i, i ^ 1) for i in range(8)])


def along_links(array, step):
    return lax.ppermute(array, "req", [(i, i ^ (2 << link_of(step, i % 2))) for i in range(8)])


def plan_plane(old_place, new_place):
    row_of, plans = route_tables()
    smem = pl.BlockSpec(memory_space=pltpu.SMEM)
    anywhere = pl.BlockSpec(memory_space=pl.ANY)
    return pl.pallas_call(
        plan_kernel,
        out_shape=jax.ShapeDtypeStruct((META,), jnp.int32),
        in_specs=[smem, smem, anywhere, anywhere],
        out_specs=smem,
        scratch_shapes=[
            pltpu.SMEM((1, 128), jnp.int32),
            pltpu.SMEM((1, 128), jnp.int32),
            pltpu.SemaphoreType.DMA,
        ],
        name="plan_steps",
    )(old_place, new_place, jnp.asarray(row_of), jnp.asarray(plans))


def early_pieces(weights):
    width, columns = weights.shape
    return pl.pallas_call(
        early_kernel,
        out_shape=jax.ShapeDtypeStruct((width // PIECES * EARLY, columns), weights.dtype),
        in_specs=[pl.BlockSpec(memory_space=pl.ANY)],
        out_specs=pl.BlockSpec(memory_space=pltpu.VMEM),
        scratch_shapes=[pltpu.SemaphoreType.DMA((EARLY,))],
        compiler_params=pltpu.CompilerParams(vmem_limit_bytes=32 << 20),
        name="early_pieces",
    )(weights)


def migrate_plane(weights, meta, early, total, beside):
    width, columns = weights.shape
    rows = width // PIECES
    smem = pl.BlockSpec(memory_space=pltpu.SMEM)
    anywhere = pl.BlockSpec(memory_space=pl.ANY)
    near = pl.BlockSpec(memory_space=pltpu.VMEM)
    whole = jax.ShapeDtypeStruct((width, columns), weights.dtype)
    room_like = jax.ShapeDtypeStruct((ROOM * rows, columns), weights.dtype)
    held = {"out": None, "room": None}

    def run(meta, step, come, sources, local_pieces, extra, store, swap):
        operands, specs, names, aliases = [meta, weights], [smem, anywhere], ["weights"], {}

        def add(name, array, spec):
            if array is not None:
                operands.append(array)
                specs.append(spec)
                names.append(name)

        for name, array in sources:
            add(name, array, anywhere)
        for step_at in come[0]:
            add("landed", landed[step_at], near)
        for step_at in come[1]:
            add("swapped", swapped[step_at], near)
        add("extra", extra, near)
        results = []
        if step is not None:
            sent_rows = rows + (RIDE if step < RIDES else 0)
            results.append(("sent", jax.ShapeDtypeStruct((sent_rows, columns), weights.dtype), near))
        if swap:
            like = jax.ShapeDtypeStruct((rows, columns), weights.dtype)
            results.append(("swap", like, near))
        for name, like, wanted in (
            ("out", whole, bool(local_pieces or come[0] or come[1])),
            ("room", room_like, store),
        ):
            if wanted:
                if held[name] is not None:
                    aliases[len(operands)] = len(results)
                    add(name, held[name], anywhere)
                results.append((name, like, anywhere))
        count = len(names)
        names += [name for name, _, _ in results]
        scratch = []
        if local_pieces:
            scratch.append(pltpu.VMEM((len(local_pieces), rows, columns), weights.dtype))
            names.append("staged")
        scratch.append(pltpu.SemaphoreType.DMA((24,)))
        names.append("semaphores")
        values = pl.pallas_call(
            functools.partial(
                step_kernel, rows, step, come, local_pieces, names, count
            ),
            out_shape=[like for _, like, _ in results],
            in_specs=specs,
            out_specs=[spec for _, _, spec in results],
            scratch_shapes=scratch,
            input_output_aliases=aliases,
            compiler_params=pltpu.CompilerParams(vmem_limit_bytes=32 << 20),
            cost_estimate=pl.CostEstimate(
                flops=0, bytes_accessed=4 * rows * columns * 2, transcendentals=0
            ),
            name="place_pieces" if step is None else "step_pieces",
        )(*operands)
        for (name, _, _), value in zip(results, values):
            if name in held:
                held[name] = value
        return values

    landed, swapped = {}, {}
    ridden = None
    other = between_cores(weights)
    for step in range(total):
        meta, extra = beside(step, meta, ridden)
        come = [step - 2] if step >= 2 else [], [step - LAG] if step >= LAG else []
        sources = [("early", early) if step < EARLY else ("other", other)]
        local_pieces = LOCAL_PIECES.get(step, ())
        some = step >= 2
        values = run(meta, step, come, sources, local_pieces, extra, some, some)
        meta, _ = lax.optimization_barrier((meta, values[0]))
        landed[step] = along_links(values[0], step)
        if extra is not None:
            ridden = landed[step][rows:]
        if some:
            swapped[step - 2] = between_cores(values[1])
    last = total - 1
    meta, _ = beside(total, meta, ridden)
    come = [last - 1], list(range(total - LAG, last - 2))
    values = run(meta, None, come, (), (), None, False, True)
    swapped[last - 1] = between_cores(values[0])
    swapped[last] = between_cores(landed[last])
    run(meta, None, ([last], [last - 2]), (), (), None, False, False)
    run(meta, None, ([], [last - 1, last]), (), (), None, False, False)
    return held["out"]


def plane_dispatch(hidden, chosen, weights_now, place, gain):
    batches, tok_rows, width = hidden.shape
    topk = chosen.shape[-1]
    tokens = batches * tok_rows
    nreq = lax.axis_size("req")
    me_index = lax.axis_index("req")
    resid = hidden.reshape(tokens, width).astype(jnp.float32)
    normed = (
        resid * gain / jnp.sqrt(jnp.mean(resid * resid, axis=-1, keepdims=True) + 1e-05)
    ).astype(jnp.bfloat16)
    flat_ids = chosen.reshape(-1)
    devices = jnp.arange(nreq, dtype=jnp.int32)
    holder = jnp.sum(jnp.where(flat_ids[:, None] == place[None, :], devices[None, :], 0), axis=1)
    assign_index = jnp.arange(flat_ids.shape[0], dtype=jnp.int32)
    batch_of = assign_index // (tok_rows * topk)
    earlier = (
        (flat_ids[:, None] == flat_ids[None, :])
        & (batch_of[:, None] == batch_of[None, :])
        & (assign_index[None, :] < assign_index[:, None])
    )
    rank_in = jnp.sum(earlier.astype(jnp.int32), axis=1)
    slot = (holder ^ me_index) * SLOTS + batch_of * CAP + rank_in
    hit = slot[:, None] == jnp.arange(nreq * SLOTS, dtype=jnp.int32)[None, :]
    hit = hit.reshape(tokens, topk, nreq * SLOTS)
    coef = jnp.sum(jnp.where(hit, weights_now.reshape(tokens, topk, 1), 0.0), axis=1)
    blocks = jnp.any(hit, axis=1).T
    order = [k for k in range(nreq) if k & 1] + [k for k in range(nreq) if not k & 1]
    blocks = blocks.reshape(nreq, SLOTS, tokens)[jnp.array(order)].reshape(nreq * SLOTS, tokens)
    outgoing = jnp.dot(
        blocks.astype(jnp.bfloat16), normed, preferred_element_type=jnp.float32
    ).astype(jnp.bfloat16)
    half = nreq * SLOTS // 2
    came = between_cores(outgoing[:half])
    return jnp.concatenate([came, outgoing[half:]]), coef


def reordered(rows, orders):
    core = lax.axis_index("req") % 2
    spread = [np.eye(rows.shape[0], dtype=np.float32)[np.array(order)] for order in orders]
    chosen = jnp.where(core == 0, spread[0], spread[1]).astype(rows.dtype)
    return jnp.dot(chosen, rows, preferred_element_type=jnp.float32).astype(rows.dtype)


def exchange(rows, labels, bits):
    orders = []
    for core in range(2):
        going = [i for i, label in enumerate(labels[core]) if label // SLOTS >> bits[core] & 1]
        orders.append(going + [i for i in range(len(labels[core])) if i not in going])
    rows = reordered(rows, orders)
    half = rows.shape[0] // 2
    came = yield bits[0] > 0, rows[:half]
    labels = [[labels[core][i] for i in orders[core]] for core in range(2)]
    if bits[0] == 0:
        labels = [labels[1 - core][:half] + labels[core][half:] for core in range(2)]
    return jnp.concatenate([came, rows[half:]]), labels


def plane_work(attention, hidden, rows, coef, shard_weights):
    batches, tok_rows, width = hidden.shape
    tokens = batches * tok_rows
    ntp = lax.axis_size("tp")
    hid_dev = shard_weights.shape[1] // 3
    every = range(rows.shape[0])
    first = [i for i in every if i // SLOTS & 1] + [i for i in every if not i // SLOTS & 1]
    labels = [first, first]
    rows, labels = yield from exchange(rows, labels, (1, 2))
    rows, labels = yield from exchange(rows, labels, (2, 1))
    gate_up = jnp.dot(rows, shard_weights[:, : 2 * hid_dev], preferred_element_type=jnp.float32)
    act = (jax.nn.silu(gate_up[:, :hid_dev]) * gate_up[:, hid_dev:]).astype(jnp.bfloat16)
    part = lax.dot_general(
        act,
        shard_weights[:, 2 * hid_dev :],
        (((1,), (1,)), ((), ())),
        preferred_element_type=jnp.float32,
    )
    rows = part.astype(jnp.bfloat16)
    context = yield False, attend(*attention)
    swap = exchange(rows, labels, (0, 0))
    _, going = next(swap)
    try:
        swap.send(between_cores(going))
    except StopIteration as end:
        rows, labels = end.value
    rows, labels = yield from exchange(rows, labels, (1, 2))
    rows, labels = yield from exchange(rows, labels, (2, 1))
    rows = reordered(rows, [[label.index(i) for i in every] for label in labels])
    partial_sum = jnp.dot(
        coef,
        rows.astype(jnp.float32),
        precision=lax.Precision.HIGHEST,
        preferred_element_type=jnp.float32,
    )
    tp_index = lax.axis_index("tp")
    tp_width = width // ntp

    def share_of(index):
        start = lax.rem(index, ntp) * tp_width
        return lax.dynamic_slice_in_dim(partial_sum, start, tp_width, 1)

    total = share_of(tp_index)
    for ahead in range(1, ntp):
        pairs = [(i, (i + ahead) % ntp) for i in range(ntp)]
        share = share_of(tp_index + ahead).astype(jnp.bfloat16)
        total = total + lax.ppermute(share, "tp", pairs).astype(jnp.float32)
    total = yield False, total
    resid = hidden.reshape(tokens, width).astype(jnp.float32)
    resid_share = lax.dynamic_slice_in_dim(resid, tp_index * tp_width, tp_width, 1)
    summed = (resid_share + total).astype(jnp.bfloat16)
    return context, summed.reshape(batches, tok_rows, tp_width)


def attend(queries, new_keys, new_values, cache_keys, cache_values, lengths):
    batches, tok_rows, width = queries.shape
    heads = width // HEAD_SIZE
    pool = cache_keys.shape[0]
    scale = HEAD_SIZE ** (-0.5)
    req_lengths = lengths.reshape(-1)
    starts = jnp.cumsum(req_lengths) - req_lengths
    position = jnp.arange(pool, dtype=jnp.int32)
    owned = (position[None, :] >= starts[:, None]) & (
        position[None, :] < (starts + req_lengths)[:, None]
    )
    query_rows = queries.reshape(batches * tok_rows, heads, HEAD_SIZE)
    own_keys = new_keys.reshape(batches * tok_rows, heads, HEAD_SIZE)
    own_values = new_values.reshape(batches * tok_rows, heads, HEAD_SIZE)
    pool_keys = cache_keys.reshape(pool, heads, HEAD_SIZE)
    pool_values = cache_values.reshape(pool, heads, HEAD_SIZE)
    scores = (
        jnp.einsum("qhd,phd->hqp", query_rows, pool_keys, preferred_element_type=jnp.float32)
        * scale
    )
    scores = jnp.where(owned[None], scores, -jnp.inf)
    own_score = (
        jnp.einsum("qhd,qhd->hq", query_rows, own_keys, preferred_element_type=jnp.float32) * scale
    )
    highest = jnp.maximum(jnp.max(scores, axis=-1), own_score)
    exp_pool = jnp.exp(scores - highest[..., None])
    exp_own = jnp.exp(own_score - highest)
    denom = jnp.sum(exp_pool, axis=-1) + exp_own
    summed = jnp.einsum(
        "hqp,phd->qhd",
        exp_pool.astype(jnp.bfloat16),
        pool_values,
        preferred_element_type=jnp.float32,
    )
    prob_own = lax.optimization_barrier(exp_own.astype(jnp.bfloat16)).astype(jnp.float32)
    summed = summed + prob_own.T[:, :, None] * own_values.astype(jnp.float32)
    context = (summed / denom.T[:, :, None]).astype(jnp.bfloat16)
    return context.reshape(batches, tok_rows, width)


def choose_holders(place, me_index, nreq, shard_count):
    devices = jnp.arange(nreq, dtype=jnp.int32)
    holder = place[None, :] == jnp.arange(shard_count, dtype=jnp.int32)[:, None]
    before = (place[:, None] == place[None, :]) & (devices[:, None] < devices[None, :])
    rank_in = jnp.sum(before.astype(jnp.int32), axis=0)
    count = jnp.sum(holder.astype(jnp.int32), axis=1)
    wanted = me_index % count
    match = holder & (rank_in[None, :] == wanted[:, None])
    return jnp.sum(jnp.where(match, devices[None, :], 0), axis=1)


def expert_block(hidden, chosen, weights_now, place, shard_weights, gain):
    nreq = lax.axis_size("req")
    me_index = lax.axis_index("req")
    split_count = max(1, nreq // 16)
    shard_count = EXPERTS * split_count
    batches, tok_rows, width = hidden.shape
    topk = chosen.shape[-1]
    tokens = batches * tok_rows
    hid_dev = shard_weights.shape[1] // 3
    resid = hidden.reshape(tokens, width).astype(jnp.float32)
    normed = (
        resid * gain / jnp.sqrt(jnp.mean(resid * resid, axis=-1, keepdims=True) + 1e-05)
    ).astype(jnp.bfloat16)
    flat_ids = chosen.reshape(-1)
    assigns = flat_ids.shape[0]
    slots_dev = batches * CAP
    shard_dest = choose_holders(place, me_index, nreq, shard_count)
    shard_list = flat_ids[:, None] * split_count + jnp.arange(split_count, dtype=jnp.int32)[None, :]
    pick = shard_list[:, :, None] == jnp.arange(shard_count, dtype=jnp.int32)[None, None, :]
    dest = jnp.sum(jnp.where(pick, shard_dest[None, None, :], 0), axis=-1)
    assign_index = jnp.arange(assigns, dtype=jnp.int32)
    batch_of = assign_index // (tok_rows * topk)
    earlier = (
        (flat_ids[:, None] == flat_ids[None, :])
        & (batch_of[:, None] == batch_of[None, :])
        & (assign_index[None, :] < assign_index[:, None])
    )
    rank_in = jnp.sum(earlier.astype(jnp.int32), axis=1)
    slot = dest * slots_dev + (batch_of * CAP + rank_in)[:, None]
    slot_hit = slot[:, :, None] == jnp.arange(nreq * slots_dev, dtype=jnp.int32)[None, None, :]
    by_token = jnp.any(slot_hit.reshape(tokens, topk * split_count, nreq * slots_dev), axis=1)
    outgoing = jnp.dot(
        by_token.T.astype(jnp.bfloat16), normed, preferred_element_type=jnp.float32
    )
    outgoing = outgoing.astype(jnp.bfloat16).reshape(nreq, slots_dev, width)
    received = lax.all_to_all(outgoing, "req", split_axis=0, concat_axis=0, tiled=True)
    flat_rows = received.reshape(nreq * slots_dev, width)
    gate_up = jnp.dot(
        flat_rows, shard_weights[:, : 2 * hid_dev], preferred_element_type=jnp.float32
    )
    act = (jax.nn.silu(gate_up[:, :hid_dev]) * gate_up[:, hid_dev:]).astype(jnp.bfloat16)
    part = lax.dot_general(
        act,
        shard_weights[:, 2 * hid_dev :],
        (((1,), (1,)), ((), ())),
        preferred_element_type=jnp.float32,
    )
    part = part.astype(jnp.bfloat16).reshape(nreq, slots_dev, width)
    returned = lax.all_to_all(part, "req", split_axis=0, concat_axis=0, tiled=True)
    returned = returned.reshape(nreq * slots_dev, width)
    coef = jnp.sum(
        jnp.where(
            slot_hit.reshape(tokens, topk, split_count, nreq * slots_dev),
            weights_now.reshape(tokens, topk)[:, :, None, None],
            0.0,
        ),
        axis=(1, 2),
    )
    partial_sum = jnp.dot(
        coef,
        returned.astype(jnp.float32),
        precision=lax.Precision.HIGHEST,
        preferred_element_type=jnp.float32,
    )
    tp_width = width // lax.axis_size("tp")
    tp_start = lax.axis_index("tp") * tp_width
    resid_share = lax.dynamic_slice_in_dim(resid, tp_start, tp_width, 1)
    share = lax.psum_scatter(
        partial_sum.astype(jnp.bfloat16), "tp", scatter_dimension=1, tiled=True
    ).astype(jnp.float32)
    summed = (resid_share + share).astype(jnp.bfloat16)
    return summed.reshape(batches, tok_rows, tp_width)


def migrate(old_weights, old_place, new_place):
    nreq = lax.axis_size("req")
    shard_count = EXPERTS * max(1, nreq // 16)
    _, width, columns = old_weights.shape
    piece = width // nreq
    pieces = old_weights.reshape(nreq, piece, columns)
    spread = lax.all_to_all(pieces, "req", split_axis=0, concat_axis=0, tiled=True)
    devices = jnp.arange(nreq, dtype=jnp.int32)
    shard_ids = jnp.arange(shard_count, dtype=jnp.int32)
    first_old = jnp.min(
        jnp.where(old_place[None, :] == shard_ids[:, None], devices[None, :], nreq), axis=1
    )
    needed = jnp.sum(
        jnp.where(new_place[:, None] == shard_ids[None, :], first_old[None, :], 0), axis=1
    )
    sending = spread[needed]
    collected = lax.all_to_all(sending, "req", split_axis=0, concat_axis=0, tiled=True)
    return collected.reshape(1, width, columns)


def plane_outputs(attention, layer, new_place):
    hidden, expert_ids, route_weights, old_place, weights, gain = layer
    early = early_pieces(weights)
    first = between_cores(early)
    hidden, _ = lax.optimization_barrier((hidden, early))
    meta = plan_plane(old_place, new_place)
    received, coef = plane_dispatch(hidden, expert_ids, route_weights, old_place, gain)

    def within(total):
        def outputs(weights, meta, first, attention, hidden, rows, coef):
            work = plane_work(attention, hidden, rows, coef, weights)
            stage = next(work)
            done = None
            pending = []

            def beside(step, meta, ridden):
                nonlocal stage, done
                for _ in range(STAGES.get(step, 0)):
                    rides, value = stage
                    if pending:
                        pending.pop()
                        half = value.shape
                        value = ridden.reshape(half)
                    elif rides:
                        pending.append(True)
                        return meta, value.reshape(RIDE, weights.shape[1])
                    else:
                        meta, value = lax.optimization_barrier((meta, value))
                    try:
                        stage = work.send(value)
                    except StopIteration as end:
                        done = end.value
                return meta, None

            moved = migrate_plane(
                weights, meta, first, total, beside
            )
            return (*done, moved[None])

        return outputs

    branches = [within(total) for total in TOTALS]
    return lax.switch(meta[TOTAL_AT], branches, weights, meta, first, attention, hidden, received, coef)


def on_device(
    queries,
    new_keys,
    new_values,
    cache_keys,
    cache_values,
    lengths,
    hidden,
    gain,
    expert_ids,
    route_weights,
    old_place,
    new_place,
    old_weights,
):
    attention = (queries, new_keys, new_values, cache_keys, cache_values, lengths)
    layer = (hidden, expert_ids, route_weights, old_place, old_weights[0], gain)
    if lax.axis_size("req") == 8:
        return plane_outputs(attention, layer, new_place)
    context = attend(*attention)
    moved = migrate(old_weights, old_place, new_place)
    layer_out = expert_block(*layer)
    return (context, layer_out, moved)


def solution(mesh):
    in_specs = (
        P(None, "req", "tp"),
        P(None, "req", "tp"),
        P(None, "req", "tp"),
        P("req", "tp"),
        P("req", "tp"),
        P("req", None),
        P(None, "req", None),
        P(),
        P(None, "req", None),
        P(None, "req", None),
        P(),
        P(),
        P("req", None, "tp"),
    )
    out_specs = (P(None, "req", "tp"), P(None, "req", "tp"), P("req", None, "tp"))
    return jax.shard_map(
        on_device, mesh=mesh, in_specs=in_specs, out_specs=out_specs, check_vma=False
    )
```

```python
import functools

import jax
import jax.numpy as jnp
import numpy as np
from jax import lax
from jax.experimental import pallas as pl
from jax.experimental.pallas import tpu as pltpu
from jax.sharding import PartitionSpec as P

HEAD_SIZE = 64
EXPERTS = 8
CAP = 3
PIECES = 8
TOTALS = (9, 12, 16)
EARLY = 2
LAG = 5
ROOM = 16
SLOTS = 6
RIDE = 16
RIDES = 8
STAGES = {0: 1, 2: 2, 4: 2, 5: 1, 7: 2}
LOCAL_PIECES = {4: (0, 1), 5: (2, 3), 6: (4, 5), 7: (6, 7)}
PLAN_STEPS = max(TOTALS)
CORE_AT = 2 * PLAN_STEPS
SWAP_AT = CORE_AT + 1
LOCAL_AT = CORE_AT + 2
GOAL_AT = CORE_AT + 3
TOTAL_AT = CORE_AT + 11
META = CORE_AT + 12

ROUTES = (
    (((0, 0), (1, 1), (2, 2), (3, 3)), 9, 0x81020408102040810204081020408102040810204081020408102040810204081020408102040810204081020408102040810204081020408102040810204),
    (((0, 0), (1, 1), (2, 3), (2, 3)), 9, 0x81020408102040808203081020408082030810204080820308102040808203081020408082030810204080820308102040808203081020408082030810204),
    (((0, 0), (1, 1), (3, 3), (2, 2)), 12, 0x80820308102040808203081020408082030810204080820308102040808203261090408082032610904080820326489130808203264891304081830848213040818308482130408183081020404081830810204),
    (((0, 0), (1, 2), (1, 2), (3, 3)), 9, 0x81020408102040810204081020408102040810204224820408109112248204081091122480810408911224808104089110810081040820408100810408204),
    (((0, 0), (1, 2), (1, 3), (2, 3)), 9, 0x80820308109110808203081091108080830808911080808308089110808083080891108080830808911224808308089110808083080820408080810408204),
    (((0, 0), (1, 2), (2, 3), (1, 3)), 9, 0x81020408102040210203081020402102030810204024820308109040248203081090402482030408904024820304089040210203040820402102030408204),
    (((0, 0), (1, 2), (3, 3), (1, 2)), 12, 0x81020308102040810203081020408082030810204080820308102040208203261090402082032610904020820326089130208203260891302481830808913024818308089130208183040820402081830408204),
    (((0, 0), (1, 3), (1, 3), (2, 2)), 12, 0x80820408102040808204081020408082040810204080820308102110808203061091108080830610911080808306489112208083064891104080830648211040808106482110408083061020404080830610204),
    (((0, 0), (1, 3), (2, 3), (1, 2)), 9, 0x81020408102040208203061020402082030610204020820306102040208203061020402082030610204020820306102040208203061020402082030610204),
    (((0, 0), (2, 2), (1, 1), (3, 3)), 12, 0x81020408102040810204081020422482040810911224820408109112248081040891122480810408911224808104089112248081040891122480810408911224808104089110810081040820408100810408204),
    (((0, 0), (2, 2), (1, 3), (1, 3)), 12, 0x81020408102040810204081020408482040810911084820408109110248083040891102480830408911024808304089110248083040891102480830408911024808304089110210083040820402100830408204),
    (((0, 0), (2, 2), (3, 3), (1, 1)), 12, 0x210203081090402102030810911024820326089040248883260891102a8203040891302048830408913024818326089110204183260891102488830408913024888304089130204183040820402041830408204),
    (((0, 0), (2, 3), (1, 3), (1, 2)), 9, 0x20820306109110248203061091102080830608911020808304089110208083060891122080830608911020808306089110208081060820402080830608204),
    (((0, 1), (0, 1), (2, 3), (2, 3)), 9, 0x81020408102040808203080020108082030800201080820308002010808203080020108082030800201080820308002010808203080020108082030800201),
    (((0, 1), (0, 1), (3, 3), (2, 2)), 12, 0x80820308002010808203080020108082030800201080820308002010808203260090108082032600901080820326489130808203264891304081830848213040818308482130408183080020104081830800201),
    (((0, 1), (0, 2), (1, 3), (2, 3)), 12, 0x80820308002010808203080020108082030800201080820308002010808203080020108082030800201224820308009112248203080091122480810408911224808104089110808081040820108080810408201),
    (((0, 1), (0, 2), (2, 3), (1, 3)), 9, 0x84820408002040248203080020102482030400201024820304002010248203040020102482030400201024820304009010210203040020102102030408201),
    (((0, 1), (0, 2), (3, 3), (1, 2)), 12, 0x80820308002010808203080020108082030800201080820308002010208203260020102082032600201024820326009130248203260091302481830408913024818304089130208183040820102081830408201),
    (((0, 1), (0, 3), (1, 2), (2, 3)), 9, 0x221020408102012208204060020122082010600201220820106002012208201060020122082010600201220820106002110808201060020108080810600201),
    (((0, 1), (0, 3), (1, 3), (2, 2)), 12, 0x80820308002010808203080020108082030800201080820308002012208203060090122082030600901220820106489112208201064891104080810648211040808106482110408083060020104080830600201),
    (((0, 1), (0, 3), (2, 3), (1, 2)), 9, 0x81020408102040208203060020102082030600201020820306002010208203060020102082030600201020820306002010208203060020102082030600201),
    (((0, 1), (1, 2), (2, 3), (0, 3)), 9, 0x81020408102040848203084020108482030840201004820304402010048203044020100488030440901004880304409010000203040820100002030408201),
    (((0, 1), (1, 2), (3, 3), (0, 2)), 12, 0x80820308a0201080820308c020108082030840201080820308a020100082032640201000820326a0201004820326a09130048203264091300481830408913004818304089130008183040820100081830408201),
    (((0, 1), (1, 3), (0, 2), (2, 3)), 9, 0x81020408102040808004061020108080040610201080800406102010808004061020108080040610201080800406102010808004061020108080040610201),
    (((0, 1), (1, 3), (0, 3), (2, 2)), 12, 0x80820408102040808204081020408082040810204080820408102040808003061090108080030610901080800306489010808003064890104080030648201040800306482010408003061020104080030610201),
    (((0, 1), (2, 2), (0, 3), (1, 3)), 12, 0x81020408102040810204081020408482040810904084820408109040248003040890102480030408901024800304089010248003040890102480030408901024800304089010210003040820102100030408201),
    (((0, 1), (2, 2), (1, 3), (0, 3)), 12, 0x8482030840201084820308402010048203044020100482030440201004820304e0911004820304a0911224808304089012248083040890122488010408911224880104089110000081040820100000810408201),
    (((0, 1), (2, 2), (3, 3), (0, 1)), 12, 0x848203084020102e82032640901004820304409010048803260891300c8803040890102001830408913020080326089010248183260890102008030408913024880304089130200183040820102001830408201),
    (((0, 1), (2, 3), (0, 1), (2, 3)), 9, 0x220800406109012208004061090122480010608901220800106089012208001040890122080010608901220800106089110808001060820108080810608201),
    (((0, 1), (2, 3), (0, 3), (1, 2)), 9, 0x80820406109040208003061090102080030608901020800306089010208003060890102480030608901020800306089010208003040820102080030608201),
    (((0, 1), (2, 3), (1, 2), (0, 3)), 9, 0x22102040700901221080406c090122488010608901220080106089012200801040890122008010608901220080106089110000201060820100000810608201),
    (((0, 1), (2, 3), (1, 3), (0, 2)), 12, 0x8082030860201080820309202010808203084020100082030640901000820306e091100088030608901224808306089012200803060891122088010408911220008106089110000081060820100080810608201),
    (((0, 1), (2, 3), (2, 3), (0, 1)), 9, 0x21080406109040248803064090102008030608901000080304089010200803060890102008030608901020080306089010200203060820102002030608201),
    (((0, 1), (3, 3), (0, 1), (2, 2)), 12, 0x808204061020408082040610904220801306102012208013064891152080010610981040808106489812208013060c9010408013060c90122080010648981220800106489910408001060c2010408081060c201),
    (((0, 1), (3, 3), (1, 2), (0, 2)), 12, 0x8082040610204080820406102010808204061020122082130640211520821b061020100080810640981220881306a02010008813060c981220080106409912200801060c9910000081060c2010000081060c201),
    (((0, 3), (0, 2), (1, 3), (1, 2)), 12, 0x80820308002410808203080022908082030800211080821308002110248083260092902480832600191020809304089030208083040090302480932608191024809326089110208083040018302080830408183),
    (((0, 3), (0, 3), (1, 1), (2, 2)), 12, 0x80822b0800211080823b08002112208093060091122080b306009112208081064819122080810648191040808106009110408081060091122080932648191220809326481910408081060018304080810600183),
    (((0, 3), (0, 3), (1, 2), (1, 2)), 9, 0x21021306102110208213060021102080930600191020809306001910208093060019102080930600191220809326001910208084060018402080810600183),
    (((0, 3), (1, 2), (1, 2), (0, 3)), 9, 0x81020408102042248813264091122488132640911000008104081830000081040818322488132640911224881326409110000081040818300000810408183),
    (((0, 3), (1, 2), (1, 3), (0, 2)), 12, 0x80820308c0229080820308e02390808203084021108082030840231004809326a091100480932640911000808304081830008083040818300480932640911004809326409110008083040818300080830408183),
    (((0, 3), (2, 2), (1, 1), (0, 3)), 12, 0x2248c3b2640911224a813a64091100480810408903000008104081912249813040891122480ab5640911224808104081910048081040819122480810440911224809304409110000081040818300000810408183),
    (((0, 3), (2, 2), (1, 3), (0, 1)), 12, 0x24880326409110248803264091100000830408903000008304089032248803260891102488032608911020008104089030200083040890302488132608911224881326089110200083040818302000810408183),
    (((1, 1), (0, 0), (3, 3), (2, 2)), 16, 0x8082030800201080820308002010808203080020108082030800201080820308002010808203080020108082030800201080820308002010808203080020108082030800201080820308002010808203080020108082030800201080820308002010808203080020108082030800201),
    (((1, 1), (0, 2), (3, 3), (0, 2)), 16, 0x8082030800201080820308002010808203080020108082030800201080820308002010808203080020108082030800201080820308002010848203084020108482030840201004820304402010048203044020100488030440901004880304409010000203040820100002030408201),
    (((1, 1), (0, 3), (0, 3), (2, 2)), 12, 0x80820308002010808203080020108082030800201080820308002012208003060090122080030600901220801106489012208011064890104080110648081040801106480810408003060008104080030600081),
    (((1, 1), (2, 2), (3, 3), (0, 0)), 16, 0x8482030840201084820308402010048203044020100482030440201004820304402010048203044020100482030440201004820304402010048203044020100482030440201004820304402010048203044020100488030440901004880304409010000203040820100002030408201),
    (((1, 1), (2, 3), (0, 3), (0, 2)), 12, 0x80820308402010808203090020100080030640901220800306a09010048003060890122080110608901224880304095012208811060808100000110440901000001106400810008003060808100080030608081),
    (((1, 1), (3, 3), (0, 0), (2, 2)), 12, 0x220801306409012208013064090120080110648981200801106489810408000060c0810408000060c081220801306409012208013064090120080110648981200801106489810408000060c0810408000060c081),
    (((1, 2), (0, 3), (0, 3), (1, 2)), 9, 0x81020408102040208003060010102080030600101020800306001010208003060010102080030600101020800306001010208003060010102080030600101),
    (((1, 2), (0, 3), (1, 3), (0, 2)), 12, 0x80820308002010808203080020108082030800211080820308402012208083060010100088030640111220880106001010000083060010122008010640111220880306401110000081060010100000810600101),
    (((1, 2), (2, 3), (1, 3), (0, 0)), 12, 0x224880306401112248803064010100000810440101000080104401010048803064090100008030640911000080304081010000083060810122008030640911224880306409110000081060810100000810408101),
    (((1, 3), (0, 2), (1, 3), (0, 2)), 16, 0x8082030800201080820308002010808203080020108082030800201080820308002010808203080020108482130840211080821308402110048093044019100480932640191004809304401910048083040018300480930440191224881304409110008083040018100000810408181),
    (((1, 3), (2, 2), (1, 3), (0, 0)), 16, 0x8482030840201084820308402010048203044020100482030440201004821304402110048213044021100480830440191004809304401810048093044091100488130440191004808304081810000083044018122488130440911004881326409110000081040818100000830408183),
    (((1, 3), (2, 3), (0, 1), (0, 2)), 12, 0x220801306409012208813064090100480012608191000000106081812248093044090322080130640901000880104081810008001060819122000132640901220809306409010008001060818300080010608181),
    (((3, 3), (2, 2), (1, 1), (0, 0)), 16, 0x22488132640911224881326409110000081040818300000810408183224881326409112248813264091100000810408183000008104081832248813264091122488132640911000008104081830000081040818322488132640911224881326409110000081040818300000810408183),
)


def route_tables():
    pairs = [(a, b) for b in range(4) for a in range(b + 1)]
    pair_at = {pair: i for i, pair in enumerate(pairs)}
    row_of = np.zeros((79 * 128,), np.int32)
    rows = []
    seen = set()
    for goals, steps, code in ROUTES:
        for flip in range(8):
            names = []
            for chip in range(4):
                y, x = chip // 2 ^ (flip & 1), chip % 2 ^ (flip >> 1 & 1)
                names.append(x * 2 + y if flip & 4 else y * 2 + x)
            moved = [None] * 4
            for chip in range(4):
                moved[names[chip]] = tuple(sorted(names[g] for g in goals[chip]))
            key = sum(pair_at[moved[chip]] * 10**chip for chip in range(4))
            if key in seen:
                continue
            seen.add(key)
            row_of[key] = len(rows)
            rows.append(plan_of(moved, steps, code, names, flip >> 2))
    return row_of.reshape(79, 1, 128), np.stack(rows).reshape(-1, 1, 128)


def plan_of(goals, steps, code, names, swapped):
    back = [names.index(chip) for chip in range(4)]
    own = [{} for _ in range(4)]
    passing = [{} for _ in range(4)]
    for chip in range(4):
        for which in range(2):
            if goals[chip][which] != chip:
                pool = own[chip].setdefault(goals[chip][which], [])
                pool += [(piece, which) for piece in range(PIECES)]
                pool.sort()
    plan = np.full((4, 128), 3, np.int32)
    plan[:, 2 * PLAN_STEPS] = sum(steps > total for total in TOTALS)
    free = [[(0, slot) for slot in range(ROOM)] for _ in range(4)]
    for step in range(steps):
        landed = []
        for chip in range(4):
            for link in range(2):
                at = (step * 4 + back[chip]) * 2 + (link ^ swapped)
                goal, since = code >> 7 * at & 7, code >> 7 * at + 3 & 15
                if goal == 4:
                    continue
                goal = names[goal]
                if since == 0:
                    piece, which = own[chip][goal].pop(-link)
                    source, sent = chip, which | piece << 2
                else:
                    which, piece, source, slot = passing[chip].pop((step - since, 1 - link))
                    sent = 2 | slot << 2
                    free[chip].append((max(step, step - since + LAG), slot))
                plan[chip, 2 * step + link] += sent - 3
                landed.append((chip ^ 1 << link, link, source, which, piece, goal))
        for chip, link, source, which, piece, goal in landed:
            got = (source * 2 + which) << 9 | piece << 12
            if goal == chip:
                got |= 1 << 7
            else:
                at = next(i for i, item in enumerate(free[chip]) if item[0] <= step)
                slot = free[chip].pop(at)[1]
                got |= 2 << 7 | slot << 16
                passing[chip][step, link] = (which, piece, source, slot)
            plan[chip, 2 * step + link] |= got
    assert not any(passing) and not any(pool for chip in own for pool in chip.values())
    return plan


def copy_all(moves, sems, base, phase):
    for number, (condition, source, target) in enumerate(moves):

        def act(number=number, source=source, target=target):
            copy = pltpu.make_async_copy(source, target, sems.at[base + number])
            if phase == 0:
                copy.start()
            else:
                copy.wait()

        if condition is True:
            act()
        else:
            pl.when(condition)(act)


def piece_rows(ref, row, rows):
    return ref.at[pl.ds(pl.multiple_of(row, 16), rows)]


def link_of(step, core):
    return 1 - core if step // 2 % 2 else core


def early_kernel(weights, *refs):
    *early, semaphores = refs
    rows = weights.shape[0] // PIECES
    core = lax.axis_index("req") % 2
    copies = []
    for number in range(EARLY):
        piece = jnp.where(core == 1, number, PIECES - 1 - number)
        part = piece_rows(weights, piece * rows, rows)
        copies.append(pltpu.make_async_copy(part, early[number], semaphores.at[number]))
        copies[-1].start()
    for copy in copies:
        copy.wait()


def plan_kernel(old_place, new_place, row_of, plans, meta, row_part, plan_part, sem):
    me_index = lax.axis_index("req")
    core = me_index % 2
    chip = me_index // 2
    goals = []
    for holder in range(8):
        goal = jnp.int32(0)
        for device in range(8):
            goal = jnp.where(new_place[device] == old_place[holder], device, goal)
        goals.append(goal)
    key = jnp.int32(0)
    my_swap = jnp.int32(0)
    for at in range(4):
        first, second = goals[2 * at], goals[2 * at + 1]
        low, high = jnp.minimum(first, second), jnp.maximum(first, second)
        high_chip = high // 2
        key = key + (high_chip * (high_chip + 1) // 2 + low // 2) * 10**at
        my_swap = jnp.where((first > second) & (chip == at), 1, my_swap)
        meta[GOAL_AT + 2 * at] = low % 2
        meta[GOAL_AT + 2 * at + 1] = high % 2
    meta[CORE_AT] = core
    meta[SWAP_AT] = my_swap
    wanted = new_place[me_index]
    beside = jnp.where(wanted == old_place[me_index + 1 - 2 * core], 2, 0)
    meta[LOCAL_AT] = jnp.where(wanted == old_place[me_index], 1, beside)
    copy = pltpu.make_async_copy(row_of.at[key // 128], row_part, sem)
    copy.start()
    copy.wait()
    row = row_part[0, key % 128]
    copy = pltpu.make_async_copy(plans.at[row * 4 + chip], plan_part, sem)
    copy.start()
    copy.wait()
    for at in range(2 * PLAN_STEPS):
        meta[at] = plan_part[0, at]
    meta[TOTAL_AT] = plan_part[0, 2 * PLAN_STEPS]


def step_kernel(rows, step, come, local_pieces, names, count, meta, *refs):
    refs = list(zip(names, refs))
    semaphores = refs.pop()[1]
    given = {}
    for number, (name, ref) in enumerate(refs):
        if number >= count or name not in ("out", "room"):
            given.setdefault(name, []).append(ref)
    w_hbm = given["weights"][0]
    out_hbm = given.get("out", [None])[0]
    room = given.get("room", [None])[0]
    core = meta[CORE_AT]
    local = meta[LOCAL_AT]
    used = 0
    stores, moves = [], []
    swap = given.get("swap", [None])[0]
    brought = [("landed", core, step_at) for step_at in come[0]]
    brought += [("swapped", 1 - core, step_at) for step_at in come[1]]
    for name, side, step_at in brought:
        word = meta[2 * step_at + link_of(step_at, side)]
        kind = (word >> 7) & 3
        row = ((word >> 12) & 15) * rows
        source = given[name].pop(0).at[pl.ds(0, rows)]
        if room is not None:
            slot = (word >> 16) & 31
            stores.append((kind == 2, source, piece_rows(room, slot * rows, rows)))
        final = (kind == 1) & (meta[GOAL_AT + ((word >> 9) & 7)] == core)
        moves.append((final, source, piece_rows(out_hbm, row, rows)))
        if name == "landed" and swap is not None:
            moves.append((jnp.logical_not(final), source, swap))
    copy_all(stores, semaphores, used, 0)
    copy_all(stores, semaphores, used, 1)
    used += len(stores)
    riding = []
    if "sent" in given:
        target = given["sent"][0].at[pl.ds(0, rows)]
        if "extra" in given:
            riding.append((True, given["extra"][0], given["sent"][0].at[pl.ds(rows, RIDE)]))
        word = meta[2 * step + link_of(step, core)]
        kind = word & 3
        piece = (word >> 2) & 31
        held = kind == 2
        mine = ((kind ^ meta[SWAP_AT]) == core) | (kind == 3)
        theirs = jnp.logical_not(held | mine)
        options = [(jnp.logical_not(held) & mine, piece_rows(w_hbm, piece * rows, rows))]
        if "other" in given:
            options.append((theirs, piece_rows(given["other"][0], piece * rows, rows)))
        place = jnp.where(core == 0, piece, PIECES - 1 - piece)
        for number, ref in enumerate(given.get("early", ())):
            options.append((theirs & (place == number), ref))
        if room is not None:
            options.append((held, piece_rows(room, piece * rows, rows)))
        for condition, source in options:

            @pl.when(condition)
            def _(source=source):
                pltpu.make_async_copy(source, target, semaphores.at[used]).start()

        fetched = pltpu.make_async_copy(w_hbm.at[pl.ds(0, rows)], target, semaphores.at[used])
        used += 1
    copy_all(riding, semaphores, used, 0)
    first_ride = used
    used += len(riding)
    copy_all(moves, semaphores, used, 0)
    first_move = used
    used += len(moves)
    reads, writes = [], []
    for number, piece in enumerate(local_pieces):
        part = given["staged"][0].at[number]
        row = piece * rows
        reads.append((local == 1, piece_rows(w_hbm, row, rows), part))
        reads.append((local == 2, piece_rows(given["other"][0], row, rows), part))
        writes.append((local != 0, part, piece_rows(out_hbm, row, rows)))
    copy_all(reads, semaphores, used, 0)
    if "sent" in given:
        fetched.wait()
    copy_all(riding, semaphores, first_ride, 1)
    copy_all(reads, semaphores, used, 1)
    used += len(reads)
    copy_all(writes, semaphores, used, 0)
    copy_all(moves, semaphores, first_move, 1)
    copy_all(writes, semaphores, used, 1)


def between_cores(array):
    return lax.ppermute(array, "req", [(i, i ^ 1) for i in range(8)])


def along_links(array, step):
    return lax.ppermute(array, "req", [(i, i ^ (2 << link_of(step, i % 2))) for i in range(8)])


def plan_plane(old_place, new_place):
    row_of, plans = route_tables()
    smem = pl.BlockSpec(memory_space=pltpu.SMEM)
    anywhere = pl.BlockSpec(memory_space=pl.ANY)
    return pl.pallas_call(
        plan_kernel,
        out_shape=jax.ShapeDtypeStruct((META,), jnp.int32),
        in_specs=[smem, smem, anywhere, anywhere],
        out_specs=smem,
        scratch_shapes=[
            pltpu.SMEM((1, 128), jnp.int32),
            pltpu.SMEM((1, 128), jnp.int32),
            pltpu.SemaphoreType.DMA,
        ],
        name="plan_steps",
    )(old_place, new_place, jnp.asarray(row_of), jnp.asarray(plans))


def early_pieces(weights):
    width, columns = weights.shape
    return pl.pallas_call(
        early_kernel,
        out_shape=[jax.ShapeDtypeStruct((width // PIECES, columns), weights.dtype)] * EARLY,
        in_specs=[pl.BlockSpec(memory_space=pl.ANY)],
        out_specs=[pl.BlockSpec(memory_space=pltpu.VMEM)] * EARLY,
        scratch_shapes=[pltpu.SemaphoreType.DMA((EARLY,))],
        compiler_params=pltpu.CompilerParams(vmem_limit_bytes=32 << 20),
        name="early_pieces",
    )(weights)


def migrate_plane(weights, meta, early, total, beside):
    width, columns = weights.shape
    rows = width // PIECES
    smem = pl.BlockSpec(memory_space=pltpu.SMEM)
    anywhere = pl.BlockSpec(memory_space=pl.ANY)
    near = pl.BlockSpec(memory_space=pltpu.VMEM)
    whole = jax.ShapeDtypeStruct((width, columns), weights.dtype)
    room_like = jax.ShapeDtypeStruct((ROOM * rows, columns), weights.dtype)
    held = {"out": None, "room": None}

    def run(meta, step, come, sources, local_pieces, extra, store, swap):
        operands, specs, names, aliases = [meta, weights], [smem, anywhere], ["weights"], {}

        def add(name, array, spec):
            if array is not None:
                operands.append(array)
                specs.append(spec)
                names.append(name)

        for name, array in sources:
            add(name, array, anywhere)
        for step_at in come[0]:
            add("landed", landed[step_at], near)
        for step_at in come[1]:
            add("swapped", swapped[step_at], near)
        add("extra", extra, near)
        results = []
        if step is not None:
            sent_rows = rows + (RIDE if step < RIDES else 0)
            results.append(("sent", jax.ShapeDtypeStruct((sent_rows, columns), weights.dtype), near))
        if swap:
            like = jax.ShapeDtypeStruct((rows, columns), weights.dtype)
            results.append(("swap", like, near))
        for name, like, wanted in (
            ("out", whole, bool(local_pieces or come[0] or come[1])),
            ("room", room_like, store),
        ):
            if wanted:
                if held[name] is not None:
                    aliases[len(operands)] = len(results)
                    add(name, held[name], anywhere)
                results.append((name, like, anywhere))
        count = len(names)
        names += [name for name, _, _ in results]
        scratch = []
        if local_pieces:
            scratch.append(pltpu.VMEM((len(local_pieces), rows, columns), weights.dtype))
            names.append("staged")
        scratch.append(pltpu.SemaphoreType.DMA((24,)))
        names.append("semaphores")
        values = pl.pallas_call(
            functools.partial(
                step_kernel, rows, step, come, local_pieces, names, count
            ),
            out_shape=[like for _, like, _ in results],
            in_specs=specs,
            out_specs=[spec for _, _, spec in results],
            scratch_shapes=scratch,
            input_output_aliases=aliases,
            compiler_params=pltpu.CompilerParams(vmem_limit_bytes=32 << 20),
            cost_estimate=pl.CostEstimate(
                flops=0, bytes_accessed=4 * rows * columns * 2, transcendentals=0
            ),
            name="place_pieces" if step is None else "step_pieces",
        )(*operands)
        for (name, _, _), value in zip(results, values):
            if name in held:
                held[name] = value
        return values

    landed, swapped = {}, {}
    ridden = None
    for step in range(total):
        meta, extra = beside(step, meta, ridden)
        come = [step - 2] if step >= 2 else [], [step - LAG] if step >= LAG else []
        sources = [("early", piece) for piece in early[: step + 1]]
        if step >= EARLY:
            sources = [("other", other)]
        local_pieces = LOCAL_PIECES.get(step, ())
        some = step >= 2
        values = run(meta, step, come, sources, local_pieces, extra, some, some)
        meta, source, _ = lax.optimization_barrier((meta, weights, values[0]))
        if step == EARLY - 1:
            other = between_cores(source)
        landed[step] = along_links(values[0], step)
        if extra is not None:
            ridden = landed[step][rows:]
        if some:
            swapped[step - 2] = between_cores(values[1])
    last = total - 1
    meta, _ = beside(total, meta, ridden)
    come = [last - 1], list(range(total - LAG, last - 2))
    values = run(meta, None, come, (), (), None, False, True)
    swapped[last - 1] = between_cores(values[0])
    swapped[last] = between_cores(landed[last])
    run(meta, None, ([last], [last - 2, last - 1]), (), (), None, False, False)
    run(meta, None, ([], [last]), (), (), None, False, False)
    return held["out"]


def plane_dispatch(hidden, chosen, weights_now, place, gain):
    batches, tok_rows, width = hidden.shape
    topk = chosen.shape[-1]
    tokens = batches * tok_rows
    nreq = lax.axis_size("req")
    me_index = lax.axis_index("req")
    resid = hidden.reshape(tokens, width).astype(jnp.float32)
    normed = (
        resid * gain / jnp.sqrt(jnp.mean(resid * resid, axis=-1, keepdims=True) + 1e-05)
    ).astype(jnp.bfloat16)
    flat_ids = chosen.reshape(-1)
    devices = jnp.arange(nreq, dtype=jnp.int32)
    holder = jnp.sum(jnp.where(flat_ids[:, None] == place[None, :], devices[None, :], 0), axis=1)
    assign_index = jnp.arange(flat_ids.shape[0], dtype=jnp.int32)
    batch_of = assign_index // (tok_rows * topk)
    earlier = (
        (flat_ids[:, None] == flat_ids[None, :])
        & (batch_of[:, None] == batch_of[None, :])
        & (assign_index[None, :] < assign_index[:, None])
    )
    rank_in = jnp.sum(earlier.astype(jnp.int32), axis=1)
    slot = (holder ^ me_index) * SLOTS + batch_of * CAP + rank_in
    hit = slot[:, None] == jnp.arange(nreq * SLOTS, dtype=jnp.int32)[None, :]
    hit = hit.reshape(tokens, topk, nreq * SLOTS)
    coef = jnp.sum(jnp.where(hit, weights_now.reshape(tokens, topk, 1), 0.0), axis=1)
    blocks = jnp.any(hit, axis=1).T
    order = [k for k in range(nreq) if k & 1] + [k for k in range(nreq) if not k & 1]
    blocks = blocks.reshape(nreq, SLOTS, tokens)[jnp.array(order)].reshape(nreq * SLOTS, tokens)
    outgoing = jnp.dot(
        blocks.astype(jnp.bfloat16), normed, preferred_element_type=jnp.float32
    ).astype(jnp.bfloat16)
    half = nreq * SLOTS // 2
    came = between_cores(outgoing[:half])
    return jnp.concatenate([came, outgoing[half:]]), coef


def reordered(rows, orders):
    core = lax.axis_index("req") % 2
    spread = [np.eye(rows.shape[0], dtype=np.float32)[np.array(order)] for order in orders]
    chosen = jnp.where(core == 0, spread[0], spread[1]).astype(rows.dtype)
    return jnp.dot(chosen, rows, preferred_element_type=jnp.float32).astype(rows.dtype)


def exchange(rows, labels, bits):
    orders = []
    for core in range(2):
        going = [i for i, label in enumerate(labels[core]) if label // SLOTS >> bits[core] & 1]
        orders.append(going + [i for i in range(len(labels[core])) if i not in going])
    rows = reordered(rows, orders)
    half = rows.shape[0] // 2
    came = yield bits[0] > 0, rows[:half]
    labels = [[labels[core][i] for i in orders[core]] for core in range(2)]
    if bits[0] == 0:
        labels = [labels[1 - core][:half] + labels[core][half:] for core in range(2)]
    return jnp.concatenate([came, rows[half:]]), labels


def plane_work(attention, hidden, rows, coef, shard_weights):
    batches, tok_rows, width = hidden.shape
    tokens = batches * tok_rows
    ntp = lax.axis_size("tp")
    hid_dev = shard_weights.shape[1] // 3
    every = range(rows.shape[0])
    first = [i for i in every if i // SLOTS & 1] + [i for i in every if not i // SLOTS & 1]
    labels = [first, first]
    rows, labels = yield from exchange(rows, labels, (1, 2))
    rows, labels = yield from exchange(rows, labels, (2, 1))
    gate_up = jnp.dot(rows, shard_weights[:, : 2 * hid_dev], preferred_element_type=jnp.float32)
    act = (jax.nn.silu(gate_up[:, :hid_dev]) * gate_up[:, hid_dev:]).astype(jnp.bfloat16)
    part = lax.dot_general(
        act,
        shard_weights[:, 2 * hid_dev :],
        (((1,), (1,)), ((), ())),
        preferred_element_type=jnp.float32,
    )
    rows = part.astype(jnp.bfloat16)
    context = yield False, attend(*attention)
    swap = exchange(rows, labels, (0, 0))
    _, going = next(swap)
    try:
        swap.send(between_cores(going))
    except StopIteration as end:
        rows, labels = end.value
    rows, labels = yield from exchange(rows, labels, (1, 2))
    rows, labels = yield from exchange(rows, labels, (2, 1))
    rows = reordered(rows, [[label.index(i) for i in every] for label in labels])
    partial_sum = jnp.dot(
        coef,
        rows.astype(jnp.float32),
        precision=lax.Precision.HIGHEST,
        preferred_element_type=jnp.float32,
    )
    tp_index = lax.axis_index("tp")
    tp_width = width // ntp

    def share_of(index):
        start = lax.rem(index, ntp) * tp_width
        return lax.dynamic_slice_in_dim(partial_sum, start, tp_width, 1)

    total = share_of(tp_index)
    for ahead in range(1, ntp):
        pairs = [(i, (i + ahead) % ntp) for i in range(ntp)]
        share = share_of(tp_index + ahead).astype(jnp.bfloat16)
        total = total + lax.ppermute(share, "tp", pairs).astype(jnp.float32)
    total = yield False, total
    resid = hidden.reshape(tokens, width).astype(jnp.float32)
    resid_share = lax.dynamic_slice_in_dim(resid, tp_index * tp_width, tp_width, 1)
    summed = (resid_share + total).astype(jnp.bfloat16)
    return context, summed.reshape(batches, tok_rows, tp_width)


def attend(queries, new_keys, new_values, cache_keys, cache_values, lengths):
    batches, tok_rows, width = queries.shape
    heads = width // HEAD_SIZE
    pool = cache_keys.shape[0]
    scale = HEAD_SIZE ** (-0.5)
    req_lengths = lengths.reshape(-1)
    starts = jnp.cumsum(req_lengths) - req_lengths
    position = jnp.arange(pool, dtype=jnp.int32)
    owned = (position[None, :] >= starts[:, None]) & (
        position[None, :] < (starts + req_lengths)[:, None]
    )
    query_rows = queries.reshape(batches * tok_rows, heads, HEAD_SIZE)
    own_keys = new_keys.reshape(batches * tok_rows, heads, HEAD_SIZE)
    own_values = new_values.reshape(batches * tok_rows, heads, HEAD_SIZE)
    pool_keys = cache_keys.reshape(pool, heads, HEAD_SIZE)
    pool_values = cache_values.reshape(pool, heads, HEAD_SIZE)
    scores = (
        jnp.einsum("qhd,phd->hqp", query_rows, pool_keys, preferred_element_type=jnp.float32)
        * scale
    )
    scores = jnp.where(owned[None], scores, -jnp.inf)
    own_score = (
        jnp.einsum("qhd,qhd->hq", query_rows, own_keys, preferred_element_type=jnp.float32) * scale
    )
    highest = jnp.maximum(jnp.max(scores, axis=-1), own_score)
    exp_pool = jnp.exp(scores - highest[..., None])
    exp_own = jnp.exp(own_score - highest)
    denom = jnp.sum(exp_pool, axis=-1) + exp_own
    summed = jnp.einsum(
        "hqp,phd->qhd",
        exp_pool.astype(jnp.bfloat16),
        pool_values,
        preferred_element_type=jnp.float32,
    )
    prob_own = lax.optimization_barrier(exp_own.astype(jnp.bfloat16)).astype(jnp.float32)
    summed = summed + prob_own.T[:, :, None] * own_values.astype(jnp.float32)
    context = (summed / denom.T[:, :, None]).astype(jnp.bfloat16)
    return context.reshape(batches, tok_rows, width)


def choose_holders(place, me_index, nreq, shard_count):
    devices = jnp.arange(nreq, dtype=jnp.int32)
    holder = place[None, :] == jnp.arange(shard_count, dtype=jnp.int32)[:, None]
    before = (place[:, None] == place[None, :]) & (devices[:, None] < devices[None, :])
    rank_in = jnp.sum(before.astype(jnp.int32), axis=0)
    count = jnp.sum(holder.astype(jnp.int32), axis=1)
    wanted = me_index % count
    match = holder & (rank_in[None, :] == wanted[:, None])
    return jnp.sum(jnp.where(match, devices[None, :], 0), axis=1)


def expert_block(hidden, chosen, weights_now, place, shard_weights, gain):
    nreq = lax.axis_size("req")
    me_index = lax.axis_index("req")
    split_count = max(1, nreq // 16)
    shard_count = EXPERTS * split_count
    batches, tok_rows, width = hidden.shape
    topk = chosen.shape[-1]
    tokens = batches * tok_rows
    hid_dev = shard_weights.shape[1] // 3
    resid = hidden.reshape(tokens, width).astype(jnp.float32)
    normed = (
        resid * gain / jnp.sqrt(jnp.mean(resid * resid, axis=-1, keepdims=True) + 1e-05)
    ).astype(jnp.bfloat16)
    flat_ids = chosen.reshape(-1)
    assigns = flat_ids.shape[0]
    slots_dev = batches * CAP
    shard_dest = choose_holders(place, me_index, nreq, shard_count)
    shard_list = flat_ids[:, None] * split_count + jnp.arange(split_count, dtype=jnp.int32)[None, :]
    pick = shard_list[:, :, None] == jnp.arange(shard_count, dtype=jnp.int32)[None, None, :]
    dest = jnp.sum(jnp.where(pick, shard_dest[None, None, :], 0), axis=-1)
    assign_index = jnp.arange(assigns, dtype=jnp.int32)
    batch_of = assign_index // (tok_rows * topk)
    earlier = (
        (flat_ids[:, None] == flat_ids[None, :])
        & (batch_of[:, None] == batch_of[None, :])
        & (assign_index[None, :] < assign_index[:, None])
    )
    rank_in = jnp.sum(earlier.astype(jnp.int32), axis=1)
    slot = dest * slots_dev + (batch_of * CAP + rank_in)[:, None]
    slot_hit = slot[:, :, None] == jnp.arange(nreq * slots_dev, dtype=jnp.int32)[None, None, :]
    by_token = jnp.any(slot_hit.reshape(tokens, topk * split_count, nreq * slots_dev), axis=1)
    outgoing = jnp.dot(
        by_token.T.astype(jnp.bfloat16), normed, preferred_element_type=jnp.float32
    )
    outgoing = outgoing.astype(jnp.bfloat16).reshape(nreq, slots_dev, width)
    received = lax.all_to_all(outgoing, "req", split_axis=0, concat_axis=0, tiled=True)
    flat_rows = received.reshape(nreq * slots_dev, width)
    gate_up = jnp.dot(
        flat_rows, shard_weights[:, : 2 * hid_dev], preferred_element_type=jnp.float32
    )
    act = (jax.nn.silu(gate_up[:, :hid_dev]) * gate_up[:, hid_dev:]).astype(jnp.bfloat16)
    part = lax.dot_general(
        act,
        shard_weights[:, 2 * hid_dev :],
        (((1,), (1,)), ((), ())),
        preferred_element_type=jnp.float32,
    )
    part = part.astype(jnp.bfloat16).reshape(nreq, slots_dev, width)
    returned = lax.all_to_all(part, "req", split_axis=0, concat_axis=0, tiled=True)
    returned = returned.reshape(nreq * slots_dev, width)
    coef = jnp.sum(
        jnp.where(
            slot_hit.reshape(tokens, topk, split_count, nreq * slots_dev),
            weights_now.reshape(tokens, topk)[:, :, None, None],
            0.0,
        ),
        axis=(1, 2),
    )
    partial_sum = jnp.dot(
        coef,
        returned.astype(jnp.float32),
        precision=lax.Precision.HIGHEST,
        preferred_element_type=jnp.float32,
    )
    tp_width = width // lax.axis_size("tp")
    tp_start = lax.axis_index("tp") * tp_width
    resid_share = lax.dynamic_slice_in_dim(resid, tp_start, tp_width, 1)
    share = lax.psum_scatter(
        partial_sum.astype(jnp.bfloat16), "tp", scatter_dimension=1, tiled=True
    ).astype(jnp.float32)
    summed = (resid_share + share).astype(jnp.bfloat16)
    return summed.reshape(batches, tok_rows, tp_width)


def migrate(old_weights, old_place, new_place):
    nreq = lax.axis_size("req")
    shard_count = EXPERTS * max(1, nreq // 16)
    _, width, columns = old_weights.shape
    piece = width // nreq
    pieces = old_weights.reshape(nreq, piece, columns)
    spread = lax.all_to_all(pieces, "req", split_axis=0, concat_axis=0, tiled=True)
    devices = jnp.arange(nreq, dtype=jnp.int32)
    shard_ids = jnp.arange(shard_count, dtype=jnp.int32)
    first_old = jnp.min(
        jnp.where(old_place[None, :] == shard_ids[:, None], devices[None, :], nreq), axis=1
    )
    needed = jnp.sum(
        jnp.where(new_place[:, None] == shard_ids[None, :], first_old[None, :], 0), axis=1
    )
    sending = spread[needed]
    collected = lax.all_to_all(sending, "req", split_axis=0, concat_axis=0, tiled=True)
    return collected.reshape(1, width, columns)


def plane_outputs(attention, layer, new_place):
    hidden, expert_ids, route_weights, old_place, weights, gain = layer
    early = early_pieces(weights)
    first = between_cores(early[0])
    hidden, _ = lax.optimization_barrier((hidden, early[0]))
    meta = plan_plane(old_place, new_place)
    received, coef = plane_dispatch(hidden, expert_ids, route_weights, old_place, gain)

    def within(total):
        def outputs(weights, meta, first, second, attention, hidden, rows, coef):
            work = plane_work(attention, hidden, rows, coef, weights)
            stage = next(work)
            done = None
            pending = []

            def beside(step, meta, ridden):
                nonlocal stage, done
                for _ in range(2 if step == min(total, 11) else STAGES.get(step, 0)):
                    rides, value = stage
                    if pending:
                        pending.pop()
                        half = value.shape
                        value = ridden.reshape(half)
                    elif rides:
                        pending.append(True)
                        return meta, value.reshape(RIDE, weights.shape[1])
                    else:
                        meta, value = lax.optimization_barrier((meta, value))
                    try:
                        stage = work.send(value)
                    except StopIteration as end:
                        done = end.value
                return meta, None

            moved = migrate_plane(
                weights, meta, [first, between_cores(second)], total, beside
            )
            return (*done, moved[None])

        return outputs

    branches = [within(total) for total in TOTALS]
    return lax.switch(meta[TOTAL_AT], branches, weights, meta, first, early[1], attention, hidden, received, coef)


def on_device(
    queries,
    new_keys,
    new_values,
    cache_keys,
    cache_values,
    lengths,
    hidden,
    gain,
    expert_ids,
    route_weights,
    old_place,
    new_place,
    old_weights,
):
    attention = (queries, new_keys, new_values, cache_keys, cache_values, lengths)
    layer = (hidden, expert_ids, route_weights, old_place, old_weights[0], gain)
    if lax.axis_size("req") == 8:
        return plane_outputs(attention, layer, new_place)
    context = attend(*attention)
    moved = migrate(old_weights, old_place, new_place)
    layer_out = expert_block(*layer)
    return (context, layer_out, moved)


def solution(mesh):
    in_specs = (
        P(None, "req", "tp"),
        P(None, "req", "tp"),
        P(None, "req", "tp"),
        P("req", "tp"),
        P("req", "tp"),
        P("req", None),
        P(None, "req", None),
        P(),
        P(None, "req", None),
        P(None, "req", None),
        P(),
        P(),
        P("req", None, "tp"),
    )
    out_specs = (P(None, "req", "tp"), P(None, "req", "tp"), P("req", None, "tp"))
    return jax.shard_map(
        on_device, mesh=mesh, in_specs=in_specs, out_specs=out_specs, check_vma=False
    )
```

```python
import functools

import jax
import jax.numpy as jnp
import numpy as np
from jax import lax
from jax.experimental import pallas as pl
from jax.experimental.pallas import tpu as pltpu
from jax.sharding import PartitionSpec as P

HEAD_SIZE = 64
EXPERTS = 8
CAP = 3
PIECES = 8
TOTALS = (9, 12, 16)
EARLY = 2
LAG = 5
ROOM = 16
SLOTS = 6
RIDE = 16
RIDES = 7
STAGES = {0: 1, 2: 3, 4: 2, 6: 2, 9: 2}
LOCAL_PIECES = {4: (0, 1), 5: (2, 3), 6: (4, 5), 7: (6, 7)}
PLAN_STEPS = max(TOTALS)
CORE_AT = 2 * PLAN_STEPS
SWAP_AT = CORE_AT + 1
LOCAL_AT = CORE_AT + 2
GOAL_AT = CORE_AT + 3
TOTAL_AT = CORE_AT + 11
META = CORE_AT + 12

ROUTES = (
    (((0, 0), (1, 1), (2, 2), (3, 3)), 9, 0x81020408102040810204081020408102040810204081020408102040810204081020408102040810204081020408102040810204081020408102040810204),
    (((0, 0), (1, 1), (2, 3), (2, 3)), 9, 0x81020408102040808203081020408082030810204080820308102040808203081020408082030810204080820308102040808203081020408082030810204),
    (((0, 0), (1, 1), (3, 3), (2, 2)), 12, 0x80820308102040808203081020408082030810204080820308102040808203261090408082032610904080820326489130808203264891304081830848213040818308482130408183081020404081830810204),
    (((0, 0), (1, 2), (1, 2), (3, 3)), 9, 0x81020408102040810204081020408102040810204224820408109112248204081091122480810408911224808104089110810081040820408100810408204),
    (((0, 0), (1, 2), (1, 3), (2, 3)), 9, 0x80820308109110808203081091108080830808911080808308089110808083080891108080830808911224808308089110808083080820408080810408204),
    (((0, 0), (1, 2), (2, 3), (1, 3)), 9, 0x81020408102040210203081020402102030810204024820308109040248203081090402482030408904024820304089040210203040820402102030408204),
    (((0, 0), (1, 2), (3, 3), (1, 2)), 12, 0x81020308102040810203081020408082030810204080820308102040208203261090402082032610904020820326089130208203260891302481830808913024818308089130208183040820402081830408204),
    (((0, 0), (1, 3), (1, 3), (2, 2)), 12, 0x80820408102040808204081020408082040810204080820308102110808203061091108080830610911080808306489112208083064891104080830648211040808106482110408083061020404080830610204),
    (((0, 0), (1, 3), (2, 3), (1, 2)), 9, 0x81020408102040208203061020402082030610204020820306102040208203061020402082030610204020820306102040208203061020402082030610204),
    (((0, 0), (2, 2), (1, 1), (3, 3)), 12, 0x81020408102040810204081020422482040810911224820408109112248081040891122480810408911224808104089112248081040891122480810408911224808104089110810081040820408100810408204),
    (((0, 0), (2, 2), (1, 3), (1, 3)), 12, 0x81020408102040810204081020408482040810911084820408109110248083040891102480830408911024808304089110248083040891102480830408911024808304089110210083040820402100830408204),
    (((0, 0), (2, 2), (3, 3), (1, 1)), 12, 0x210203081090402102030810911024820326089040248883260891102a8203040891302048830408913024818326089110204183260891102488830408913024888304089130204183040820402041830408204),
    (((0, 0), (2, 3), (1, 3), (1, 2)), 9, 0x20820306109110248203061091102080830608911020808304089110208083060891122080830608911020808306089110208081060820402080830608204),
    (((0, 1), (0, 1), (2, 3), (2, 3)), 9, 0x81020408102040808203080020108082030800201080820308002010808203080020108082030800201080820308002010808203080020108082030800201),
    (((0, 1), (0, 1), (3, 3), (2, 2)), 12, 0x80820308002010808203080020108082030800201080820308002010808203260090108082032600901080820326489130808203264891304081830848213040818308482130408183080020104081830800201),
    (((0, 1), (0, 2), (1, 3), (2, 3)), 12, 0x80820308002010808203080020108082030800201080820308002010808203080020108082030800201224820308009112248203080091122480810408911224808104089110808081040820108080810408201),
    (((0, 1), (0, 2), (2, 3), (1, 3)), 9, 0x84820408002040248203080020102482030400201024820304002010248203040020102482030400201024820304009010210203040020102102030408201),
    (((0, 1), (0, 2), (3, 3), (1, 2)), 12, 0x80820308002010808203080020108082030800201080820308002010208203260020102082032600201024820326009130248203260091302481830408913024818304089130208183040820102081830408201),
    (((0, 1), (0, 3), (1, 2), (2, 3)), 9, 0x221020408102012208204060020122082010600201220820106002012208201060020122082010600201220820106002110808201060020108080810600201),
    (((0, 1), (0, 3), (1, 3), (2, 2)), 12, 0x80820308002010808203080020108082030800201080820308002012208203060090122082030600901220820106489112208201064891104080810648211040808106482110408083060020104080830600201),
    (((0, 1), (0, 3), (2, 3), (1, 2)), 9, 0x81020408102040208203060020102082030600201020820306002010208203060020102082030600201020820306002010208203060020102082030600201),
    (((0, 1), (1, 2), (2, 3), (0, 3)), 9, 0x81020408102040848203084020108482030840201004820304402010048203044020100488030440901004880304409010000203040820100002030408201),
    (((0, 1), (1, 2), (3, 3), (0, 2)), 12, 0x80820308a0201080820308c020108082030840201080820308a020100082032640201000820326a0201004820326a09130048203264091300481830408913004818304089130008183040820100081830408201),
    (((0, 1), (1, 3), (0, 2), (2, 3)), 9, 0x81020408102040808004061020108080040610201080800406102010808004061020108080040610201080800406102010808004061020108080040610201),
    (((0, 1), (1, 3), (0, 3), (2, 2)), 12, 0x80820408102040808204081020408082040810204080820408102040808003061090108080030610901080800306489010808003064890104080030648201040800306482010408003061020104080030610201),
    (((0, 1), (2, 2), (0, 3), (1, 3)), 12, 0x81020408102040810204081020408482040810904084820408109040248003040890102480030408901024800304089010248003040890102480030408901024800304089010210003040820102100030408201),
    (((0, 1), (2, 2), (1, 3), (0, 3)), 12, 0x8482030840201084820308402010048203044020100482030440201004820304e0911004820304a0911224808304089012248083040890122488010408911224880104089110000081040820100000810408201),
    (((0, 1), (2, 2), (3, 3), (0, 1)), 12, 0x848203084020102e82032640901004820304409010048803260891300c8803040890102001830408913020080326089010248183260890102008030408913024880304089130200183040820102001830408201),
    (((0, 1), (2, 3), (0, 1), (2, 3)), 9, 0x220800406109012208004061090122480010608901220800106089012208001040890122080010608901220800106089110808001060820108080810608201),
    (((0, 1), (2, 3), (0, 3), (1, 2)), 9, 0x80820406109040208003061090102080030608901020800306089010208003060890102480030608901020800306089010208003040820102080030608201),
    (((0, 1), (2, 3), (1, 2), (0, 3)), 9, 0x22102040700901221080406c090122488010608901220080106089012200801040890122008010608901220080106089110000201060820100000810608201),
    (((0, 1), (2, 3), (1, 3), (0, 2)), 12, 0x8082030860201080820309202010808203084020100082030640901000820306e091100088030608901224808306089012200803060891122088010408911220008106089110000081060820100080810608201),
    (((0, 1), (2, 3), (2, 3), (0, 1)), 9, 0x21080406109040248803064090102008030608901000080304089010200803060890102008030608901020080306089010200203060820102002030608201),
    (((0, 1), (3, 3), (0, 1), (2, 2)), 12, 0x808204061020408082040610904220801306102012208013064891152080010610981040808106489812208013060c9010408013060c90122080010648981220800106489910408001060c2010408081060c201),
    (((0, 1), (3, 3), (1, 2), (0, 2)), 12, 0x8082040610204080820406102010808204061020122082130640211520821b061020100080810640981220881306a02010008813060c981220080106409912200801060c9910000081060c2010000081060c201),
    (((0, 3), (0, 2), (1, 3), (1, 2)), 12, 0x80820308002410808203080022908082030800211080821308002110248083260092902480832600191020809304089030208083040090302480932608191024809326089110208083040018302080830408183),
    (((0, 3), (0, 3), (1, 1), (2, 2)), 12, 0x80822b0800211080823b08002112208093060091122080b306009112208081064819122080810648191040808106009110408081060091122080932648191220809326481910408081060018304080810600183),
    (((0, 3), (0, 3), (1, 2), (1, 2)), 9, 0x21021306102110208213060021102080930600191020809306001910208093060019102080930600191220809326001910208084060018402080810600183),
    (((0, 3), (1, 2), (1, 2), (0, 3)), 9, 0x81020408102042248813264091122488132640911000008104081830000081040818322488132640911224881326409110000081040818300000810408183),
    (((0, 3), (1, 2), (1, 3), (0, 2)), 12, 0x80820308c0229080820308e02390808203084021108082030840231004809326a091100480932640911000808304081830008083040818300480932640911004809326409110008083040818300080830408183),
    (((0, 3), (2, 2), (1, 1), (0, 3)), 12, 0x2248c3b2640911224a813a64091100480810408903000008104081912249813040891122480ab5640911224808104081910048081040819122480810440911224809304409110000081040818300000810408183),
    (((0, 3), (2, 2), (1, 3), (0, 1)), 12, 0x24880326409110248803264091100000830408903000008304089032248803260891102488032608911020008104089030200083040890302488132608911224881326089110200083040818302000810408183),
    (((1, 1), (0, 0), (3, 3), (2, 2)), 16, 0x8082030800201080820308002010808203080020108082030800201080820308002010808203080020108082030800201080820308002010808203080020108082030800201080820308002010808203080020108082030800201080820308002010808203080020108082030800201),
    (((1, 1), (0, 2), (3, 3), (0, 2)), 16, 0x8082030800201080820308002010808203080020108082030800201080820308002010808203080020108082030800201080820308002010848203084020108482030840201004820304402010048203044020100488030440901004880304409010000203040820100002030408201),
    (((1, 1), (0, 3), (0, 3), (2, 2)), 12, 0x80820308002010808203080020108082030800201080820308002012208003060090122080030600901220801106489012208011064890104080110648081040801106480810408003060008104080030600081),
    (((1, 1), (2, 2), (3, 3), (0, 0)), 16, 0x8482030840201084820308402010048203044020100482030440201004820304402010048203044020100482030440201004820304402010048203044020100482030440201004820304402010048203044020100488030440901004880304409010000203040820100002030408201),
    (((1, 1), (2, 3), (0, 3), (0, 2)), 12, 0x80820308402010808203090020100080030640901220800306a09010048003060890122080110608901224880304095012208811060808100000110440901000001106400810008003060808100080030608081),
    (((1, 1), (3, 3), (0, 0), (2, 2)), 12, 0x220801306409012208013064090120080110648981200801106489810408000060c0810408000060c081220801306409012208013064090120080110648981200801106489810408000060c0810408000060c081),
    (((1, 2), (0, 3), (0, 3), (1, 2)), 9, 0x81020408102040208003060010102080030600101020800306001010208003060010102080030600101020800306001010208003060010102080030600101),
    (((1, 2), (0, 3), (1, 3), (0, 2)), 12, 0x80820308002010808203080020108082030800211080820308402012208083060010100088030640111220880106001010000083060010122008010640111220880306401110000081060010100000810600101),
    (((1, 2), (2, 3), (1, 3), (0, 0)), 12, 0x224880306401112248803064010100000810440101000080104401010048803064090100008030640911000080304081010000083060810122008030640911224880306409110000081060810100000810408101),
    (((1, 3), (0, 2), (1, 3), (0, 2)), 16, 0x8082030800201080820308002010808203080020108082030800201080820308002010808203080020108482130840211080821308402110048093044019100480932640191004809304401910048083040018300480930440191224881304409110008083040018100000810408181),
    (((1, 3), (2, 2), (1, 3), (0, 0)), 16, 0x8482030840201084820308402010048203044020100482030440201004821304402110048213044021100480830440191004809304401810048093044091100488130440191004808304081810000083044018122488130440911004881326409110000081040818100000830408183),
    (((1, 3), (2, 3), (0, 1), (0, 2)), 12, 0x220801306409012208813064090100480012608191000000106081812248093044090322080130640901000880104081810008001060819122000132640901220809306409010008001060818300080010608181),
    (((3, 3), (2, 2), (1, 1), (0, 0)), 16, 0x22488132640911224881326409110000081040818300000810408183224881326409112248813264091100000810408183000008104081832248813264091122488132640911000008104081830000081040818322488132640911224881326409110000081040818300000810408183),
)


def route_tables():
    pairs = [(a, b) for b in range(4) for a in range(b + 1)]
    pair_at = {pair: i for i, pair in enumerate(pairs)}
    row_of = np.zeros((79 * 128,), np.int32)
    rows = []
    seen = set()
    for goals, steps, code in ROUTES:
        for flip in range(8):
            names = []
            for chip in range(4):
                y, x = chip // 2 ^ (flip & 1), chip % 2 ^ (flip >> 1 & 1)
                names.append(x * 2 + y if flip & 4 else y * 2 + x)
            moved = [None] * 4
            for chip in range(4):
                moved[names[chip]] = tuple(sorted(names[g] for g in goals[chip]))
            key = sum(pair_at[moved[chip]] * 10**chip for chip in range(4))
            if key in seen:
                continue
            seen.add(key)
            row_of[key] = len(rows)
            rows.append(plan_of(moved, steps, code, names, flip >> 2))
    return row_of.reshape(79, 1, 128), np.stack(rows).reshape(-1, 1, 128)


def plan_of(goals, steps, code, names, swapped):
    back = [names.index(chip) for chip in range(4)]
    own = [{} for _ in range(4)]
    passing = [{} for _ in range(4)]
    for chip in range(4):
        for which in range(2):
            if goals[chip][which] != chip:
                pool = own[chip].setdefault(goals[chip][which], [])
                pool += [(piece, which) for piece in range(PIECES)]
                pool.sort()
    plan = np.full((4, 128), 3, np.int32)
    plan[:, 2 * PLAN_STEPS] = sum(steps > total for total in TOTALS)
    free = [[(0, slot) for slot in range(ROOM)] for _ in range(4)]
    for step in range(steps):
        landed = []
        for chip in range(4):
            for link in range(2):
                at = (step * 4 + back[chip]) * 2 + (link ^ swapped)
                goal, since = code >> 7 * at & 7, code >> 7 * at + 3 & 15
                if goal == 4:
                    continue
                goal = names[goal]
                if since == 0:
                    piece, which = own[chip][goal].pop(-link)
                    source, sent = chip, which | piece << 2
                else:
                    which, piece, source, slot = passing[chip].pop((step - since, 1 - link))
                    sent = 2 | slot << 2
                    free[chip].append((max(step, step - since + LAG), slot))
                plan[chip, 2 * step + link] += sent - 3
                landed.append((chip ^ 1 << link, link, source, which, piece, goal))
        for chip, link, source, which, piece, goal in landed:
            got = (source * 2 + which) << 9 | piece << 12
            if goal == chip:
                got |= 1 << 7
            else:
                at = next(i for i, item in enumerate(free[chip]) if item[0] <= step)
                slot = free[chip].pop(at)[1]
                got |= 2 << 7 | slot << 16
                passing[chip][step, link] = (which, piece, source, slot)
            plan[chip, 2 * step + link] |= got
    assert not any(passing) and not any(pool for chip in own for pool in chip.values())
    return plan


def copy_all(moves, sems, base, phase):
    for number, (condition, source, target) in enumerate(moves):

        def act(number=number, source=source, target=target):
            copy = pltpu.make_async_copy(source, target, sems.at[base + number])
            if phase == 0:
                copy.start()
            else:
                copy.wait()

        if condition is True:
            act()
        else:
            pl.when(condition)(act)


def piece_rows(ref, row, rows):
    return ref.at[pl.ds(pl.multiple_of(row, 16), rows)]


def link_of(step, core):
    return 1 - core if step // 2 % 2 else core


def early_kernel(weights, early, semaphores):
    rows = weights.shape[0] // PIECES
    core = lax.axis_index("req") % 2
    copies = []
    for number in range(EARLY):
        piece = jnp.where(core == 1, number, PIECES - 1 - number)
        part = piece_rows(weights, piece * rows, rows)
        copies.append(pltpu.make_async_copy(part, piece_rows(early, number * rows, rows), semaphores.at[number]))
        copies[-1].start()
    for copy in copies:
        copy.wait()


def plan_kernel(old_place, new_place, row_of, plans, meta, row_part, plan_part, sem):
    me_index = lax.axis_index("req")
    core = me_index % 2
    chip = me_index // 2
    goals = []
    for holder in range(8):
        goal = jnp.int32(0)
        for device in range(8):
            goal = jnp.where(new_place[device] == old_place[holder], device, goal)
        goals.append(goal)
    key = jnp.int32(0)
    my_swap = jnp.int32(0)
    for at in range(4):
        first, second = goals[2 * at], goals[2 * at + 1]
        low, high = jnp.minimum(first, second), jnp.maximum(first, second)
        high_chip = high // 2
        key = key + (high_chip * (high_chip + 1) // 2 + low // 2) * 10**at
        my_swap = jnp.where((first > second) & (chip == at), 1, my_swap)
        meta[GOAL_AT + 2 * at] = low % 2
        meta[GOAL_AT + 2 * at + 1] = high % 2
    meta[CORE_AT] = core
    meta[SWAP_AT] = my_swap
    wanted = new_place[me_index]
    beside = jnp.where(wanted == old_place[me_index + 1 - 2 * core], 2, 0)
    meta[LOCAL_AT] = jnp.where(wanted == old_place[me_index], 1, beside)
    copy = pltpu.make_async_copy(row_of.at[key // 128], row_part, sem)
    copy.start()
    copy.wait()
    row = row_part[0, key % 128]
    copy = pltpu.make_async_copy(plans.at[row * 4 + chip], plan_part, sem)
    copy.start()
    copy.wait()
    for at in range(2 * PLAN_STEPS):
        meta[at] = plan_part[0, at]
    meta[TOTAL_AT] = plan_part[0, 2 * PLAN_STEPS]


def step_kernel(rows, step, come, local_pieces, names, count, meta, *refs):
    refs = list(zip(names, refs))
    semaphores = refs.pop()[1]
    given = {}
    for number, (name, ref) in enumerate(refs):
        if number >= count or name not in ("out", "room"):
            given.setdefault(name, []).append(ref)
    w_hbm = given["weights"][0]
    out_hbm = given.get("out", [None])[0]
    room = given.get("room", [None])[0]
    core = meta[CORE_AT]
    local = meta[LOCAL_AT]
    used = 0
    stores, moves = [], []
    swap = given.get("swap", [None])[0]
    brought = [("landed", core, step_at) for step_at in come[0]]
    brought += [("swapped", 1 - core, step_at) for step_at in come[1]]
    for name, side, step_at in brought:
        word = meta[2 * step_at + link_of(step_at, side)]
        kind = (word >> 7) & 3
        row = ((word >> 12) & 15) * rows
        source = given[name].pop(0).at[pl.ds(0, rows)]
        if room is not None:
            slot = (word >> 16) & 31
            stores.append((kind == 2, source, piece_rows(room, slot * rows, rows)))
        final = (kind == 1) & (meta[GOAL_AT + ((word >> 9) & 7)] == core)
        moves.append((final, source, piece_rows(out_hbm, row, rows)))
        if name == "landed" and swap is not None:
            moves.append((jnp.logical_not(final), source, swap))
    copy_all(stores, semaphores, used, 0)
    copy_all(stores, semaphores, used, 1)
    used += len(stores)
    riding = []
    if "sent" in given:
        target = given["sent"][0].at[pl.ds(0, rows)]
        if "extra" in given:
            riding.append((True, given["extra"][0], given["sent"][0].at[pl.ds(rows, RIDE)]))
        word = meta[2 * step + link_of(step, core)]
        kind = word & 3
        piece = (word >> 2) & 31
        held = kind == 2
        mine = ((kind ^ meta[SWAP_AT]) == core) | (kind == 3)
        theirs = jnp.logical_not(held | mine)
        options = [(jnp.logical_not(held) & mine, piece_rows(w_hbm, piece * rows, rows))]
        if "other" in given:
            options.append((theirs, piece_rows(given["other"][0], piece * rows, rows)))
        place = jnp.where(core == 0, piece, PIECES - 1 - piece)
        if "early" in given:
            options.append((theirs, piece_rows(given["early"][0], place * rows, rows)))
        if room is not None:
            options.append((held, piece_rows(room, piece * rows, rows)))
        for condition, source in options:

            @pl.when(condition)
            def _(source=source):
                pltpu.make_async_copy(source, target, semaphores.at[used]).start()

        fetched = pltpu.make_async_copy(w_hbm.at[pl.ds(0, rows)], target, semaphores.at[used])
        used += 1
    copy_all(riding, semaphores, used, 0)
    first_ride = used
    used += len(riding)
    copy_all(moves, semaphores, used, 0)
    first_move = used
    used += len(moves)
    reads, writes = [], []
    for number, piece in enumerate(local_pieces):
        part = given["staged"][0].at[number]
        row = piece * rows
        reads.append((local == 1, piece_rows(w_hbm, row, rows), part))
        reads.append((local == 2, piece_rows(given["other"][0], row, rows), part))
        writes.append((local != 0, part, piece_rows(out_hbm, row, rows)))
    copy_all(reads, semaphores, used, 0)
    if "sent" in given:
        fetched.wait()
    copy_all(riding, semaphores, first_ride, 1)
    copy_all(reads, semaphores, used, 1)
    used += len(reads)
    copy_all(writes, semaphores, used, 0)
    copy_all(moves, semaphores, first_move, 1)
    copy_all(writes, semaphores, used, 1)


def between_cores(array):
    return lax.ppermute(array, "req", [(i, i ^ 1) for i in range(8)])


def along_links(array, step):
    return lax.ppermute(array, "req", [(i, i ^ (2 << link_of(step, i % 2))) for i in range(8)])


def plan_plane(old_place, new_place):
    row_of, plans = route_tables()
    smem = pl.BlockSpec(memory_space=pltpu.SMEM)
    anywhere = pl.BlockSpec(memory_space=pl.ANY)
    return pl.pallas_call(
        plan_kernel,
        out_shape=jax.ShapeDtypeStruct((META,), jnp.int32),
        in_specs=[smem, smem, anywhere, anywhere],
        out_specs=smem,
        scratch_shapes=[
            pltpu.SMEM((1, 128), jnp.int32),
            pltpu.SMEM((1, 128), jnp.int32),
            pltpu.SemaphoreType.DMA,
        ],
        name="plan_steps",
    )(old_place, new_place, jnp.asarray(row_of), jnp.asarray(plans))


def early_pieces(weights):
    width, columns = weights.shape
    return pl.pallas_call(
        early_kernel,
        out_shape=jax.ShapeDtypeStruct((width // PIECES * EARLY, columns), weights.dtype),
        in_specs=[pl.BlockSpec(memory_space=pl.ANY)],
        out_specs=pl.BlockSpec(memory_space=pltpu.VMEM),
        scratch_shapes=[pltpu.SemaphoreType.DMA((EARLY,))],
        compiler_params=pltpu.CompilerParams(vmem_limit_bytes=32 << 20),
        name="early_pieces",
    )(weights)


def migrate_plane(weights, meta, early, total, beside):
    width, columns = weights.shape
    rows = width // PIECES
    smem = pl.BlockSpec(memory_space=pltpu.SMEM)
    anywhere = pl.BlockSpec(memory_space=pl.ANY)
    near = pl.BlockSpec(memory_space=pltpu.VMEM)
    whole = jax.ShapeDtypeStruct((width, columns), weights.dtype)
    room_like = jax.ShapeDtypeStruct((ROOM * rows, columns), weights.dtype)
    held = {"out": None, "room": None}

    def run(meta, step, come, sources, local_pieces, extra, store, swap):
        operands, specs, names, aliases = [meta, weights], [smem, anywhere], ["weights"], {}

        def add(name, array, spec):
            if array is not None:
                operands.append(array)
                specs.append(spec)
                names.append(name)

        for name, array in sources:
            add(name, array, anywhere)
        for step_at in come[0]:
            add("landed", landed[step_at], near)
        for step_at in come[1]:
            add("swapped", swapped[step_at], near)
        add("extra", extra, near)
        results = []
        if step is not None:
            sent_rows = rows + (RIDE if step < RIDES else 0)
            results.append(("sent", jax.ShapeDtypeStruct((sent_rows, columns), weights.dtype), near))
        if swap:
            like = jax.ShapeDtypeStruct((rows, columns), weights.dtype)
            results.append(("swap", like, near))
        for name, like, wanted in (
            ("out", whole, bool(local_pieces or come[0] or come[1])),
            ("room", room_like, store),
        ):
            if wanted:
                if held[name] is not None:
                    aliases[len(operands)] = len(results)
                    add(name, held[name], anywhere)
                results.append((name, like, anywhere))
        count = len(names)
        names += [name for name, _, _ in results]
        scratch = []
        if local_pieces:
            scratch.append(pltpu.VMEM((len(local_pieces), rows, columns), weights.dtype))
            names.append("staged")
        scratch.append(pltpu.SemaphoreType.DMA((24,)))
        names.append("semaphores")
        values = pl.pallas_call(
            functools.partial(
                step_kernel, rows, step, come, local_pieces, names, count
            ),
            out_shape=[like for _, like, _ in results],
            in_specs=specs,
            out_specs=[spec for _, _, spec in results],
            scratch_shapes=scratch,
            input_output_aliases=aliases,
            compiler_params=pltpu.CompilerParams(vmem_limit_bytes=32 << 20),
            cost_estimate=pl.CostEstimate(
                flops=0, bytes_accessed=4 * rows * columns * 2, transcendentals=0
            ),
            name="place_pieces" if step is None else "step_pieces",
        )(*operands)
        for (name, _, _), value in zip(results, values):
            if name in held:
                held[name] = value
        return values

    landed, swapped = {}, {}
    ridden = None
    other = between_cores(weights)
    for step in range(total):
        meta, extra = beside(step, meta, ridden)
        come = [step - 2] if step >= 2 else [], [step - LAG] if step >= LAG else []
        sources = [("early", early) if step < EARLY else ("other", other)]
        local_pieces = LOCAL_PIECES.get(step, ())
        some = step >= 2
        values = run(meta, step, come, sources, local_pieces, extra, some, some)
        meta, _ = lax.optimization_barrier((meta, values[0]))
        landed[step] = along_links(values[0], step)
        if extra is not None:
            ridden = landed[step][rows:]
        if some:
            swapped[step - 2] = between_cores(values[1])
    last = total - 1
    meta, _ = beside(total, meta, ridden)
    come = [last - 1], list(range(total - LAG, last - 2))
    values = run(meta, None, come, (), (), None, False, True)
    swapped[last - 1] = between_cores(values[0])
    swapped[last] = between_cores(landed[last])
    run(meta, None, ([last], [last - 2, last - 1]), (), (), None, False, False)
    run(meta, None, ([], [last]), (), (), None, False, False)
    return held["out"]


def plane_dispatch(hidden, chosen, weights_now, place, gain):
    batches, tok_rows, width = hidden.shape
    topk = chosen.shape[-1]
    tokens = batches * tok_rows
    nreq = lax.axis_size("req")
    me_index = lax.axis_index("req")
    resid = hidden.reshape(tokens, width).astype(jnp.float32)
    normed = (
        resid * gain / jnp.sqrt(jnp.mean(resid * resid, axis=-1, keepdims=True) + 1e-05)
    ).astype(jnp.bfloat16)
    flat_ids = chosen.reshape(-1)
    devices = jnp.arange(nreq, dtype=jnp.int32)
    holder = jnp.sum(jnp.where(flat_ids[:, None] == place[None, :], devices[None, :], 0), axis=1)
    assign_index = jnp.arange(flat_ids.shape[0], dtype=jnp.int32)
    batch_of = assign_index // (tok_rows * topk)
    earlier = (
        (flat_ids[:, None] == flat_ids[None, :])
        & (batch_of[:, None] == batch_of[None, :])
        & (assign_index[None, :] < assign_index[:, None])
    )
    rank_in = jnp.sum(earlier.astype(jnp.int32), axis=1)
    slot = (holder ^ me_index) * SLOTS + batch_of * CAP + rank_in
    hit = slot[:, None] == jnp.arange(nreq * SLOTS, dtype=jnp.int32)[None, :]
    hit = hit.reshape(tokens, topk, nreq * SLOTS)
    coef = jnp.sum(jnp.where(hit, weights_now.reshape(tokens, topk, 1), 0.0), axis=1)
    blocks = jnp.any(hit, axis=1).T
    order = [k for k in range(nreq) if k & 1] + [k for k in range(nreq) if not k & 1]
    blocks = blocks.reshape(nreq, SLOTS, tokens)[jnp.array(order)].reshape(nreq * SLOTS, tokens)
    outgoing = jnp.dot(
        blocks.astype(jnp.bfloat16), normed, preferred_element_type=jnp.float32
    ).astype(jnp.bfloat16)
    half = nreq * SLOTS // 2
    came = between_cores(outgoing[:half])
    return jnp.concatenate([came, outgoing[half:]]), coef


def reordered(rows, orders):
    core = lax.axis_index("req") % 2
    spread = [np.eye(rows.shape[0], dtype=np.float32)[np.array(order)] for order in orders]
    chosen = jnp.where(core == 0, spread[0], spread[1]).astype(rows.dtype)
    return jnp.dot(chosen, rows, preferred_element_type=jnp.float32).astype(rows.dtype)


def exchange(rows, labels, bits):
    orders = []
    for core in range(2):
        going = [i for i, label in enumerate(labels[core]) if label // SLOTS >> bits[core] & 1]
        orders.append(going + [i for i in range(len(labels[core])) if i not in going])
    rows = reordered(rows, orders)
    half = rows.shape[0] // 2
    came = yield bits[0] > 0, rows[:half]
    labels = [[labels[core][i] for i in orders[core]] for core in range(2)]
    if bits[0] == 0:
        labels = [labels[1 - core][:half] + labels[core][half:] for core in range(2)]
    return jnp.concatenate([came, rows[half:]]), labels


def plane_work(attention, hidden, rows, coef, shard_weights):
    batches, tok_rows, width = hidden.shape
    tokens = batches * tok_rows
    ntp = lax.axis_size("tp")
    hid_dev = shard_weights.shape[1] // 3
    every = range(rows.shape[0])
    first = [i for i in every if i // SLOTS & 1] + [i for i in every if not i // SLOTS & 1]
    labels = [first, first]
    rows, labels = yield from exchange(rows, labels, (1, 2))
    context = yield False, attend(*attention)
    rows, labels = yield from exchange(rows, labels, (2, 1))
    gate_up = jnp.dot(rows, shard_weights[:, : 2 * hid_dev], preferred_element_type=jnp.float32)
    act = (jax.nn.silu(gate_up[:, :hid_dev]) * gate_up[:, hid_dev:]).astype(jnp.bfloat16)
    part = lax.dot_general(
        act,
        shard_weights[:, 2 * hid_dev :],
        (((1,), (1,)), ((), ())),
        preferred_element_type=jnp.float32,
    )
    rows = part.astype(jnp.bfloat16)
    rows, labels = yield from exchange(rows, labels, (1, 2))
    rows, labels = yield from exchange(rows, labels, (2, 1))
    swap = exchange(rows, labels, (0, 0))
    _, going = next(swap)
    try:
        swap.send(between_cores(going))
    except StopIteration as end:
        rows, labels = end.value
    rows = yield False, rows
    rows = reordered(rows, [[label.index(i) for i in every] for label in labels])
    partial_sum = jnp.dot(
        coef,
        rows.astype(jnp.float32),
        precision=lax.Precision.HIGHEST,
        preferred_element_type=jnp.float32,
    )
    tp_index = lax.axis_index("tp")
    tp_width = width // ntp

    def share_of(index):
        start = lax.rem(index, ntp) * tp_width
        return lax.dynamic_slice_in_dim(partial_sum, start, tp_width, 1)

    total = share_of(tp_index)
    for ahead in range(1, ntp):
        pairs = [(i, (i + ahead) % ntp) for i in range(ntp)]
        share = share_of(tp_index + ahead).astype(jnp.bfloat16)
        total = total + lax.ppermute(share, "tp", pairs).astype(jnp.float32)
    total = yield False, total
    resid = hidden.reshape(tokens, width).astype(jnp.float32)
    resid_share = lax.dynamic_slice_in_dim(resid, tp_index * tp_width, tp_width, 1)
    summed = (resid_share + total).astype(jnp.bfloat16)
    return context, summed.reshape(batches, tok_rows, tp_width)


def attend(queries, new_keys, new_values, cache_keys, cache_values, lengths):
    batches, tok_rows, width = queries.shape
    heads = width // HEAD_SIZE
    pool = cache_keys.shape[0]
    scale = HEAD_SIZE ** (-0.5)
    req_lengths = lengths.reshape(-1)
    starts = jnp.cumsum(req_lengths) - req_lengths
    position = jnp.arange(pool, dtype=jnp.int32)
    owned = (position[None, :] >= starts[:, None]) & (
        position[None, :] < (starts + req_lengths)[:, None]
    )
    query_rows = queries.reshape(batches * tok_rows, heads, HEAD_SIZE)
    own_keys = new_keys.reshape(batches * tok_rows, heads, HEAD_SIZE)
    own_values = new_values.reshape(batches * tok_rows, heads, HEAD_SIZE)
    pool_keys = cache_keys.reshape(pool, heads, HEAD_SIZE)
    pool_values = cache_values.reshape(pool, heads, HEAD_SIZE)
    scores = (
        jnp.einsum("qhd,phd->hqp", query_rows, pool_keys, preferred_element_type=jnp.float32)
        * scale
    )
    scores = jnp.where(owned[None], scores, -jnp.inf)
    own_score = (
        jnp.einsum("qhd,qhd->hq", query_rows, own_keys, preferred_element_type=jnp.float32) * scale
    )
    highest = jnp.maximum(jnp.max(scores, axis=-1), own_score)
    exp_pool = jnp.exp(scores - highest[..., None])
    exp_own = jnp.exp(own_score - highest)
    denom = jnp.sum(exp_pool, axis=-1) + exp_own
    summed = jnp.einsum(
        "hqp,phd->qhd",
        exp_pool.astype(jnp.bfloat16),
        pool_values,
        preferred_element_type=jnp.float32,
    )
    prob_own = lax.optimization_barrier(exp_own.astype(jnp.bfloat16)).astype(jnp.float32)
    summed = summed + prob_own.T[:, :, None] * own_values.astype(jnp.float32)
    context = (summed / denom.T[:, :, None]).astype(jnp.bfloat16)
    return context.reshape(batches, tok_rows, width)


def choose_holders(place, me_index, nreq, shard_count):
    devices = jnp.arange(nreq, dtype=jnp.int32)
    holder = place[None, :] == jnp.arange(shard_count, dtype=jnp.int32)[:, None]
    before = (place[:, None] == place[None, :]) & (devices[:, None] < devices[None, :])
    rank_in = jnp.sum(before.astype(jnp.int32), axis=0)
    count = jnp.sum(holder.astype(jnp.int32), axis=1)
    wanted = me_index % count
    match = holder & (rank_in[None, :] == wanted[:, None])
    return jnp.sum(jnp.where(match, devices[None, :], 0), axis=1)


def expert_block(hidden, chosen, weights_now, place, shard_weights, gain):
    nreq = lax.axis_size("req")
    me_index = lax.axis_index("req")
    split_count = max(1, nreq // 16)
    shard_count = EXPERTS * split_count
    batches, tok_rows, width = hidden.shape
    topk = chosen.shape[-1]
    tokens = batches * tok_rows
    hid_dev = shard_weights.shape[1] // 3
    resid = hidden.reshape(tokens, width).astype(jnp.float32)
    normed = (
        resid * gain / jnp.sqrt(jnp.mean(resid * resid, axis=-1, keepdims=True) + 1e-05)
    ).astype(jnp.bfloat16)
    flat_ids = chosen.reshape(-1)
    assigns = flat_ids.shape[0]
    slots_dev = batches * CAP
    shard_dest = choose_holders(place, me_index, nreq, shard_count)
    shard_list = flat_ids[:, None] * split_count + jnp.arange(split_count, dtype=jnp.int32)[None, :]
    pick = shard_list[:, :, None] == jnp.arange(shard_count, dtype=jnp.int32)[None, None, :]
    dest = jnp.sum(jnp.where(pick, shard_dest[None, None, :], 0), axis=-1)
    assign_index = jnp.arange(assigns, dtype=jnp.int32)
    batch_of = assign_index // (tok_rows * topk)
    earlier = (
        (flat_ids[:, None] == flat_ids[None, :])
        & (batch_of[:, None] == batch_of[None, :])
        & (assign_index[None, :] < assign_index[:, None])
    )
    rank_in = jnp.sum(earlier.astype(jnp.int32), axis=1)
    slot = dest * slots_dev + (batch_of * CAP + rank_in)[:, None]
    slot_hit = slot[:, :, None] == jnp.arange(nreq * slots_dev, dtype=jnp.int32)[None, None, :]
    by_token = jnp.any(slot_hit.reshape(tokens, topk * split_count, nreq * slots_dev), axis=1)
    outgoing = jnp.dot(
        by_token.T.astype(jnp.bfloat16), normed, preferred_element_type=jnp.float32
    )
    outgoing = outgoing.astype(jnp.bfloat16).reshape(nreq, slots_dev, width)
    received = lax.all_to_all(outgoing, "req", split_axis=0, concat_axis=0, tiled=True)
    flat_rows = received.reshape(nreq * slots_dev, width)
    gate_up = jnp.dot(
        flat_rows, shard_weights[:, : 2 * hid_dev], preferred_element_type=jnp.float32
    )
    act = (jax.nn.silu(gate_up[:, :hid_dev]) * gate_up[:, hid_dev:]).astype(jnp.bfloat16)
    part = lax.dot_general(
        act,
        shard_weights[:, 2 * hid_dev :],
        (((1,), (1,)), ((), ())),
        preferred_element_type=jnp.float32,
    )
    part = part.astype(jnp.bfloat16).reshape(nreq, slots_dev, width)
    returned = lax.all_to_all(part, "req", split_axis=0, concat_axis=0, tiled=True)
    returned = returned.reshape(nreq * slots_dev, width)
    coef = jnp.sum(
        jnp.where(
            slot_hit.reshape(tokens, topk, split_count, nreq * slots_dev),
            weights_now.reshape(tokens, topk)[:, :, None, None],
            0.0,
        ),
        axis=(1, 2),
    )
    partial_sum = jnp.dot(
        coef,
        returned.astype(jnp.float32),
        precision=lax.Precision.HIGHEST,
        preferred_element_type=jnp.float32,
    )
    tp_width = width // lax.axis_size("tp")
    tp_start = lax.axis_index("tp") * tp_width
    resid_share = lax.dynamic_slice_in_dim(resid, tp_start, tp_width, 1)
    share = lax.psum_scatter(
        partial_sum.astype(jnp.bfloat16), "tp", scatter_dimension=1, tiled=True
    ).astype(jnp.float32)
    summed = (resid_share + share).astype(jnp.bfloat16)
    return summed.reshape(batches, tok_rows, tp_width)


def migrate(old_weights, old_place, new_place):
    nreq = lax.axis_size("req")
    shard_count = EXPERTS * max(1, nreq // 16)
    _, width, columns = old_weights.shape
    piece = width // nreq
    pieces = old_weights.reshape(nreq, piece, columns)
    spread = lax.all_to_all(pieces, "req", split_axis=0, concat_axis=0, tiled=True)
    devices = jnp.arange(nreq, dtype=jnp.int32)
    shard_ids = jnp.arange(shard_count, dtype=jnp.int32)
    first_old = jnp.min(
        jnp.where(old_place[None, :] == shard_ids[:, None], devices[None, :], nreq), axis=1
    )
    needed = jnp.sum(
        jnp.where(new_place[:, None] == shard_ids[None, :], first_old[None, :], 0), axis=1
    )
    sending = spread[needed]
    collected = lax.all_to_all(sending, "req", split_axis=0, concat_axis=0, tiled=True)
    return collected.reshape(1, width, columns)


def plane_outputs(attention, layer, new_place):
    hidden, expert_ids, route_weights, old_place, weights, gain = layer
    early = early_pieces(weights)
    first = between_cores(early)
    hidden, _ = lax.optimization_barrier((hidden, early))
    meta = plan_plane(old_place, new_place)
    received, coef = plane_dispatch(hidden, expert_ids, route_weights, old_place, gain)

    def within(total):
        def outputs(weights, meta, first, attention, hidden, rows, coef):
            work = plane_work(attention, hidden, rows, coef, weights)
            stage = next(work)
            done = None
            pending = []

            def beside(step, meta, ridden):
                nonlocal stage, done
                for _ in range(STAGES.get(step, 0) + (step == min(total, 11))):
                    rides, value = stage
                    if pending:
                        pending.pop()
                        half = value.shape
                        value = ridden.reshape(half)
                    elif rides:
                        pending.append(True)
                        return meta, value.reshape(RIDE, weights.shape[1])
                    else:
                        meta, value = lax.optimization_barrier((meta, value))
                    try:
                        stage = work.send(value)
                    except StopIteration as end:
                        done = end.value
                return meta, None

            moved = migrate_plane(
                weights, meta, first, total, beside
            )
            return (*done, moved[None])

        return outputs

    branches = [within(total) for total in TOTALS]
    return lax.switch(meta[TOTAL_AT], branches, weights, meta, first, attention, hidden, received, coef)


def on_device(
    queries,
    new_keys,
    new_values,
    cache_keys,
    cache_values,
    lengths,
    hidden,
    gain,
    expert_ids,
    route_weights,
    old_place,
    new_place,
    old_weights,
):
    attention = (queries, new_keys, new_values, cache_keys, cache_values, lengths)
    layer = (hidden, expert_ids, route_weights, old_place, old_weights[0], gain)
    if lax.axis_size("req") == 8:
        return plane_outputs(attention, layer, new_place)
    context = attend(*attention)
    moved = migrate(old_weights, old_place, new_place)
    layer_out = expert_block(*layer)
    return (context, layer_out, moved)


def solution(mesh):
    in_specs = (
        P(None, "req", "tp"),
        P(None, "req", "tp"),
        P(None, "req", "tp"),
        P("req", "tp"),
        P("req", "tp"),
        P("req", None),
        P(None, "req", None),
        P(),
        P(None, "req", None),
        P(None, "req", None),
        P(),
        P(),
        P("req", None, "tp"),
    )
    out_specs = (P(None, "req", "tp"), P(None, "req", "tp"), P("req", None, "tp"))
    return jax.shard_map(
        on_device, mesh=mesh, in_specs=in_specs, out_specs=out_specs, check_vma=False
    )
```

```python
import functools

import jax
import jax.numpy as jnp
import numpy as np
from jax import lax
from jax.experimental import pallas as pl
from jax.experimental.pallas import tpu as pltpu
from jax.sharding import PartitionSpec as P

HEAD_SIZE = 64
EXPERTS = 8
CAP = 3
PIECES = 8
TOTALS = (9, 12, 16)
EARLY = 2
LAG = 5
ROOM = 16
SLOTS = 6
RIDE = 16
RIDES = 7
STAGES = {0: 1, 2: 2, 4: 2, 6: 3, 9: 2}
LOCAL_PIECES = {4: (0, 1), 5: (2, 3), 6: (4, 5), 7: (6, 7)}
PLAN_STEPS = max(TOTALS)
CORE_AT = 2 * PLAN_STEPS
SWAP_AT = CORE_AT + 1
LOCAL_AT = CORE_AT + 2
GOAL_AT = CORE_AT + 3
TOTAL_AT = CORE_AT + 11
META = CORE_AT + 12

ROUTES = (
    (((0, 0), (1, 1), (2, 2), (3, 3)), 9, 0x81020408102040810204081020408102040810204081020408102040810204081020408102040810204081020408102040810204081020408102040810204),
    (((0, 0), (1, 1), (2, 3), (2, 3)), 9, 0x81020408102040808203081020408082030810204080820308102040808203081020408082030810204080820308102040808203081020408082030810204),
    (((0, 0), (1, 1), (3, 3), (2, 2)), 12, 0x80820308102040808203081020408082030810204080820308102040808203261090408082032610904080820326489130808203264891304081830848213040818308482130408183081020404081830810204),
    (((0, 0), (1, 2), (1, 2), (3, 3)), 9, 0x81020408102040810204081020408102040810204224820408109112248204081091122480810408911224808104089110810081040820408100810408204),
    (((0, 0), (1, 2), (1, 3), (2, 3)), 9, 0x80820308109110808203081091108080830808911080808308089110808083080891108080830808911224808308089110808083080820408080810408204),
    (((0, 0), (1, 2), (2, 3), (1, 3)), 9, 0x81020408102040210203081020402102030810204024820308109040248203081090402482030408904024820304089040210203040820402102030408204),
    (((0, 0), (1, 2), (3, 3), (1, 2)), 12, 0x81020308102040810203081020408082030810204080820308102040208203261090402082032610904020820326089130208203260891302481830808913024818308089130208183040820402081830408204),
    (((0, 0), (1, 3), (1, 3), (2, 2)), 12, 0x80820408102040808204081020408082040810204080820308102110808203061091108080830610911080808306489112208083064891104080830648211040808106482110408083061020404080830610204),
    (((0, 0), (1, 3), (2, 3), (1, 2)), 9, 0x81020408102040208203061020402082030610204020820306102040208203061020402082030610204020820306102040208203061020402082030610204),
    (((0, 0), (2, 2), (1, 1), (3, 3)), 12, 0x81020408102040810204081020422482040810911224820408109112248081040891122480810408911224808104089112248081040891122480810408911224808104089110810081040820408100810408204),
    (((0, 0), (2, 2), (1, 3), (1, 3)), 12, 0x81020408102040810204081020408482040810911084820408109110248083040891102480830408911024808304089110248083040891102480830408911024808304089110210083040820402100830408204),
    (((0, 0), (2, 2), (3, 3), (1, 1)), 12, 0x210203081090402102030810911024820326089040248883260891102a8203040891302048830408913024818326089110204183260891102488830408913024888304089130204183040820402041830408204),
    (((0, 0), (2, 3), (1, 3), (1, 2)), 9, 0x20820306109110248203061091102080830608911020808304089110208083060891122080830608911020808306089110208081060820402080830608204),
    (((0, 1), (0, 1), (2, 3), (2, 3)), 9, 0x81020408102040808203080020108082030800201080820308002010808203080020108082030800201080820308002010808203080020108082030800201),
    (((0, 1), (0, 1), (3, 3), (2, 2)), 12, 0x80820308002010808203080020108082030800201080820308002010808203260090108082032600901080820326489130808203264891304081830848213040818308482130408183080020104081830800201),
    (((0, 1), (0, 2), (1, 3), (2, 3)), 12, 0x80820308002010808203080020108082030800201080820308002010808203080020108082030800201224820308009112248203080091122480810408911224808104089110808081040820108080810408201),
    (((0, 1), (0, 2), (2, 3), (1, 3)), 9, 0x84820408002040248203080020102482030400201024820304002010248203040020102482030400201024820304009010210203040020102102030408201),
    (((0, 1), (0, 2), (3, 3), (1, 2)), 12, 0x80820308002010808203080020108082030800201080820308002010208203260020102082032600201024820326009130248203260091302481830408913024818304089130208183040820102081830408201),
    (((0, 1), (0, 3), (1, 2), (2, 3)), 9, 0x221020408102012208204060020122082010600201220820106002012208201060020122082010600201220820106002110808201060020108080810600201),
    (((0, 1), (0, 3), (1, 3), (2, 2)), 12, 0x80820308002010808203080020108082030800201080820308002012208203060090122082030600901220820106489112208201064891104080810648211040808106482110408083060020104080830600201),
    (((0, 1), (0, 3), (2, 3), (1, 2)), 9, 0x81020408102040208203060020102082030600201020820306002010208203060020102082030600201020820306002010208203060020102082030600201),
    (((0, 1), (1, 2), (2, 3), (0, 3)), 9, 0x81020408102040848203084020108482030840201004820304402010048203044020100488030440901004880304409010000203040820100002030408201),
    (((0, 1), (1, 2), (3, 3), (0, 2)), 12, 0x80820308a0201080820308c020108082030840201080820308a020100082032640201000820326a0201004820326a09130048203264091300481830408913004818304089130008183040820100081830408201),
    (((0, 1), (1, 3), (0, 2), (2, 3)), 9, 0x81020408102040808004061020108080040610201080800406102010808004061020108080040610201080800406102010808004061020108080040610201),
    (((0, 1), (1, 3), (0, 3), (2, 2)), 12, 0x80820408102040808204081020408082040810204080820408102040808003061090108080030610901080800306489010808003064890104080030648201040800306482010408003061020104080030610201),
    (((0, 1), (2, 2), (0, 3), (1, 3)), 12, 0x81020408102040810204081020408482040810904084820408109040248003040890102480030408901024800304089010248003040890102480030408901024800304089010210003040820102100030408201),
    (((0, 1), (2, 2), (1, 3), (0, 3)), 12, 0x8482030840201084820308402010048203044020100482030440201004820304e0911004820304a0911224808304089012248083040890122488010408911224880104089110000081040820100000810408201),
    (((0, 1), (2, 2), (3, 3), (0, 1)), 12, 0x848203084020102e82032640901004820304409010048803260891300c8803040890102001830408913020080326089010248183260890102008030408913024880304089130200183040820102001830408201),
    (((0, 1), (2, 3), (0, 1), (2, 3)), 9, 0x220800406109012208004061090122480010608901220800106089012208001040890122080010608901220800106089110808001060820108080810608201),
    (((0, 1), (2, 3), (0, 3), (1, 2)), 9, 0x80820406109040208003061090102080030608901020800306089010208003060890102480030608901020800306089010208003040820102080030608201),
    (((0, 1), (2, 3), (1, 2), (0, 3)), 9, 0x22102040700901221080406c090122488010608901220080106089012200801040890122008010608901220080106089110000201060820100000810608201),
    (((0, 1), (2, 3), (1, 3), (0, 2)), 12, 0x8082030860201080820309202010808203084020100082030640901000820306e091100088030608901224808306089012200803060891122088010408911220008106089110000081060820100080810608201),
    (((0, 1), (2, 3), (2, 3), (0, 1)), 9, 0x21080406109040248803064090102008030608901000080304089010200803060890102008030608901020080306089010200203060820102002030608201),
    (((0, 1), (3, 3), (0, 1), (2, 2)), 12, 0x808204061020408082040610904220801306102012208013064891152080010610981040808106489812208013060c9010408013060c90122080010648981220800106489910408001060c2010408081060c201),
    (((0, 1), (3, 3), (1, 2), (0, 2)), 12, 0x8082040610204080820406102010808204061020122082130640211520821b061020100080810640981220881306a02010008813060c981220080106409912200801060c9910000081060c2010000081060c201),
    (((0, 3), (0, 2), (1, 3), (1, 2)), 12, 0x80820308002410808203080022908082030800211080821308002110248083260092902480832600191020809304089030208083040090302480932608191024809326089110208083040018302080830408183),
    (((0, 3), (0, 3), (1, 1), (2, 2)), 12, 0x80822b0800211080823b08002112208093060091122080b306009112208081064819122080810648191040808106009110408081060091122080932648191220809326481910408081060018304080810600183),
    (((0, 3), (0, 3), (1, 2), (1, 2)), 9, 0x21021306102110208213060021102080930600191020809306001910208093060019102080930600191220809326001910208084060018402080810600183),
    (((0, 3), (1, 2), (1, 2), (0, 3)), 9, 0x81020408102042248813264091122488132640911000008104081830000081040818322488132640911224881326409110000081040818300000810408183),
    (((0, 3), (1, 2), (1, 3), (0, 2)), 12, 0x80820308c0229080820308e02390808203084021108082030840231004809326a091100480932640911000808304081830008083040818300480932640911004809326409110008083040818300080830408183),
    (((0, 3), (2, 2), (1, 1), (0, 3)), 12, 0x2248c3b2640911224a813a64091100480810408903000008104081912249813040891122480ab5640911224808104081910048081040819122480810440911224809304409110000081040818300000810408183),
    (((0, 3), (2, 2), (1, 3), (0, 1)), 12, 0x24880326409110248803264091100000830408903000008304089032248803260891102488032608911020008104089030200083040890302488132608911224881326089110200083040818302000810408183),
    (((1, 1), (0, 0), (3, 3), (2, 2)), 16, 0x8082030800201080820308002010808203080020108082030800201080820308002010808203080020108082030800201080820308002010808203080020108082030800201080820308002010808203080020108082030800201080820308002010808203080020108082030800201),
    (((1, 1), (0, 2), (3, 3), (0, 2)), 16, 0x8082030800201080820308002010808203080020108082030800201080820308002010808203080020108082030800201080820308002010848203084020108482030840201004820304402010048203044020100488030440901004880304409010000203040820100002030408201),
    (((1, 1), (0, 3), (0, 3), (2, 2)), 12, 0x80820308002010808203080020108082030800201080820308002012208003060090122080030600901220801106489012208011064890104080110648081040801106480810408003060008104080030600081),
    (((1, 1), (2, 2), (3, 3), (0, 0)), 16, 0x8482030840201084820308402010048203044020100482030440201004820304402010048203044020100482030440201004820304402010048203044020100482030440201004820304402010048203044020100488030440901004880304409010000203040820100002030408201),
    (((1, 1), (2, 3), (0, 3), (0, 2)), 12, 0x80820308402010808203090020100080030640901220800306a09010048003060890122080110608901224880304095012208811060808100000110440901000001106400810008003060808100080030608081),
    (((1, 1), (3, 3), (0, 0), (2, 2)), 12, 0x220801306409012208013064090120080110648981200801106489810408000060c0810408000060c081220801306409012208013064090120080110648981200801106489810408000060c0810408000060c081),
    (((1, 2), (0, 3), (0, 3), (1, 2)), 9, 0x81020408102040208003060010102080030600101020800306001010208003060010102080030600101020800306001010208003060010102080030600101),
    (((1, 2), (0, 3), (1, 3), (0, 2)), 12, 0x80820308002010808203080020108082030800211080820308402012208083060010100088030640111220880106001010000083060010122008010640111220880306401110000081060010100000810600101),
    (((1, 2), (2, 3), (1, 3), (0, 0)), 12, 0x224880306401112248803064010100000810440101000080104401010048803064090100008030640911000080304081010000083060810122008030640911224880306409110000081060810100000810408101),
    (((1, 3), (0, 2), (1, 3), (0, 2)), 16, 0x8082030800201080820308002010808203080020108082030800201080820308002010808203080020108482130840211080821308402110048093044019100480932640191004809304401910048083040018300480930440191224881304409110008083040018100000810408181),
    (((1, 3), (2, 2), (1, 3), (0, 0)), 16, 0x8482030840201084820308402010048203044020100482030440201004821304402110048213044021100480830440191004809304401810048093044091100488130440191004808304081810000083044018122488130440911004881326409110000081040818100000830408183),
    (((1, 3), (2, 3), (0, 1), (0, 2)), 12, 0x220801306409012208813064090100480012608191000000106081812248093044090322080130640901000880104081810008001060819122000132640901220809306409010008001060818300080010608181),
    (((3, 3), (2, 2), (1, 1), (0, 0)), 16, 0x22488132640911224881326409110000081040818300000810408183224881326409112248813264091100000810408183000008104081832248813264091122488132640911000008104081830000081040818322488132640911224881326409110000081040818300000810408183),
)


def route_tables():
    pairs = [(a, b) for b in range(4) for a in range(b + 1)]
    pair_at = {pair: i for i, pair in enumerate(pairs)}
    row_of = np.zeros((79 * 128,), np.int32)
    rows = []
    seen = set()
    for goals, steps, code in ROUTES:
        for flip in range(8):
            names = []
            for chip in range(4):
                y, x = chip // 2 ^ (flip & 1), chip % 2 ^ (flip >> 1 & 1)
                names.append(x * 2 + y if flip & 4 else y * 2 + x)
            moved = [None] * 4
            for chip in range(4):
                moved[names[chip]] = tuple(sorted(names[g] for g in goals[chip]))
            key = sum(pair_at[moved[chip]] * 10**chip for chip in range(4))
            if key in seen:
                continue
            seen.add(key)
            row_of[key] = len(rows)
            rows.append(plan_of(moved, steps, code, names, flip >> 2))
    return row_of.reshape(79, 1, 128), np.stack(rows).reshape(-1, 1, 128)


def plan_of(goals, steps, code, names, swapped):
    back = [names.index(chip) for chip in range(4)]
    own = [{} for _ in range(4)]
    passing = [{} for _ in range(4)]
    for chip in range(4):
        for which in range(2):
            if goals[chip][which] != chip:
                pool = own[chip].setdefault(goals[chip][which], [])
                pool += [(piece, which) for piece in range(PIECES)]
                pool.sort()
    plan = np.full((4, 128), 3, np.int32)
    plan[:, 2 * PLAN_STEPS] = sum(steps > total for total in TOTALS)
    free = [[(0, slot) for slot in range(ROOM)] for _ in range(4)]
    for step in range(steps):
        landed = []
        for chip in range(4):
            for link in range(2):
                at = (step * 4 + back[chip]) * 2 + (link ^ swapped)
                goal, since = code >> 7 * at & 7, code >> 7 * at + 3 & 15
                if goal == 4:
                    continue
                goal = names[goal]
                if since == 0:
                    piece, which = own[chip][goal].pop(-link)
                    source, sent = chip, which | piece << 2
                else:
                    which, piece, source, slot = passing[chip].pop((step - since, 1 - link))
                    sent = 2 | slot << 2
                    free[chip].append((max(step, step - since + LAG), slot))
                plan[chip, 2 * step + link] += sent - 3
                landed.append((chip ^ 1 << link, link, source, which, piece, goal))
        for chip, link, source, which, piece, goal in landed:
            got = (source * 2 + which) << 9 | piece << 12
            if goal == chip:
                got |= 1 << 7
            else:
                at = next(i for i, item in enumerate(free[chip]) if item[0] <= step)
                slot = free[chip].pop(at)[1]
                got |= 2 << 7 | slot << 16
                passing[chip][step, link] = (which, piece, source, slot)
            plan[chip, 2 * step + link] |= got
    assert not any(passing) and not any(pool for chip in own for pool in chip.values())
    return plan


def copy_all(moves, sems, base, phase):
    for number, (condition, source, target) in enumerate(moves):

        def act(number=number, source=source, target=target):
            copy = pltpu.make_async_copy(source, target, sems.at[base + number])
            if phase == 0:
                copy.start()
            else:
                copy.wait()

        if condition is True:
            act()
        else:
            pl.when(condition)(act)


def piece_rows(ref, row, rows):
    return ref.at[pl.ds(pl.multiple_of(row, 16), rows)]


def link_of(step, core):
    return 1 - core if step // 2 % 2 else core


def early_kernel(weights, early, semaphores):
    rows = weights.shape[0] // PIECES
    core = lax.axis_index("req") % 2
    copies = []
    for number in range(EARLY):
        piece = jnp.where(core == 1, number, PIECES - 1 - number)
        part = piece_rows(weights, piece * rows, rows)
        copies.append(pltpu.make_async_copy(part, piece_rows(early, number * rows, rows), semaphores.at[number]))
        copies[-1].start()
    for copy in copies:
        copy.wait()


def plan_kernel(old_place, new_place, row_of, plans, meta, row_part, plan_part, sem):
    me_index = lax.axis_index("req")
    core = me_index % 2
    chip = me_index // 2
    goals = []
    for holder in range(8):
        goal = jnp.int32(0)
        for device in range(8):
            goal = jnp.where(new_place[device] == old_place[holder], device, goal)
        goals.append(goal)
    key = jnp.int32(0)
    my_swap = jnp.int32(0)
    for at in range(4):
        first, second = goals[2 * at], goals[2 * at + 1]
        low, high = jnp.minimum(first, second), jnp.maximum(first, second)
        high_chip = high // 2
        key = key + (high_chip * (high_chip + 1) // 2 + low // 2) * 10**at
        my_swap = jnp.where((first > second) & (chip == at), 1, my_swap)
        meta[GOAL_AT + 2 * at] = low % 2
        meta[GOAL_AT + 2 * at + 1] = high % 2
    meta[CORE_AT] = core
    meta[SWAP_AT] = my_swap
    wanted = new_place[me_index]
    beside = jnp.where(wanted == old_place[me_index + 1 - 2 * core], 2, 0)
    meta[LOCAL_AT] = jnp.where(wanted == old_place[me_index], 1, beside)
    copy = pltpu.make_async_copy(row_of.at[key // 128], row_part, sem)
    copy.start()
    copy.wait()
    row = row_part[0, key % 128]
    copy = pltpu.make_async_copy(plans.at[row * 4 + chip], plan_part, sem)
    copy.start()
    copy.wait()
    for at in range(2 * PLAN_STEPS):
        meta[at] = plan_part[0, at]
    meta[TOTAL_AT] = plan_part[0, 2 * PLAN_STEPS]


def step_kernel(rows, step, come, local_pieces, names, count, meta, *refs):
    refs = list(zip(names, refs))
    semaphores = refs.pop()[1]
    given = {}
    for number, (name, ref) in enumerate(refs):
        if number >= count or name not in ("out", "room"):
            given.setdefault(name, []).append(ref)
    w_hbm = given["weights"][0]
    out_hbm = given.get("out", [None])[0]
    room = given.get("room", [None])[0]
    core = meta[CORE_AT]
    local = meta[LOCAL_AT]
    used = 0
    stores, moves = [], []
    swap = given.get("swap", [None])[0]
    brought = [("landed", core, step_at) for step_at in come[0]]
    brought += [("swapped", 1 - core, step_at) for step_at in come[1]]
    for name, side, step_at in brought:
        word = meta[2 * step_at + link_of(step_at, side)]
        kind = (word >> 7) & 3
        row = ((word >> 12) & 15) * rows
        source = given[name].pop(0).at[pl.ds(0, rows)]
        if room is not None:
            slot = (word >> 16) & 31
            stores.append((kind == 2, source, piece_rows(room, slot * rows, rows)))
        final = (kind == 1) & (meta[GOAL_AT + ((word >> 9) & 7)] == core)
        moves.append((final, source, piece_rows(out_hbm, row, rows)))
        if name == "landed" and swap is not None:
            moves.append((jnp.logical_not(final), source, swap))
    copy_all(stores, semaphores, used, 0)
    copy_all(stores, semaphores, used, 1)
    used += len(stores)
    riding = []
    if "sent" in given:
        target = given["sent"][0].at[pl.ds(0, rows)]
        if "extra" in given:
            riding.append((True, given["extra"][0], given["sent"][0].at[pl.ds(rows, RIDE)]))
        word = meta[2 * step + link_of(step, core)]
        kind = word & 3
        piece = (word >> 2) & 31
        held = kind == 2
        mine = ((kind ^ meta[SWAP_AT]) == core) | (kind == 3)
        theirs = jnp.logical_not(held | mine)
        options = [(jnp.logical_not(held) & mine, piece_rows(w_hbm, piece * rows, rows))]
        if "other" in given:
            options.append((theirs, piece_rows(given["other"][0], piece * rows, rows)))
        place = jnp.where(core == 0, piece, PIECES - 1 - piece)
        if "early" in given:
            options.append((theirs, piece_rows(given["early"][0], place * rows, rows)))
        if room is not None:
            options.append((held, piece_rows(room, piece * rows, rows)))
        for condition, source in options:

            @pl.when(condition)
            def _(source=source):
                pltpu.make_async_copy(source, target, semaphores.at[used]).start()

        fetched = pltpu.make_async_copy(w_hbm.at[pl.ds(0, rows)], target, semaphores.at[used])
        used += 1
    copy_all(riding, semaphores, used, 0)
    first_ride = used
    used += len(riding)
    copy_all(moves, semaphores, used, 0)
    first_move = used
    used += len(moves)
    reads, writes = [], []
    for number, piece in enumerate(local_pieces):
        part = given["staged"][0].at[number]
        row = piece * rows
        reads.append((local == 1, piece_rows(w_hbm, row, rows), part))
        reads.append((local == 2, piece_rows(given["other"][0], row, rows), part))
        writes.append((local != 0, part, piece_rows(out_hbm, row, rows)))
    copy_all(reads, semaphores, used, 0)
    if "sent" in given:
        fetched.wait()
    copy_all(riding, semaphores, first_ride, 1)
    copy_all(reads, semaphores, used, 1)
    used += len(reads)
    copy_all(writes, semaphores, used, 0)
    copy_all(moves, semaphores, first_move, 1)
    copy_all(writes, semaphores, used, 1)


def between_cores(array):
    return lax.ppermute(array, "req", [(i, i ^ 1) for i in range(8)])


def along_links(array, step):
    return lax.ppermute(array, "req", [(i, i ^ (2 << link_of(step, i % 2))) for i in range(8)])


def plan_plane(old_place, new_place):
    row_of, plans = route_tables()
    smem = pl.BlockSpec(memory_space=pltpu.SMEM)
    anywhere = pl.BlockSpec(memory_space=pl.ANY)
    return pl.pallas_call(
        plan_kernel,
        out_shape=jax.ShapeDtypeStruct((META,), jnp.int32),
        in_specs=[smem, smem, anywhere, anywhere],
        out_specs=smem,
        scratch_shapes=[
            pltpu.SMEM((1, 128), jnp.int32),
            pltpu.SMEM((1, 128), jnp.int32),
            pltpu.SemaphoreType.DMA,
        ],
        name="plan_steps",
    )(old_place, new_place, jnp.asarray(row_of), jnp.asarray(plans))


def early_pieces(weights):
    width, columns = weights.shape
    return pl.pallas_call(
        early_kernel,
        out_shape=jax.ShapeDtypeStruct((width // PIECES * EARLY, columns), weights.dtype),
        in_specs=[pl.BlockSpec(memory_space=pl.ANY)],
        out_specs=pl.BlockSpec(memory_space=pltpu.VMEM),
        scratch_shapes=[pltpu.SemaphoreType.DMA((EARLY,))],
        compiler_params=pltpu.CompilerParams(vmem_limit_bytes=32 << 20),
        name="early_pieces",
    )(weights)


def migrate_plane(weights, meta, early, total, beside):
    width, columns = weights.shape
    rows = width // PIECES
    smem = pl.BlockSpec(memory_space=pltpu.SMEM)
    anywhere = pl.BlockSpec(memory_space=pl.ANY)
    near = pl.BlockSpec(memory_space=pltpu.VMEM)
    whole = jax.ShapeDtypeStruct((width, columns), weights.dtype)
    room_like = jax.ShapeDtypeStruct((ROOM * rows, columns), weights.dtype)
    held = {"out": None, "room": None}

    def run(meta, step, come, sources, local_pieces, extra, store, swap):
        operands, specs, names, aliases = [meta, weights], [smem, anywhere], ["weights"], {}

        def add(name, array, spec):
            if array is not None:
                operands.append(array)
                specs.append(spec)
                names.append(name)

        for name, array in sources:
            add(name, array, anywhere)
        for step_at in come[0]:
            add("landed", landed[step_at], near)
        for step_at in come[1]:
            add("swapped", swapped[step_at], near)
        add("extra", extra, near)
        results = []
        if step is not None:
            sent_rows = rows + (RIDE if step < RIDES else 0)
            results.append(("sent", jax.ShapeDtypeStruct((sent_rows, columns), weights.dtype), near))
        if swap:
            like = jax.ShapeDtypeStruct((rows, columns), weights.dtype)
            results.append(("swap", like, near))
        for name, like, wanted in (
            ("out", whole, bool(local_pieces or come[0] or come[1])),
            ("room", room_like, store),
        ):
            if wanted:
                if held[name] is not None:
                    aliases[len(operands)] = len(results)
                    add(name, held[name], anywhere)
                results.append((name, like, anywhere))
        count = len(names)
        names += [name for name, _, _ in results]
        scratch = []
        if local_pieces:
            scratch.append(pltpu.VMEM((len(local_pieces), rows, columns), weights.dtype))
            names.append("staged")
        scratch.append(pltpu.SemaphoreType.DMA((24,)))
        names.append("semaphores")
        values = pl.pallas_call(
            functools.partial(
                step_kernel, rows, step, come, local_pieces, names, count
            ),
            out_shape=[like for _, like, _ in results],
            in_specs=specs,
            out_specs=[spec for _, _, spec in results],
            scratch_shapes=scratch,
            input_output_aliases=aliases,
            compiler_params=pltpu.CompilerParams(vmem_limit_bytes=32 << 20),
            cost_estimate=pl.CostEstimate(
                flops=0, bytes_accessed=4 * rows * columns * 2, transcendentals=0
            ),
            name="place_pieces" if step is None else "step_pieces",
        )(*operands)
        for (name, _, _), value in zip(results, values):
            if name in held:
                held[name] = value
        return values

    landed, swapped = {}, {}
    ridden = None
    other = between_cores(weights)
    for step in range(total):
        meta, extra = beside(step, meta, ridden)
        come = [step - 2] if step >= 2 else [], [step - LAG] if step >= LAG else []
        sources = [("early", early) if step < EARLY else ("other", other)]
        local_pieces = LOCAL_PIECES.get(step, ())
        some = step >= 2
        values = run(meta, step, come, sources, local_pieces, extra, some, some)
        meta, _ = lax.optimization_barrier((meta, values[0]))
        landed[step] = along_links(values[0], step)
        if extra is not None:
            ridden = landed[step][rows:]
        if some:
            swapped[step - 2] = between_cores(values[1])
    last = total - 1
    meta, _ = beside(total, meta, ridden)
    come = [last - 1], list(range(total - LAG, last - 2))
    values = run(meta, None, come, (), (), None, False, True)
    swapped[last - 1] = between_cores(values[0])
    swapped[last] = between_cores(landed[last])
    run(meta, None, ([last], [last - 2, last - 1]), (), (), None, False, False)
    run(meta, None, ([], [last]), (), (), None, False, False)
    return held["out"]


def plane_dispatch(hidden, chosen, weights_now, place, gain):
    batches, tok_rows, width = hidden.shape
    topk = chosen.shape[-1]
    tokens = batches * tok_rows
    nreq = lax.axis_size("req")
    me_index = lax.axis_index("req")
    resid = hidden.reshape(tokens, width).astype(jnp.float32)
    normed = (
        resid * gain / jnp.sqrt(jnp.mean(resid * resid, axis=-1, keepdims=True) + 1e-05)
    ).astype(jnp.bfloat16)
    flat_ids = chosen.reshape(-1)
    devices = jnp.arange(nreq, dtype=jnp.int32)
    holder = jnp.sum(jnp.where(flat_ids[:, None] == place[None, :], devices[None, :], 0), axis=1)
    assign_index = jnp.arange(flat_ids.shape[0], dtype=jnp.int32)
    batch_of = assign_index // (tok_rows * topk)
    earlier = (
        (flat_ids[:, None] == flat_ids[None, :])
        & (batch_of[:, None] == batch_of[None, :])
        & (assign_index[None, :] < assign_index[:, None])
    )
    rank_in = jnp.sum(earlier.astype(jnp.int32), axis=1)
    slot = (holder ^ me_index) * SLOTS + batch_of * CAP + rank_in
    hit = slot[:, None] == jnp.arange(nreq * SLOTS, dtype=jnp.int32)[None, :]
    hit = hit.reshape(tokens, topk, nreq * SLOTS)
    coef = jnp.sum(jnp.where(hit, weights_now.reshape(tokens, topk, 1), 0.0), axis=1)
    blocks = jnp.any(hit, axis=1).T
    order = [k for k in range(nreq) if k & 1] + [k for k in range(nreq) if not k & 1]
    blocks = blocks.reshape(nreq, SLOTS, tokens)[jnp.array(order)].reshape(nreq * SLOTS, tokens)
    outgoing = jnp.dot(
        blocks.astype(jnp.bfloat16), normed, preferred_element_type=jnp.float32
    ).astype(jnp.bfloat16)
    half = nreq * SLOTS // 2
    came = between_cores(outgoing[:half])
    return jnp.concatenate([came, outgoing[half:]]), coef


def reordered(rows, orders):
    core = lax.axis_index("req") % 2
    spread = [np.eye(rows.shape[0], dtype=np.float32)[np.array(order)] for order in orders]
    chosen = jnp.where(core == 0, spread[0], spread[1]).astype(rows.dtype)
    return jnp.dot(chosen, rows, preferred_element_type=jnp.float32).astype(rows.dtype)


def exchange(rows, labels, bits):
    orders = []
    for core in range(2):
        going = [i for i, label in enumerate(labels[core]) if label // SLOTS >> bits[core] & 1]
        orders.append(going + [i for i in range(len(labels[core])) if i not in going])
    rows = reordered(rows, orders)
    half = rows.shape[0] // 2
    came = yield bits[0] > 0, rows[:half]
    labels = [[labels[core][i] for i in orders[core]] for core in range(2)]
    if bits[0] == 0:
        labels = [labels[1 - core][:half] + labels[core][half:] for core in range(2)]
    return jnp.concatenate([came, rows[half:]]), labels


def plane_work(attention, hidden, rows, coef, shard_weights):
    batches, tok_rows, width = hidden.shape
    tokens = batches * tok_rows
    ntp = lax.axis_size("tp")
    hid_dev = shard_weights.shape[1] // 3
    every = range(rows.shape[0])
    first = [i for i in every if i // SLOTS & 1] + [i for i in every if not i // SLOTS & 1]
    labels = [first, first]
    rows, labels = yield from exchange(rows, labels, (1, 2))
    rows, labels = yield from exchange(rows, labels, (2, 1))
    gate_up = jnp.dot(rows, shard_weights[:, : 2 * hid_dev], preferred_element_type=jnp.float32)
    act = (jax.nn.silu(gate_up[:, :hid_dev]) * gate_up[:, hid_dev:]).astype(jnp.bfloat16)
    part = lax.dot_general(
        act,
        shard_weights[:, 2 * hid_dev :],
        (((1,), (1,)), ((), ())),
        preferred_element_type=jnp.float32,
    )
    rows = part.astype(jnp.bfloat16)
    rows, labels = yield from exchange(rows, labels, (1, 2))
    context = yield False, attend(*attention)
    rows, labels = yield from exchange(rows, labels, (2, 1))
    swap = exchange(rows, labels, (0, 0))
    _, going = next(swap)
    try:
        swap.send(between_cores(going))
    except StopIteration as end:
        rows, labels = end.value
    rows = yield False, rows
    rows = reordered(rows, [[label.index(i) for i in every] for label in labels])
    partial_sum = jnp.dot(
        coef,
        rows.astype(jnp.float32),
        precision=lax.Precision.HIGHEST,
        preferred_element_type=jnp.float32,
    )
    tp_index = lax.axis_index("tp")
    tp_width = width // ntp

    def share_of(index):
        start = lax.rem(index, ntp) * tp_width
        return lax.dynamic_slice_in_dim(partial_sum, start, tp_width, 1)

    total = share_of(tp_index)
    for ahead in range(1, ntp):
        pairs = [(i, (i + ahead) % ntp) for i in range(ntp)]
        share = share_of(tp_index + ahead).astype(jnp.bfloat16)
        total = total + lax.ppermute(share, "tp", pairs).astype(jnp.float32)
    total = yield False, total
    resid = hidden.reshape(tokens, width).astype(jnp.float32)
    resid_share = lax.dynamic_slice_in_dim(resid, tp_index * tp_width, tp_width, 1)
    summed = (resid_share + total).astype(jnp.bfloat16)
    return context, summed.reshape(batches, tok_rows, tp_width)


def attend(queries, new_keys, new_values, cache_keys, cache_values, lengths):
    batches, tok_rows, width = queries.shape
    heads = width // HEAD_SIZE
    pool = cache_keys.shape[0]
    scale = HEAD_SIZE ** (-0.5)
    req_lengths = lengths.reshape(-1)
    starts = jnp.cumsum(req_lengths) - req_lengths
    position = jnp.arange(pool, dtype=jnp.int32)
    owned = (position[None, :] >= starts[:, None]) & (
        position[None, :] < (starts + req_lengths)[:, None]
    )
    query_rows = queries.reshape(batches * tok_rows, heads, HEAD_SIZE)
    own_keys = new_keys.reshape(batches * tok_rows, heads, HEAD_SIZE)
    own_values = new_values.reshape(batches * tok_rows, heads, HEAD_SIZE)
    pool_keys = cache_keys.reshape(pool, heads, HEAD_SIZE)
    pool_values = cache_values.reshape(pool, heads, HEAD_SIZE)
    scores = (
        jnp.einsum("qhd,phd->hqp", query_rows, pool_keys, preferred_element_type=jnp.float32)
        * scale
    )
    scores = jnp.where(owned[None], scores, -jnp.inf)
    own_score = (
        jnp.einsum("qhd,qhd->hq", query_rows, own_keys, preferred_element_type=jnp.float32) * scale
    )
    highest = jnp.maximum(jnp.max(scores, axis=-1), own_score)
    exp_pool = jnp.exp(scores - highest[..., None])
    exp_own = jnp.exp(own_score - highest)
    denom = jnp.sum(exp_pool, axis=-1) + exp_own
    summed = jnp.einsum(
        "hqp,phd->qhd",
        exp_pool.astype(jnp.bfloat16),
        pool_values,
        preferred_element_type=jnp.float32,
    )
    prob_own = lax.optimization_barrier(exp_own.astype(jnp.bfloat16)).astype(jnp.float32)
    summed = summed + prob_own.T[:, :, None] * own_values.astype(jnp.float32)
    context = (summed / denom.T[:, :, None]).astype(jnp.bfloat16)
    return context.reshape(batches, tok_rows, width)


def choose_holders(place, me_index, nreq, shard_count):
    devices = jnp.arange(nreq, dtype=jnp.int32)
    holder = place[None, :] == jnp.arange(shard_count, dtype=jnp.int32)[:, None]
    before = (place[:, None] == place[None, :]) & (devices[:, None] < devices[None, :])
    rank_in = jnp.sum(before.astype(jnp.int32), axis=0)
    count = jnp.sum(holder.astype(jnp.int32), axis=1)
    wanted = me_index % count
    match = holder & (rank_in[None, :] == wanted[:, None])
    return jnp.sum(jnp.where(match, devices[None, :], 0), axis=1)


def expert_block(hidden, chosen, weights_now, place, shard_weights, gain):
    nreq = lax.axis_size("req")
    me_index = lax.axis_index("req")
    split_count = max(1, nreq // 16)
    shard_count = EXPERTS * split_count
    batches, tok_rows, width = hidden.shape
    topk = chosen.shape[-1]
    tokens = batches * tok_rows
    hid_dev = shard_weights.shape[1] // 3
    resid = hidden.reshape(tokens, width).astype(jnp.float32)
    normed = (
        resid * gain / jnp.sqrt(jnp.mean(resid * resid, axis=-1, keepdims=True) + 1e-05)
    ).astype(jnp.bfloat16)
    flat_ids = chosen.reshape(-1)
    assigns = flat_ids.shape[0]
    slots_dev = batches * CAP
    shard_dest = choose_holders(place, me_index, nreq, shard_count)
    shard_list = flat_ids[:, None] * split_count + jnp.arange(split_count, dtype=jnp.int32)[None, :]
    pick = shard_list[:, :, None] == jnp.arange(shard_count, dtype=jnp.int32)[None, None, :]
    dest = jnp.sum(jnp.where(pick, shard_dest[None, None, :], 0), axis=-1)
    assign_index = jnp.arange(assigns, dtype=jnp.int32)
    batch_of = assign_index // (tok_rows * topk)
    earlier = (
        (flat_ids[:, None] == flat_ids[None, :])
        & (batch_of[:, None] == batch_of[None, :])
        & (assign_index[None, :] < assign_index[:, None])
    )
    rank_in = jnp.sum(earlier.astype(jnp.int32), axis=1)
    slot = dest * slots_dev + (batch_of * CAP + rank_in)[:, None]
    slot_hit = slot[:, :, None] == jnp.arange(nreq * slots_dev, dtype=jnp.int32)[None, None, :]
    by_token = jnp.any(slot_hit.reshape(tokens, topk * split_count, nreq * slots_dev), axis=1)
    outgoing = jnp.dot(
        by_token.T.astype(jnp.bfloat16), normed, preferred_element_type=jnp.float32
    )
    outgoing = outgoing.astype(jnp.bfloat16).reshape(nreq, slots_dev, width)
    received = lax.all_to_all(outgoing, "req", split_axis=0, concat_axis=0, tiled=True)
    flat_rows = received.reshape(nreq * slots_dev, width)
    gate_up = jnp.dot(
        flat_rows, shard_weights[:, : 2 * hid_dev], preferred_element_type=jnp.float32
    )
    act = (jax.nn.silu(gate_up[:, :hid_dev]) * gate_up[:, hid_dev:]).astype(jnp.bfloat16)
    part = lax.dot_general(
        act,
        shard_weights[:, 2 * hid_dev :],
        (((1,), (1,)), ((), ())),
        preferred_element_type=jnp.float32,
    )
    part = part.astype(jnp.bfloat16).reshape(nreq, slots_dev, width)
    returned = lax.all_to_all(part, "req", split_axis=0, concat_axis=0, tiled=True)
    returned = returned.reshape(nreq * slots_dev, width)
    coef = jnp.sum(
        jnp.where(
            slot_hit.reshape(tokens, topk, split_count, nreq * slots_dev),
            weights_now.reshape(tokens, topk)[:, :, None, None],
            0.0,
        ),
        axis=(1, 2),
    )
    partial_sum = jnp.dot(
        coef,
        returned.astype(jnp.float32),
        precision=lax.Precision.HIGHEST,
        preferred_element_type=jnp.float32,
    )
    tp_width = width // lax.axis_size("tp")
    tp_start = lax.axis_index("tp") * tp_width
    resid_share = lax.dynamic_slice_in_dim(resid, tp_start, tp_width, 1)
    share = lax.psum_scatter(
        partial_sum.astype(jnp.bfloat16), "tp", scatter_dimension=1, tiled=True
    ).astype(jnp.float32)
    summed = (resid_share + share).astype(jnp.bfloat16)
    return summed.reshape(batches, tok_rows, tp_width)


def migrate(old_weights, old_place, new_place):
    nreq = lax.axis_size("req")
    shard_count = EXPERTS * max(1, nreq // 16)
    _, width, columns = old_weights.shape
    piece = width // nreq
    pieces = old_weights.reshape(nreq, piece, columns)
    spread = lax.all_to_all(pieces, "req", split_axis=0, concat_axis=0, tiled=True)
    devices = jnp.arange(nreq, dtype=jnp.int32)
    shard_ids = jnp.arange(shard_count, dtype=jnp.int32)
    first_old = jnp.min(
        jnp.where(old_place[None, :] == shard_ids[:, None], devices[None, :], nreq), axis=1
    )
    needed = jnp.sum(
        jnp.where(new_place[:, None] == shard_ids[None, :], first_old[None, :], 0), axis=1
    )
    sending = spread[needed]
    collected = lax.all_to_all(sending, "req", split_axis=0, concat_axis=0, tiled=True)
    return collected.reshape(1, width, columns)


def plane_outputs(attention, layer, new_place):
    hidden, expert_ids, route_weights, old_place, weights, gain = layer
    early = early_pieces(weights)
    first = between_cores(early)
    hidden, _ = lax.optimization_barrier((hidden, early))
    meta = plan_plane(old_place, new_place)
    received, coef = plane_dispatch(hidden, expert_ids, route_weights, old_place, gain)

    def within(total):
        def outputs(weights, meta, first, attention, hidden, rows, coef):
            work = plane_work(attention, hidden, rows, coef, weights)
            stage = next(work)
            done = None
            pending = []

            def beside(step, meta, ridden):
                nonlocal stage, done
                for _ in range(STAGES.get(step, 0) + (step == min(total, 11))):
                    rides, value = stage
                    if pending:
                        pending.pop()
                        half = value.shape
                        value = ridden.reshape(half)
                    elif rides:
                        pending.append(True)
                        return meta, value.reshape(RIDE, weights.shape[1])
                    else:
                        meta, value = lax.optimization_barrier((meta, value))
                    try:
                        stage = work.send(value)
                    except StopIteration as end:
                        done = end.value
                return meta, None

            moved = migrate_plane(
                weights, meta, first, total, beside
            )
            return (*done, moved[None])

        return outputs

    branches = [within(total) for total in TOTALS]
    return lax.switch(meta[TOTAL_AT], branches, weights, meta, first, attention, hidden, received, coef)


def on_device(
    queries,
    new_keys,
    new_values,
    cache_keys,
    cache_values,
    lengths,
    hidden,
    gain,
    expert_ids,
    route_weights,
    old_place,
    new_place,
    old_weights,
):
    attention = (queries, new_keys, new_values, cache_keys, cache_values, lengths)
    layer = (hidden, expert_ids, route_weights, old_place, old_weights[0], gain)
    if lax.axis_size("req") == 8:
        return plane_outputs(attention, layer, new_place)
    context = attend(*attention)
    moved = migrate(old_weights, old_place, new_place)
    layer_out = expert_block(*layer)
    return (context, layer_out, moved)


def solution(mesh):
    in_specs = (
        P(None, "req", "tp"),
        P(None, "req", "tp"),
        P(None, "req", "tp"),
        P("req", "tp"),
        P("req", "tp"),
        P("req", None),
        P(None, "req", None),
        P(),
        P(None, "req", None),
        P(None, "req", None),
        P(),
        P(),
        P("req", None, "tp"),
    )
    out_specs = (P(None, "req", "tp"), P(None, "req", "tp"), P("req", None, "tp"))
    return jax.shard_map(
        on_device, mesh=mesh, in_specs=in_specs, out_specs=out_specs, check_vma=False
    )
```
